32 devices in a mesh: clip: 4 (over x, core), win: 8 (over z, y).
Axes of the slice: x: 2, y: 2, z: 4, core: 2. Of those that a mesh axis runs over, the one named last changes fastest.
Arguments:
- tokens: bfloat16 [4, 8, 1, 5, 128, 1024], P('clip', 'win'), may hold values from -6 to 6
- grad_output: bfloat16 [4, 8, 1, 5, 128, 1024], P('clip', 'win'), may hold values from -16 to 16
- clip_height: int32 [4], P('clip'), may hold values from 9 to 16
- clip_width: int32 [4], P('clip'), may hold values from 33 to 64
- modulation: float32 [4, 12, 1024], P('clip'), may hold values from -3 to 3
- sp_qkv: float32 [1024, 3072], P('clip', 'win'), may hold values from -0.1875 to 0.1875
- sp_out: float32 [1024, 1024], P('clip', 'win'), may hold values from -0.75 to 0.75
- sp_up: float32 [1024, 4096], P('clip', 'win'), may hold values from -0.1875 to 0.1875
- sp_down: float32 [4096, 1024], P('clip', 'win'), may hold values from -0.09375 to 0.09375
- sp_table: float32 [16, 31, 31], replicated, may hold values from -3 to 3
- st_qkv: float32 [1024, 3072], P('clip', 'win'), may hold values from -0.1875 to 0.1875
- st_out: float32 [1024, 1024], P('clip', 'win'), may hold values from -0.75 to 0.75
- st_up: float32 [1024, 4096], P('clip', 'win'), may hold values from -0.1875 to 0.1875
- st_down: float32 [4096, 1024], P('clip', 'win'), may hold values from -0.09375 to 0.09375
- st_table: float32 [16, 9, 15, 15], replicated, may hold values from -3 to 3
Outputs:
- out_tokens: float32 [4, 8, 1, 5, 128, 1024], P('clip', 'win')
- grad_tokens: float32 [4, 8, 1, 5, 128, 1024], P('clip', 'win')
- grad_modulation: float32 [4, 12, 1024], P('clip')
- grad_sp_qkv: float32 [1024, 3072], P('clip', 'win')
- grad_sp_out: float32 [1024, 1024], P('clip', 'win')
- grad_sp_up: float32 [1024, 4096], P('clip', 'win')
- grad_sp_down: float32 [4096, 1024], P('clip', 'win')
- grad_sp_table: float32 [16, 31, 31], replicated
- grad_st_qkv: float32 [1024, 2048], P('clip', 'win')
- grad_st_value: float32 [1024, 1024], P('clip', 'win')
- grad_st_out: float32 [1024, 1024], P('clip', 'win')
- grad_st_up: float32 [1024, 4096], P('clip', 'win')
- grad_st_down: float32 [4096, 1024], P('clip', 'win')
- grad_st_table: float32 [16, 9, 15, 15], replicated
The draws below stay inside these ranges and needn't reach their ends.
All inputs are finite; a program needn't handle non-finite values.
Results may differ from the reference program's by a relative error of at most 0.03.
Values may be sent and summed in bfloat16 or wider, within the bound.
No kernel may reach another device: no remote copies, remote signals or barrier semaphores. Data moves between devices by JAX's collectives and lax.ppermute only.
A program may use at most 448 MiB of HBM per device.

```python
import jax
import jax.numpy as jnp
from jax import lax

D = 1024
HEADS = 16
FF = 4096
WS = 16
FR = 5
LOC_W = 4
PAIR_LOCS = 1
HS = 8
HW = 128
CLIPS = 4
WIN_SHARDS = 8
LOC_H = 1


def draw_grad_output(key, part):
    key = jax.random.fold_in(key, 11)
    full_shape = (CLIPS, WIN_SHARDS, PAIR_LOCS, FR, HW, D)
    base_draw = jnp.clip(jax.random.normal(key, full_shape, jnp.float32), -4.0, 4.0)
    clip_rise = 1.0 + lax.broadcasted_iota(jnp.float32, full_shape, 0) / (CLIPS - 1)
    shard_rise = 1.0 + lax.broadcasted_iota(jnp.float32, full_shape, 1) / (WIN_SHARDS - 1)
    return (base_draw * clip_rise * shard_rise).astype(jnp.bfloat16)


def with_ends(entries, own_key, smallest, top_value):
    longest = entries.shape.index(max(entries.shape))
    spots = []
    for shift in (0, 1):
        where = [jax.random.randint(jax.random.fold_in(own_key, axis), (), 0, length) for axis, length in enumerate(entries.shape)]
        where[longest] = (where[longest] + shift) % entries.shape[longest]
        spots.append(tuple(where))
    return entries.at[spots[0]].set(smallest).at[spots[1]].set(top_value)


def level_of(stream_key, extent, shards, low, largest):
    def one(position, shards_of):
        heights = jax.random.uniform(jax.random.fold_in(jax.random.fold_in(stream_key, 6), position), (shards_of,), jnp.float32, low / len(shards), largest / len(shards))
        return jnp.repeat(jnp.exp(heights), extent[position] // shards_of).reshape((-1,) + (1,) * (len(extent) - position - 1))

    level = one(*shards[0])
    for cut in shards[1:]:
        level = level * one(*cut)
    return level


def bell_draw(rng, dims, scale, limit, shards=(), kind=jnp.bfloat16):
    entries = scale * jax.random.normal(rng, dims, jnp.float32)
    if shards:
        entries = entries * level_of(rng, dims, shards, -0.22, 0.18)
    return jnp.clip(entries, -limit, limit).astype(kind)


def setup_inputs(seed: int = 0) -> dict:
    seeds = jax.random.split(jax.random.key(seed), 16)
    return {
        "tokens": bell_draw(seeds[0], (CLIPS, WIN_SHARDS, PAIR_LOCS, FR, HW, D), 1.0, 6.0, ((0, 4), (1, 8))),
        "grad_output": draw_grad_output(jax.random.fold_in(seeds[15], 71), 0),
        "clip_height": with_ends(jax.random.randint(seeds[2], (CLIPS,), LOC_H * WS // 2 + 1, LOC_H * WS + 1), jax.random.fold_in(seeds[2], 1), LOC_H * WS // 2 + 1, LOC_H * WS).astype(jnp.int32),
        "clip_width": with_ends(jax.random.randint(seeds[3], (CLIPS,), LOC_W * WS // 2 + 1, LOC_W * WS + 1), jax.random.fold_in(seeds[3], 1), LOC_W * WS // 2 + 1, LOC_W * WS).astype(jnp.int32),
        "modulation": bell_draw(seeds[4], (CLIPS, 12, D), 0.5, 3.0, ((0, 4),), jnp.float32),
        "sp_qkv": bell_draw(seeds[5], (D, 3 * D), D ** -0.5, 0.1875, ((0, 4), (1, 8)), jnp.float32),
        "sp_out": bell_draw(seeds[6], (D, D), (D // 16) ** -0.5, 0.75, ((0, 4), (1, 8)), jnp.float32),
        "sp_up": bell_draw(seeds[7], (D, FF), D ** -0.5, 0.1875, ((0, 4), (1, 8)), jnp.float32),
        "sp_down": bell_draw(seeds[8], (FF, D), FF ** -0.5, 0.09375, ((0, 4), (1, 8)), jnp.float32),
        "sp_table": bell_draw(seeds[9], (HEADS, 2 * WS - 1, 2 * WS - 1), 0.5, 3.0, (), jnp.float32),
        "st_qkv": bell_draw(seeds[10], (D, 3 * D), D ** -0.5, 0.1875, ((0, 4), (1, 8)), jnp.float32),
        "st_out": bell_draw(seeds[11], (D, D), (D // 16) ** -0.5, 0.75, ((0, 4), (1, 8)), jnp.float32),
        "st_up": bell_draw(seeds[12], (D, FF), D ** -0.5, 0.1875, ((0, 4), (1, 8)), jnp.float32),
        "st_down": bell_draw(seeds[13], (FF, D), FF ** -0.5, 0.09375, ((0, 4), (1, 8)), jnp.float32),
        "st_table": bell_draw(seeds[14], (HEADS, 2 * FR - 1, 2 * HS - 1, 2 * HS - 1), 0.5, 3.0, (), jnp.float32),
    }


epsilon = 1e-06
masked_score = -1000000000.0
highest = lax.Precision.HIGHEST

@jax.custom_vjp
def low(v):
    return lax.optimization_barrier(v.astype(jnp.bfloat16)).astype(jnp.float32)

@jax.custom_vjp
def low_back(v):
    return v

def low_keep(v):
    return (low(v), None)

def low_pass(kept, grad):
    return (grad,)

def back_keep(v):
    return (v, None)

def back_low(kept, grad):
    return (low(grad),)
low.defvjp(low_keep, low_pass)
low_back.defvjp(back_keep, back_low)

def modulated_norm(values, shift_vec, scale_vec):
    center = values - lax.optimization_barrier(jnp.mean(values, axis=-1, keepdims=True))
    spread = lax.optimization_barrier(jnp.mean(center * center, axis=-1, keepdims=True))
    return center * lax.rsqrt(spread + epsilon) * (1.0 + scale_vec) + shift_vec

def token_valid(clip_height, clip_width):
    shard_ids = jnp.arange(WIN_SHARDS, dtype=jnp.int32)
    local_ids = jnp.arange(PAIR_LOCS, dtype=jnp.int32)
    token_ids = jnp.arange(HW, dtype=jnp.int32)
    location = (shard_ids // 2)[:, None] * PAIR_LOCS + local_ids[None, :]
    row_pos = (location // LOC_W * WS)[:, :, None] + (shard_ids % 2 * HS)[:, None, None] + (token_ids // WS)[None, None, :]
    col_pos = (location % LOC_W * WS)[:, :, None] + (token_ids % WS)[None, None, :]
    inside = (row_pos[None] < clip_height[:, None, None, None]) & (col_pos[None] < clip_width[:, None, None, None])
    return jnp.broadcast_to(inside[:, :, :, None, :], (CLIPS, WIN_SHARDS, PAIR_LOCS, FR, HW))

def to_spatial(source):
    features = source.shape[-1]
    paired = source.reshape(CLIPS, WIN_SHARDS // 2, 2, PAIR_LOCS, FR, HW, features)
    return paired.transpose(0, 1, 3, 4, 2, 5, 6).reshape(CLIPS, WIN_SHARDS // 2 * PAIR_LOCS * FR, 2 * HW, features)

def from_spatial(source):
    features = source.shape[-1]
    paired = source.reshape(CLIPS, WIN_SHARDS // 2, PAIR_LOCS, FR, 2, HW, features)
    return paired.transpose(0, 1, 4, 2, 3, 5, 6).reshape(CLIPS, WIN_SHARDS, PAIR_LOCS, FR, HW, features)

def to_joint(source):
    features = source.shape[-1]
    split_cols = source.reshape(CLIPS, WIN_SHARDS, PAIR_LOCS, FR, HS, 2, HS, features)
    return split_cols.transpose(0, 1, 2, 5, 3, 4, 6, 7).reshape(CLIPS, WIN_SHARDS * PAIR_LOCS * 2, FR * HS * HS, features)

def from_joint(source):
    features = source.shape[-1]
    split_cols = source.reshape(CLIPS, WIN_SHARDS, PAIR_LOCS, 2, FR, HS, HS, features)
    return split_cols.transpose(0, 1, 2, 4, 5, 3, 6, 7).reshape(CLIPS, WIN_SHARDS, PAIR_LOCS, FR, HW, features)

def spatial_bias(bias_table):
    token_ids = jnp.arange(WS * WS, dtype=jnp.int32)
    row_ids = token_ids // WS
    col_ids = token_ids % WS
    row_off = row_ids[:, None] - row_ids[None, :] + WS - 1
    col_off = col_ids[:, None] - col_ids[None, :] + WS - 1
    return bias_table[:, row_off, col_off]

def joint_bias(bias_table):
    token_ids = jnp.arange(FR * HS * HS, dtype=jnp.int32)
    frame_ids = token_ids // (HS * HS)
    row_ids = token_ids // HS % HS
    col_ids = token_ids % HS
    frame_off = frame_ids[:, None] - frame_ids[None, :] + FR - 1
    row_off = row_ids[:, None] - row_ids[None, :] + HS - 1
    col_off = col_ids[:, None] - col_ids[None, :] + HS - 1
    return bias_table[:, frame_off, row_off, col_off]

def window_attention(score_bias, qkv_rows, valid_rows):
    win_count, win_len, triple = qkv_rows.shape
    head_dim = triple // (3 * HEADS)
    split_heads = qkv_rows.reshape(win_count, win_len, 3, HEADS, head_dim)
    queries = split_heads[:, :, 0]
    key_rows = split_heads[:, :, 1]
    value_rows = split_heads[:, :, 2]
    scores = jnp.einsum('wqhe,wkhe->whqk', queries, key_rows, precision=highest) * head_dim ** (-0.5) + score_bias[None]
    scores = low_back(scores)
    allowed = valid_rows[:, None, :] | jnp.eye(win_len, dtype=bool)[None]
    scores = jnp.where(allowed[:, None], scores, masked_score)
    attn_probs = low(jax.nn.softmax(scores, axis=-1))
    attn_mixed = jnp.einsum('whqk,wkhe->wqhe', attn_probs, value_rows, precision=highest)
    return low(low_back(attn_mixed.reshape(win_count, win_len, triple // 3)))

def per_clip(vector):
    return vector[:, None, None, None, None, :]

def run_block(residual, params, qkv_weight, out_weight, up_weight, down_weight, score_bias, valid_win, group, ungroup):
    attn_in = low(modulated_norm(residual, per_clip(params[:, 0]), per_clip(params[:, 1])))
    qkv_rows = low(low_back(jnp.einsum('...d,de->...e', attn_in, low(qkv_weight), precision=highest)))
    checked = jax.checkpoint(window_attention)
    attended = lax.map(lambda packed: checked(score_bias, packed[0], packed[1]), (group(qkv_rows), valid_win))
    mixed_rows = low_back(jnp.einsum('...d,de->...e', ungroup(attended), low(out_weight), precision=highest))
    middle = residual + per_clip(params[:, 2]) * mixed_rows
    mlp_in = low(modulated_norm(middle, per_clip(params[:, 3]), per_clip(params[:, 4])))
    upward = low_back(jnp.einsum('...d,de->...e', mlp_in, low(up_weight), precision=highest))
    hidden = low(jax.nn.gelu(upward, approximate=False))
    downward = low_back(jnp.einsum('...d,de->...e', hidden, low(down_weight), precision=highest))
    return middle + per_clip(params[:, 5]) * downward

def reference(tokens, grad_output, clip_height, clip_width, modulation, sp_qkv, sp_out, sp_up, sp_down, sp_table, st_qkv, st_out, st_up, st_down, st_table):
    valid_mask = token_valid(clip_height, clip_width)
    valid_spatial = to_spatial(valid_mask[..., None])[..., 0]
    valid_joint = to_joint(valid_mask[..., None])[..., 0]

    def forward(float_tokens, mod_rows, sp_qkv_w, sp_out_w, sp_up_w, sp_down_w, sp_table_w, st_qkv_w, st_out_w, st_up_w, st_down_w, st_table_w):
        middle_out = run_block(float_tokens, mod_rows[:, 0:6], sp_qkv_w, sp_out_w, sp_up_w, sp_down_w, spatial_bias(sp_table_w), valid_spatial, to_spatial, from_spatial)
        return run_block(middle_out, mod_rows[:, 6:12], st_qkv_w, st_out_w, st_up_w, st_down_w, joint_bias(st_table_w), valid_joint, to_joint, from_joint)
    out_tokens, pull_back = jax.vjp(forward, tokens.astype(jnp.float32), modulation, sp_qkv, sp_out, sp_up, sp_down, sp_table, st_qkv, st_out, st_up, st_down, st_table)
    all_grads = pull_back(grad_output.astype(jnp.float32))
    st_qkv_grad = all_grads[7]
    return (out_tokens, all_grads[0], all_grads[1], all_grads[2], all_grads[3], all_grads[4], all_grads[5], all_grads[6], st_qkv_grad[:, :2 * D], st_qkv_grad[:, 2 * D:], all_grads[8], all_grads[9], all_grads[10], all_grads[11])
```

```python
from functools import partial

import jax
import jax.numpy as jnp
from jax import lax
from jax.experimental import pallas as pl
from jax.experimental.pallas import tpu as pltpu
from jax.sharding import PartitionSpec as P

HEADS = 16
WS = 16
FR = 5
LOC_W = 4
PAIR_LOCS = 1
HS = 8
SLOTS = 3
VMEM_BYTES = 56 * 1024 * 1024

epsilon = 1e-06
masked_score = -1000000000.0
highest = lax.Precision.HIGHEST
NT = (((1,), (1,)), ((), ()))
TN = (((0,), (0,)), ((), ()))


BITS = {"core": ("clip", 1), "x": ("clip", 2), "y": ("win", 1), "z0": ("win", 2), "z1": ("win", 4)}


def hop(value, link):
    axis, mask = BITS[link]
    return lax.ppermute(value, axis, [(i, i ^ mask) for i in range(lax.axis_size(axis))])


def z_groups():
    size = lax.axis_size("win")
    return [list(range(start, size, 2)) for start in range(2)]


class Gather:
    def __init__(self, shard):
        rows, cols = shard.shape
        self.rows = rows
        halves = shard.reshape(2, rows // 2, cols)
        grown = lax.all_gather(halves, "win", axis=1, tiled=False, axis_index_groups=z_groups())
        self.values = (grown[0], grown[1])
        self.stage = 0

    def advance(self, values):
        if self.stage == 0:
            a0, b0 = values
            new = (jnp.stack([a0, hop(a0, "y")]), jnp.stack([b0, hop(b0, "x")]))
        elif self.stage == 1:
            a1, b1 = values
            new = (a1, hop(a1, "x"), hop(a1, "core"), b1, hop(b1, "y"), hop(b1, "core"))
        else:
            a1, a2, a3, b1, b2, b3 = values
            new = (a1, a2, a3, hop(a2, "core"), b1, b2, b3, hop(b2, "core"))
        self.values = new
        self.stage += 1


def assemble_kernel(row_of, y_of, *refs, rows, widths):
    count = len(widths)
    pieces = refs[:8]
    outs = refs[8 : 8 + count]
    whole = refs[8 + count : 8 + 2 * count]
    in_sems, out_sems = refs[8 + 2 * count :]
    half = rows // 2
    bands = []
    for part in range(2):
        for c_rel in range(2):
            for x_rel in range(2):
                block = row_of[c_rel * 2 + x_rel]
                row = pl.multiple_of(block * rows + part * half, half)
                copies = []
                for y_rel in range(2):
                    far, near = (x_rel, y_rel) if part == 0 else (y_rel, x_rel)
                    source = pieces[part * 4 + c_rel * 2 + far]
                    for z in range(4):
                        place = z * 2 + y_of[y_rel]
                        start = 0
                        for held, width in zip(whole, widths):
                            col = pl.multiple_of(place * width, 128)
                            copies.append(
                                pltpu.make_async_copy(
                                    source.at[near, z, :, pl.ds(start, width)],
                                    held.at[pl.ds(row, half), pl.ds(col, width)],
                                    in_sems.at[len(bands) * 8 * count + len(copies)],
                                )
                            )
                            start += width
                bands.append((row, copies))
    for row, copies in bands:
        for copy in copies:
            copy.start()
    sent = []
    for band, (row, copies) in enumerate(bands):
        for copy in copies:
            copy.wait()
        for which, (held, out) in enumerate(zip(whole, outs)):
            there = pl.ds(row, half)
            sent.append(
                pltpu.make_async_copy(held.at[there], out.at[there], out_sems.at[band * count + which])
            )
            sent[-1].start()
    for copy in sent:
        copy.wait()


def assemble(values, place, rows, widths):
    shapes = [(4 * rows, 8 * width) for width in widths]
    return pl.pallas_call(
        partial(assemble_kernel, rows=rows, widths=widths),
        out_shape=[jax.ShapeDtypeStruct(shape, jnp.bfloat16) for shape in shapes],
        in_specs=[pl.BlockSpec(memory_space=pltpu.SMEM)] * 2 + [pl.BlockSpec(memory_space=pl.ANY)] * 8,
        out_specs=[pl.BlockSpec(memory_space=pl.ANY)] * len(widths),
        scratch_shapes=[pltpu.VMEM(shape, jnp.bfloat16) for shape in shapes]
        + [pltpu.SemaphoreType.DMA((64 * len(widths),)), pltpu.SemaphoreType.DMA((8 * len(widths),))],
        compiler_params=pltpu.CompilerParams(vmem_limit_bytes=VMEM_BYTES),
        cost_estimate=pl.CostEstimate(
            flops=0, bytes_accessed=4 * sum(a * b for a, b in shapes), transcendentals=0
        ),
        name="assemble",
    )(place["rows"], place["cols"], *values)


def grad_kernel(row_of, y_of, x_ref, *refs, part, rows, widths):
    dy_refs = refs[: len(widths)]
    out_ref, turned = refs[len(widths) :]
    half = rows // 2
    total = sum(widths)

    @pl.when(pl.program_id(0) == 0)
    def turn():
        for x_rel in range(2):
            start = pl.multiple_of(row_of[part * 2 + x_rel] * rows, rows)
            turned[x_rel * rows : (x_rel + 1) * rows, :] = x_ref[:, pl.ds(start, rows)].T

    offset = 0
    for dy_ref, width in zip(dy_refs, widths):
        product = jnp.dot(turned[...], dy_ref[...], preferred_element_type=jnp.float32)
        for y in range(2):
            for x_rel in range(2):
                for ab in range(2):
                    first = x_rel * rows + ab * half
                    out_ref[ab, x_rel, y_of[y], 0, :, offset : offset + width] = product[
                        first : first + half, y * width : (y + 1) * width
                    ].astype(jnp.bfloat16)
        offset += width


def weight_grad(x, dys, place, part, rows, widths, starts):
    count = x.shape[0]
    total = sum(widths)
    return pl.pallas_call(
        partial(grad_kernel, part=part, rows=rows, widths=widths),
        grid=(4,),
        out_shape=jax.ShapeDtypeStruct((2, 2, 2, 4, rows // 2, total), jnp.bfloat16),
        in_specs=[pl.BlockSpec(memory_space=pltpu.SMEM)] * 2
        + [pl.BlockSpec((count, 4 * rows), lambda z: (0, 0))]
        + [
            pl.BlockSpec((count, 2 * width), lambda z, s=start: (0, s + z))
            for width, start in zip(widths, starts)
        ],
        out_specs=pl.BlockSpec((2, 2, 2, 1, rows // 2, total), lambda z: (0, 0, 0, z, 0, 0)),
        scratch_shapes=[pltpu.VMEM((2 * rows, count), jnp.bfloat16)],
        compiler_params=pltpu.CompilerParams(vmem_limit_bytes=VMEM_BYTES),
        cost_estimate=pl.CostEstimate(
            flops=2 * count * 2 * rows * 8 * total,
            bytes_accessed=2 * count * (4 * rows + 8 * total) + 32 * rows * total,
            transcendentals=0,
        ),
        name="weight_grad",
    )(place["rows"], place["cols"], x, *dys)


class Scatter:
    def __init__(self, values):
        self.values = values
        self.stage = 0

    def advance(self, values):
        if self.stage == 0:
            send, keep = values
            new = (keep, hop(send, "core"))
        elif self.stage == 1:
            keep, came = values
            a_send = keep[0, 1] + came[0, 1]
            b_send = keep[1, :, 1] + came[1, :, 1]
            a_keep = keep[0, 0] + came[0, 0]
            b_keep = keep[1, :, 0] + came[1, :, 0]
            new = (a_keep, hop(a_send, "x"), b_keep, hop(b_send, "y"))
        elif self.stage == 2:
            a_keep, a_came, b_keep, b_came = values
            a_send = a_keep[1] + a_came[1]
            b_send = b_keep[1] + b_came[1]
            new = (a_keep[0] + a_came[0], hop(a_send, "y"), b_keep[0] + b_came[0], hop(b_send, "x"))
        else:
            a_keep, a_came, b_keep, b_came = values
            both = jnp.stack([a_keep + a_came, b_keep + b_came], axis=1)
            mine = lax.psum_scatter(
                both.reshape(-1, both.shape[-1]),
                "win",
                scatter_dimension=0,
                tiled=True,
                axis_index_groups=z_groups(),
            )
            new = mine.astype(jnp.float32)
        self.values = new
        self.stage += 1


class Total:
    def __init__(self, value, links):
        self.shape = value.shape
        self.size = value.size
        self.values = jnp.pad(value.reshape(-1), (0, -value.size % 1024)).reshape(-1, 128)
        self.links = list(links)

    def advance(self, values):
        self.values = values + hop(values, self.links.pop(0))

    def result(self):
        return self.values.reshape(-1)[: self.size].reshape(self.shape)


def together(jobs, state):
    held, state = lax.optimization_barrier(([job.values for job in jobs], state))
    for job, values in zip(jobs, held):
        job.advance(values)
    return state


def pair_table(extent):
    table_dims = (extent, extent, 2 * extent - 1)
    query_pos = lax.broadcasted_iota(jnp.int32, table_dims, 0)
    key_pos = lax.broadcasted_iota(jnp.int32, table_dims, 1)
    offset = lax.broadcasted_iota(jnp.int32, table_dims, 2)
    return (query_pos - key_pos + extent - 1 == offset).astype(jnp.float32)


def spatial_strip(table):
    side = 2 * WS - 1
    onehot = pair_table(WS).transpose(2, 1, 0).reshape(side, WS * WS)
    strip = jnp.dot(table.reshape(HEADS * side, side), onehot, precision=highest)
    strip = strip.reshape(HEADS, side, WS, WS).transpose(0, 2, 1, 3).reshape(HEADS, WS, side * WS)
    return jnp.pad(strip, ((0, 0), (0, 0), (0, WS)))


def spatial_strip_back(strip):
    side = 2 * WS - 1
    onehot = pair_table(WS).transpose(2, 1, 0).reshape(side, WS * WS)
    shaped = strip[:, :, : side * WS].reshape(HEADS, WS, side, WS).transpose(0, 2, 1, 3)
    flat = shaped.reshape(HEADS * side, WS * WS)
    return lax.dot_general(flat, onehot, NT, precision=highest).reshape(HEADS, side, side)


def joint_onehot():
    span = 2 * HS - 1
    table_dims = (span * span, HS**4)
    offset = lax.broadcasted_iota(jnp.int32, table_dims, 0)
    pair = lax.broadcasted_iota(jnp.int32, table_dims, 1)
    key_row, key_col = pair // HS**3, pair // HS**2 % HS
    query_row, query_col = pair // HS % HS, pair % HS
    wanted = (query_row - key_row + HS - 1) * span + query_col - key_col + HS - 1
    return (offset == wanted).astype(jnp.float32)


def joint_strip(table):
    frames = 2 * FR - 1
    places = HS * HS
    strip = jnp.dot(table.reshape(HEADS * frames, -1), joint_onehot(), precision=highest)
    strip = strip.reshape(HEADS, frames, places, places).transpose(0, 2, 1, 3)
    return jnp.pad(strip.reshape(HEADS, places, frames * places), ((0, 0), (0, 0), (0, places)))


def joint_strip_back(strip):
    frames = 2 * FR - 1
    places = HS * HS
    shaped = strip[:, :, : frames * places].reshape(HEADS, places, frames, places).transpose(0, 2, 1, 3)
    flat = shaped.reshape(HEADS * frames, places * places)
    grad = lax.dot_general(flat, joint_onehot(), NT, precision=highest)
    return grad.reshape(HEADS, frames, 2 * HS - 1, 2 * HS - 1)


def head_lanes(which):
    lane = lax.broadcasted_iota(jnp.int32, (1, 128), 1)
    return (lane // 64 == which).astype(jnp.float32)


def attend_kernel(q_ref, k_ref, v_ref, strip_ref, mask_ref, out_ref, probs_ref, bias, *, wins, length):
    rows, lanes = strip_ref.shape[1:]
    blocks = length // rows
    masks = mask_ref.shape[0]
    for head in range(2):
        strip = strip_ref[head]
        for block in range(blocks):
            offset = (blocks - 1 - block) * rows
            turned = strip if offset == 0 else pltpu.roll(strip, lanes - offset, 1)
            bias[block * rows : (block + 1) * rows, :] = turned[:, :length]
        chosen = head_lanes(head)
        low = chosen.astype(jnp.bfloat16)
        for win in range(wins):
            here = slice(win * length, (win + 1) * length)
            queries = q_ref[here, :] * jnp.bfloat16(0.125)
            scores = lax.dot_general(k_ref[here, :] * low, queries, NT, preferred_element_type=jnp.float32)
            scores = jnp.where(mask_ref[win % masks] > 0.0, scores + bias[...], masked_score)
            raised = jnp.exp(scores - jnp.max(scores, axis=0, keepdims=True))
            probs = raised * (1.0 / jnp.sum(raised, axis=0, keepdims=True))
            probs = probs.astype(jnp.bfloat16)
            probs_ref[head, win] = probs
            mixed = lax.dot_general(probs, v_ref[here, :] * low, TN, preferred_element_type=jnp.float32)
            if head == 0:
                out_ref[here, :] = mixed.astype(jnp.bfloat16)
            else:
                out_ref[here, :] = out_ref[here, :] + mixed.astype(jnp.bfloat16)


def attend(qkv, strip, allowed, wins, length):
    count, triple = qkv.shape
    width = triple // 3
    rows, lanes = strip.shape[1:]
    return pl.pallas_call(
        partial(attend_kernel, wins=wins, length=length),
        grid=(HEADS // 2,),
        out_shape=[
            jax.ShapeDtypeStruct((count, width), jnp.bfloat16),
            jax.ShapeDtypeStruct((HEADS, wins, length, length), jnp.bfloat16),
        ],
        in_specs=[
            pl.BlockSpec((count, 128), lambda h: (0, h)),
            pl.BlockSpec((count, 128), lambda h: (0, HEADS // 2 + h)),
            pl.BlockSpec((count, 128), lambda h: (0, HEADS + h)),
            pl.BlockSpec((2, rows, lanes), lambda h: (h, 0, 0)),
            pl.BlockSpec(allowed.shape, lambda h: (0, 0, 0)),
        ],
        out_specs=[
            pl.BlockSpec((count, 128), lambda h: (0, h)),
            pl.BlockSpec((2, wins, length, length), lambda h: (h, 0, 0, 0)),
        ],
        scratch_shapes=[pltpu.VMEM((length, length), jnp.float32)],
        compiler_params=pltpu.CompilerParams(vmem_limit_bytes=VMEM_BYTES),
        cost_estimate=pl.CostEstimate(
            flops=8 * HEADS * wins * length * length * 64,
            bytes_accessed=8 * count * width + 2 * HEADS * wins * length * length,
            transcendentals=HEADS * wins * length * length,
        ),
        name="attend",
    )(qkv, qkv, qkv, strip, allowed)


def attend_back_kernel(q_ref, k_ref, v_ref, g_ref, probs_ref, out_ref, strip_ref, total, *, wins, length):
    rows, lanes = strip_ref.shape[1:]
    blocks = length // rows
    width = out_ref.shape[1] // 3
    step = pl.program_id(0)
    grads = [[None] * 3 for _ in range(wins)]
    total[...] = jnp.zeros_like(total)
    for head in range(2):
        chosen = head_lanes(head)
        low = chosen.astype(jnp.bfloat16)
        for win in range(wins):
            here = slice(win * length, (win + 1) * length)
            queries = q_ref[here, :] * jnp.bfloat16(0.125)
            key_rows = k_ref[here, :]
            outer = g_ref[here, :]
            probs = probs_ref[head, win]
            grad_probs = lax.dot_general(v_ref[here, :] * low, outer, NT, preferred_element_type=jnp.float32)
            wide = probs.astype(jnp.float32)
            inner = jnp.sum(wide * grad_probs, axis=0, keepdims=True)
            grad_scores = (wide * (grad_probs - inner)).astype(jnp.bfloat16)
            if win == 0:
                total[:, :length] = grad_scores.astype(jnp.float32)
            else:
                total[:, :length] = total[:, :length] + grad_scores.astype(jnp.float32)
            new = (
                lax.dot_general(grad_scores, key_rows, TN, preferred_element_type=jnp.float32) * 0.125,
                jnp.dot(grad_scores, queries, preferred_element_type=jnp.float32),
                jnp.dot(probs, outer, preferred_element_type=jnp.float32),
            )
            for kind in range(3):
                column = pl.multiple_of(step * 128 + kind * width, 128)
                if head == 0:
                    out_ref[here, pl.ds(column, 128)] = (new[kind] * chosen).astype(jnp.bfloat16)
                else:
                    out_ref[here, pl.ds(column, 128)] = out_ref[here, pl.ds(column, 128)] + (
                        new[kind] * chosen
                    ).astype(jnp.bfloat16)
        strip = total[:rows, :] if blocks == 1 else pltpu.roll(total[:rows, :], (blocks - 1) * rows, 1)
        for block in range(1, blocks):
            offset = (blocks - 1 - block) * rows
            piece = total[block * rows : (block + 1) * rows, :]
            strip = strip + (piece if offset == 0 else pltpu.roll(piece, offset, 1))
        strip_ref[head] = strip


def attend_back(qkv, probs, grad_out, wins, length, rows, lanes):
    count, triple = qkv.shape
    width = triple // 3
    return pl.pallas_call(
        partial(attend_back_kernel, wins=wins, length=length),
        grid=(HEADS // 2,),
        out_shape=[
            jax.ShapeDtypeStruct((count, triple), jnp.bfloat16),
            jax.ShapeDtypeStruct((HEADS, rows, lanes), jnp.float32),
        ],
        in_specs=[
            pl.BlockSpec((count, 128), lambda h: (0, h)),
            pl.BlockSpec((count, 128), lambda h: (0, HEADS // 2 + h)),
            pl.BlockSpec((count, 128), lambda h: (0, HEADS + h)),
            pl.BlockSpec((count, 128), lambda h: (0, h)),
            pl.BlockSpec((2, wins, length, length), lambda h: (h, 0, 0, 0)),
        ],
        out_specs=[
            pl.BlockSpec((count, triple), lambda h: (0, 0)),
            pl.BlockSpec((2, rows, lanes), lambda h: (h, 0, 0)),
        ],
        scratch_shapes=[pltpu.VMEM((length, lanes), jnp.float32)],
        compiler_params=pltpu.CompilerParams(vmem_limit_bytes=VMEM_BYTES),
        cost_estimate=pl.CostEstimate(
            flops=20 * HEADS * wins * length * length * 64,
            bytes_accessed=14 * count * width + 2 * HEADS * wins * length * length,
            transcendentals=0,
        ),
        name="attend_back",
    )(qkv, qkv, qkv, grad_out, probs)


def plain_norm(values):
    center = values - jnp.mean(values, axis=-1, keepdims=True)
    spread = jnp.mean(center * center, axis=-1, keepdims=True)
    scale = lax.rsqrt(spread + epsilon)
    return center * scale, scale


def modulated_norm(values, shift_vec, scale_vec):
    return (plain_norm(values)[0] * (1.0 + scale_vec) + shift_vec).astype(jnp.bfloat16)


def norm_back(grad_in, values, scale_vec):
    unit, scale = plain_norm(values)
    inner = grad_in * (1.0 + scale_vec)
    mean_one = jnp.mean(inner, axis=-1, keepdims=True)
    mean_two = jnp.mean(inner * unit, axis=-1, keepdims=True)
    grad = scale * (inner - mean_one - unit * mean_two)
    return grad, jnp.sum(grad_in, axis=0), jnp.sum(grad_in * unit, axis=0)


def product(left, right):
    return jnp.dot(left, right, preferred_element_type=jnp.float32)


def product_turned(left, right):
    return lax.dot_general(left, right, NT, preferred_element_type=jnp.float32)


def gelu_both(upward):
    half = 0.5 * (1.0 + lax.erf(upward * 0.7071067811865476))
    density = 0.3989422804014327 * jnp.exp(-0.5 * upward * upward)
    return (upward * half).astype(jnp.bfloat16), (half + upward * density).astype(jnp.bfloat16)


def joint_group(rows):
    split = rows.reshape(FR * HS, 2, HS, rows.shape[-1])
    return split.transpose(1, 0, 2, 3).reshape(rows.shape)


def joint_ungroup(rows):
    split = rows.reshape(2, FR * HS, HS, rows.shape[-1])
    return split.transpose(1, 0, 2, 3).reshape(rows.shape)


def window_group(flat_rows):
    return flat_rows.reshape(SLOTS, WS * WS, flat_rows.shape[-1])


def split_halves(half_rows, own_half):
    pair_windows = half_rows.shape[0]
    filler = jnp.zeros((2 * SLOTS - pair_windows,) + half_rows.shape[1:], half_rows.dtype)
    padded = jnp.concatenate([half_rows, filler], axis=0)
    keep_part = lax.dynamic_slice_in_dim(padded, own_half * SLOTS, SLOTS, 0)
    send_part = lax.dynamic_slice_in_dim(padded, (1 - own_half) * SLOTS, SLOTS, 0)
    return (keep_part, send_part)


def join_windows(keep_part, came_part, own_half):
    upper_half = jnp.where(own_half == 0, keep_part, came_part)
    lower_half = jnp.where(own_half == 0, came_part, keep_part)
    joined = jnp.concatenate([upper_half, lower_half], axis=1)
    return joined.reshape(-1, joined.shape[-1])


def split_windows(win_rows, own_half):
    grouped = window_group(win_rows)
    half_len = grouped.shape[1] // 2
    upper_half = grouped[:, :half_len]
    lower_half = grouped[:, half_len:]
    keep_part = jnp.where(own_half == 0, upper_half, lower_half)
    send_part = jnp.where(own_half == 0, lower_half, upper_half)
    return (keep_part, send_part)


def join_halves(keep_part, came_part, own_half, pair_windows):
    leading = jnp.where(own_half == 0, keep_part, came_part)
    trailing = jnp.where(own_half == 0, came_part, keep_part)
    joined = jnp.concatenate([leading, trailing], axis=0)[:pair_windows]
    return joined.reshape(-1, joined.shape[-1])


def from_pair(value):
    pairs = [(i, i ^ 1) for i in range(lax.axis_size("win"))]
    return lax.ppermute(value, "win", pairs)


def leave_windows(win_rows, own_half, pair_windows):
    keep_part, send_part = split_windows(win_rows, own_half)
    came_part = from_pair(send_part.astype(jnp.bfloat16)).astype(send_part.dtype)
    return join_halves(keep_part, came_part, own_half, pair_windows)


def enter_windows(flat_rows, own_half, pair_windows):
    half_rows = flat_rows.reshape(pair_windows, -1, flat_rows.shape[-1])
    keep_part, send_part = split_halves(half_rows, own_half)
    came_part = from_pair(send_part.astype(jnp.bfloat16)).astype(send_part.dtype)
    return join_windows(keep_part, came_part, own_half)


class Weights:
    def __init__(self, masters, place, quick):
        self.quick = quick
        low = [master.astype(jnp.bfloat16) for master in masters]
        self.place = place
        if quick:
            shards = []
            for block in range(2):
                qkv, out, up, down = low[4 * block : 4 * block + 4]
                shards += [jnp.concatenate([qkv, out], axis=1), up, down]
            self.widths = [(384, 128), (512,), (128,)] * 2
            self.jobs = [Gather(shard) for shard in shards]
        else:
            self.full = [
                lax.all_gather(lax.all_gather(shard, "win", axis=1, tiled=True), "clip", axis=0, tiled=True)
                for shard in low
            ]
            self.full = [tuple(self.full[0:2]), (self.full[2],), (self.full[3],)] + [
                tuple(self.full[4:6]),
                (self.full[6],),
                (self.full[7],),
            ]

    def round(self, active, state):
        if not self.quick:
            return state
        return together([self.jobs[unit] for unit in active], state)

    def take(self, unit):
        if not self.quick:
            return self.full[unit]
        job = self.jobs[unit]
        return assemble(job.values, self.place, job.rows, self.widths[unit])


def body(
    tokens,
    grad_output,
    clip_height,
    clip_width,
    modulation,
    sp_qkv,
    sp_out,
    sp_up,
    sp_down,
    sp_table,
    st_qkv,
    st_out,
    st_up,
    st_down,
    st_table,
    quick,
):
    model_width = tokens.shape[-1]
    half_len = tokens.shape[-2]
    pair_windows = PAIR_LOCS * FR
    shard_index = lax.axis_index("win")
    clip_index = lax.axis_index("clip")
    pair_index = shard_index // 2
    own_half = shard_index % 2
    own_core = clip_index % 2
    own_x = clip_index // 2
    row_places = [
        (own_x ^ x_rel) * 2 + (own_core ^ c_rel) for c_rel in range(2) for x_rel in range(2)
    ]
    place = {
        "rows": jnp.stack(row_places).astype(jnp.int32),
        "cols": jnp.stack([own_half, own_half ^ 1]).astype(jnp.int32),
    }
    weights = Weights(
        (sp_qkv, sp_out, sp_up, sp_down, st_qkv, st_out, st_up, st_down), place, quick
    )
    mod = modulation[0]

    location = pair_index
    token_ids = jnp.arange(WS * WS, dtype=jnp.int32)
    row_pos = location // LOC_W * WS + token_ids // WS
    col_pos = location % LOC_W * WS + token_ids % WS
    sp_valid = (row_pos < clip_height[0]) & (col_pos < clip_width[0])
    sp_allowed = (sp_valid[None, :, None] | jnp.eye(WS * WS, dtype=bool)[None]).astype(jnp.float32)
    joint_len = FR * HS * HS
    joint_ids = jnp.arange(joint_len, dtype=jnp.int32)
    joint_row = location // LOC_W * WS + own_half * HS + joint_ids // HS % HS
    joint_col = location % LOC_W * WS + jnp.arange(2, dtype=jnp.int32)[:, None] * HS + joint_ids[None] % HS
    st_valid = (joint_row[None] < clip_height[0]) & (joint_col < clip_width[0])
    st_allowed = (st_valid[:, :, None] | jnp.eye(joint_len, dtype=bool)[None]).astype(jnp.float32)

    half_tokens = tokens.reshape(pair_windows, half_len, model_width)
    win_input = enter_windows(half_tokens, own_half, pair_windows).astype(jnp.float32)
    sp_strip = spatial_strip(sp_table)
    st_strip = joint_strip(st_table)
    attn_in_a = modulated_norm(win_input, mod[0], mod[1])

    state = (win_input, attn_in_a)
    state = weights.round([0], state)
    state = weights.round([0], state)
    state = weights.round([0, 1], state)
    win_input, attn_in_a = weights.round([1], state)
    w_qkv_a, w_out_a = weights.take(0)
    qkv_a = product(attn_in_a, w_qkv_a).astype(jnp.bfloat16)
    win_input, qkv_a, w_out_a = weights.round([2], (win_input, qkv_a, w_out_a))
    attn_out_a, probs_a = attend(qkv_a, sp_strip, sp_allowed, SLOTS, WS * WS)
    win_input, attn_out_a, w_out_a = weights.round([1], (win_input, attn_out_a, w_out_a))
    mixed_a = product(attn_out_a, w_out_a)
    win_middle = win_input + mod[2] * mixed_a
    middle_a = joint_group(leave_windows(win_middle, own_half, pair_windows))
    mlp_in_a = modulated_norm(middle_a, mod[3], mod[4])

    middle_a, mlp_in_a = weights.round([2, 3], (middle_a, mlp_in_a))
    (w_up_a,) = weights.take(1)
    hidden_a, slope_a = gelu_both(product(mlp_in_a, w_up_a))
    middle_a, hidden_a, slope_a = weights.round([2], (middle_a, hidden_a, slope_a))

    middle_a, hidden_a = weights.round([3, 4], (middle_a, hidden_a))
    (w_down_a,) = weights.take(2)
    downward_a = product(hidden_a, w_down_a)
    first_out = middle_a + mod[5] * downward_a
    attn_in_b = modulated_norm(first_out, mod[6], mod[7])
    first_out, attn_in_b = weights.round([3], (first_out, attn_in_b))

    first_out, attn_in_b = weights.round([4, 5], (first_out, attn_in_b))
    w_qkv_b, w_out_b = weights.take(3)
    qkv_b = product(attn_in_b, w_qkv_b).astype(jnp.bfloat16)
    first_out, qkv_b, w_out_b = weights.round([4], (first_out, qkv_b, w_out_b))
    attn_out_b, probs_b = attend(qkv_b, st_strip, st_allowed, 2, joint_len)
    mixed_b = product(attn_out_b, w_out_b)
    middle_b = first_out + mod[8] * mixed_b
    mlp_in_b = modulated_norm(middle_b, mod[9], mod[10])

    middle_b, mlp_in_b = weights.round([5], (middle_b, mlp_in_b))
    (w_up_b,) = weights.take(4)
    hidden_b, slope_b = gelu_both(product(mlp_in_b, w_up_b))
    middle_b, hidden_b, slope_b = weights.round([5], (middle_b, hidden_b, slope_b))
    (w_down_b,) = weights.take(5)
    downward_b = product(hidden_b, w_down_b)
    out_rows = middle_b + mod[11] * downward_b
    out_tokens = joint_ungroup(out_rows).reshape(tokens.shape)

    def start_grad(x, dys, rows, widths, starts):
        if quick:
            return Scatter(
                tuple(weight_grad(x, dys, place, part, rows, widths, starts) for part in (1, 0))
            )
        return Plain(x, dys, widths, starts)

    def rounds(jobs, state):
        if quick:
            return together(jobs, state)
        return state

    grad_out_b = joint_group(grad_output.reshape(-1, model_width)).astype(jnp.float32)
    grad_down_b = (mod[11] * grad_out_b).astype(jnp.bfloat16)
    grad_gate_mb = jnp.sum(grad_out_b * downward_b, axis=0)
    d_st_down = start_grad(hidden_b, [grad_down_b], 1024, (128,), (0,))
    grad_down_b = rounds([d_st_down], grad_down_b)
    grad_up_b = (product_turned(grad_down_b, w_down_b) * slope_b).astype(jnp.bfloat16)
    grad_up_b = rounds([d_st_down], grad_up_b)
    d_st_up = start_grad(mlp_in_b, [grad_up_b], 256, (512,), (0,))
    grad_up_b = rounds([d_st_up, d_st_down], grad_up_b)
    grad_mlp_b = product_turned(grad_up_b, w_up_b)
    norm_grad, grad_shift_mb, grad_scale_mb = norm_back(grad_mlp_b, middle_b, mod[10])
    grad_middle_b = grad_out_b + norm_grad
    grad_mixed_b = (mod[8] * grad_middle_b).astype(jnp.bfloat16)
    grad_gate_ab = jnp.sum(grad_middle_b * mixed_b, axis=0)
    grad_middle_b, grad_mixed_b = rounds([d_st_up, d_st_down], (grad_middle_b, grad_mixed_b))
    d_st_out = start_grad(attn_out_b, [grad_mixed_b], 256, (128,), (0,))
    grad_attn_b = product_turned(grad_mixed_b, w_out_b).astype(jnp.bfloat16)
    grad_qkv_b, strip_grad_b = attend_back(
        qkv_b, probs_b, grad_attn_b, 2, joint_len, st_strip.shape[1], st_strip.shape[2]
    )
    grad_middle_b, grad_qkv_b = rounds([d_st_out, d_st_up], (grad_middle_b, grad_qkv_b))
    st_total = Total(joint_strip_back(strip_grad_b), ("x", "core", "y", "z0", "z1"))
    d_st_qkv = start_grad(attn_in_b, [grad_qkv_b, grad_qkv_b], 256, (256, 128), (0, 8))
    grad_middle_b, grad_qkv_b = rounds(
        [d_st_qkv, d_st_out, d_st_up], (grad_middle_b, grad_qkv_b)
    )
    grad_in_b = product_turned(grad_qkv_b, w_qkv_b)
    norm_grad, grad_shift_ab, grad_scale_ab = norm_back(grad_in_b, first_out, mod[7])
    grad_first = grad_middle_b + norm_grad
    grad_down_a = (mod[5] * grad_first).astype(jnp.bfloat16)
    grad_gate_ma = jnp.sum(grad_first * downward_a, axis=0)
    grad_first, grad_down_a = rounds([d_st_qkv, d_st_out, st_total], (grad_first, grad_down_a))

    d_sp_down = start_grad(hidden_a, [grad_down_a], 1024, (128,), (0,))
    grad_first, grad_down_a = rounds(
        [d_sp_down, d_st_qkv, d_st_out, st_total], (grad_first, grad_down_a)
    )
    grad_up_a = (product_turned(grad_down_a, w_down_a) * slope_a).astype(jnp.bfloat16)
    d_sp_up = start_grad(mlp_in_a, [grad_up_a], 256, (512,), (0,))
    grad_first, grad_up_a = rounds([d_sp_down, d_sp_up, d_st_qkv, st_total], (grad_first, grad_up_a))
    grad_mlp_a = product_turned(grad_up_a, w_up_a)
    norm_grad, grad_shift_ma, grad_scale_ma = norm_back(grad_mlp_a, middle_a, mod[4])
    grad_middle_a = joint_ungroup(grad_first + norm_grad)
    grad_win = enter_windows(grad_middle_a, own_half, pair_windows)
    grad_mixed_a = (mod[2] * grad_win).astype(jnp.bfloat16)
    grad_gate_aa = jnp.sum(grad_win * mixed_a, axis=0)
    grad_win, grad_mixed_a = rounds([d_sp_up, d_sp_down, st_total], (grad_win, grad_mixed_a))
    d_sp_out = start_grad(attn_out_a, [grad_mixed_a], 256, (128,), (0,))
    grad_attn_a = product_turned(grad_mixed_a, w_out_a).astype(jnp.bfloat16)
    grad_qkv_a, strip_grad_a = attend_back(
        qkv_a, probs_a, grad_attn_a, SLOTS, WS * WS, sp_strip.shape[1], sp_strip.shape[2]
    )
    grad_win, grad_qkv_a = rounds([d_sp_out, d_sp_up, d_sp_down, st_total], (grad_win, grad_qkv_a))
    sp_total = Total(spatial_strip_back(strip_grad_a), ("x", "core", "y", "z0", "z1"))
    d_sp_qkv = start_grad(attn_in_a, [grad_qkv_a], 256, (384,), (0,))
    grad_win, grad_qkv_a = rounds([d_sp_qkv, d_sp_out, d_sp_up, sp_total], (grad_win, grad_qkv_a))
    grad_in_a = product_turned(grad_qkv_a, w_qkv_a)
    norm_grad, grad_shift_aa, grad_scale_aa = norm_back(grad_in_a, win_input, mod[1])
    mod_rows = [
        grad_shift_aa,
        grad_scale_aa,
        grad_gate_aa,
        grad_shift_ma,
        grad_scale_ma,
        grad_gate_ma,
        grad_shift_ab,
        grad_scale_ab,
        grad_gate_ab,
        grad_shift_mb,
        grad_scale_mb,
        grad_gate_mb,
    ]
    mod_total = Total(jnp.stack(mod_rows, axis=0), ("y", "z0", "z1"))
    win_sum = grad_win + norm_grad
    win_sum = rounds([d_sp_qkv, d_sp_out, sp_total, mod_total], win_sum)
    grad_tokens = leave_windows(win_sum, own_half, pair_windows).reshape(tokens.shape)
    grad_tokens = rounds([d_sp_qkv, d_sp_out, sp_total, mod_total], grad_tokens)
    rounds([d_sp_qkv, sp_total, mod_total], ())
    rounds([sp_total], ())
    if quick:
        grad_modulation = mod_total.result()[None]
        grad_sp_table = sp_total.result()
        grad_st_table = st_total.result()
    else:
        grad_modulation = lax.psum(jnp.stack(mod_rows, axis=0), "win")[None]
        grad_sp_table = lax.psum(sp_total.result(), ("clip", "win"))
        grad_st_table = lax.psum(st_total.result(), ("clip", "win"))
    value_width = d_st_out.values.shape[1]
    return (
        out_tokens,
        grad_tokens,
        grad_modulation,
        d_sp_qkv.values,
        d_sp_out.values,
        d_sp_up.values,
        d_sp_down.values,
        grad_sp_table,
        d_st_qkv.values[:, :-value_width],
        d_st_qkv.values[:, -value_width:],
        d_st_out.values,
        d_st_up.values,
        d_st_down.values,
        grad_st_table,
    )


class Plain:
    def __init__(self, x, dys, widths, starts):
        win = lax.axis_size("win")
        grads = []
        for dy, width, start in zip(dys, widths, starts):
            part = dy[:, start * 2 * width : start * 2 * width + 8 * width]
            full = lax.dot_general(x, part, TN, preferred_element_type=jnp.float32)
            full = lax.psum_scatter(
                full.astype(jnp.bfloat16), "clip", scatter_dimension=0, tiled=True
            )
            grads.append(lax.psum_scatter(full, "win", scatter_dimension=1, tiled=True))
        self.values = jnp.concatenate(grads, axis=1).astype(jnp.float32)


def solution(mesh):
    grid = P("clip", "win")
    whole = P("clip", "win", None, None, None, None)
    in_specs = (whole, whole, P("clip"), P("clip"), P("clip", None, None)) + ((grid,) * 4 + (P(),)) * 2
    out_specs = (whole, whole, P("clip", None, None)) + (grid,) * 4 + (P(),) + (grid,) * 5 + (P(),)
    quick = mesh.shape["clip"] == 4 and mesh.shape["win"] == 8
    return jax.shard_map(
        partial(body, quick=quick), mesh=mesh, in_specs=in_specs, out_specs=out_specs, check_vma=False
    )
```

```python
from functools import partial
from typing import NamedTuple

import jax
import jax.numpy as jnp
from jax import lax
from jax.experimental import pallas as pl
from jax.experimental.pallas import tpu as pltpu
from jax.sharding import PartitionSpec as P

HEADS = 16
WS = 16
FR = 5
LOC_W = 4
PAIR_LOCS = 1
HS = 8
SLOTS = 3
VMEM_BYTES = 56 * 1024 * 1024

SMALL = pl.CostEstimate(flops=1, bytes_accessed=1, transcendentals=0)

epsilon = 1e-06
masked_score = -1000000000.0
highest = lax.Precision.HIGHEST
NT = (((1,), (1,)), ((), ()))
TN = (((0,), (0,)), ((), ()))


BITS = {"core": ("clip", 1), "x": ("clip", 2), "y": ("win", 1), "z0": ("win", 2), "z1": ("win", 4)}


def hop(value, link):
    axis, mask = BITS[link]
    return lax.ppermute(value, axis, [(i, i ^ mask) for i in range(lax.axis_size(axis))])


def z_groups():
    size = lax.axis_size("win")
    return [list(range(start, size, 2)) for start in range(2)]


class Gather:
    def __init__(self, shard):
        rows, cols = shard.shape
        self.rows = rows
        halves = shard.reshape(2, rows // 2, cols)
        grown = lax.all_gather(halves, "win", axis=1, tiled=False, axis_index_groups=z_groups())
        self.held = {"grown": (grown,)}

    def needs(self, move):
        return {"near": "grown", "far": "near", "core_near": "own", "core_far": "away"}[move]

    def go(self, move):
        values = self.held[self.needs(move)]
        if move == "near":
            (grown,) = values
            a0, b0 = grown[0], grown[1]
            self.held["near"] = (a0, hop(a0, "y"), b0, hop(b0, "x"))
        elif move == "far":
            a0, a_came, b0, b_came = values
            a1, b1 = jnp.stack([a0, a_came]), jnp.stack([b0, b_came])
            self.held["own"] = (a1, b1)
            self.held["away"] = (hop(a1, "x"), hop(b1, "y"))
        else:
            self.held[move] = tuple(hop(value, "core") for value in values)

    def values(self):
        pairs = [self.held[name] for name in ("own", "away", "core_near", "core_far")]
        return [pair[0] for pair in pairs] + [pair[1] for pair in pairs]


def gathered_kernel(row_of, y_of, x_ref, *refs, rows, widths, kind):
    count = len(widths)
    results = 2 if kind == "gelu" else 1
    pieces, refs = refs[:8], refs[8:]
    outs, wholes, held = refs[:results], refs[results : results + count], refs[results + count : -2]
    in_sems, out_sems = refs[-2:]
    half = rows // 2
    step = pl.program_id(0)

    def arrivals(z):
        copies = []
        for part in range(2):
            for c_rel in range(2):
                for x_rel in range(2):
                    row = row_of[c_rel * 2 + x_rel] * rows + part * half
                    row = pl.multiple_of(row, half)
                    for y_rel in range(2):
                        far, near = (x_rel, y_rel) if part == 0 else (y_rel, x_rel)
                        source = pieces[part * 4 + c_rel * 2 + far]
                        start = 0
                        for matrix, width in zip(held, widths):
                            col = pl.multiple_of((z * 2 + y_of[y_rel]) * width, 128)
                            copies.append(
                                pltpu.make_async_copy(
                                    source.at[near, z, :, pl.ds(start, width)],
                                    matrix.at[pl.ds(row, half), pl.ds(col, width)],
                                    in_sems.at[z * 16 * count + len(copies)],
                                )
                            )
                            start += width
        return copies

    def departures(z):
        copies = []
        for which, width in enumerate(widths):
            there = pl.ds(pl.multiple_of(z * 2 * width, 128), 2 * width)
            copies.append(
                pltpu.make_async_copy(
                    held[which].at[:, there], wholes[which].at[:, there], out_sems.at[z * count + which]
                )
            )
        return copies

    @pl.when(step == 0)
    def begin():
        for z in range(4):
            for copy in arrivals(z):
                copy.start()

    for copy in arrivals(step):
        copy.wait()
    for copy in departures(step):
        copy.start()
    wide = 2 * widths[0]
    chunk = 256 if kind == "gelu" else wide
    for first in range(0, wide, chunk):
        col = pl.multiple_of(step * wide + first, 128)
        there = slice(first, first + chunk)
        result = jnp.dot(
            x_ref[...], held[0][:, pl.ds(col, chunk)], preferred_element_type=jnp.float32
        )
        if kind == "gelu":
            outs[0][:, there], outs[1][:, there] = gelu_both(result)
        else:
            outs[0][:, there] = result.astype(outs[0].dtype)

    @pl.when(step == 3)
    def end():
        for z in range(4):
            for copy in departures(z):
                copy.wait()


def gathered(values, place, x, rows, widths, kind):
    shapes = [(4 * rows, 8 * width) for width in widths]
    results = 2 if kind == "gelu" else 1
    kept = jnp.float32 if kind == "wide" else jnp.bfloat16
    count = x.shape[0]
    return pl.pallas_call(
        partial(gathered_kernel, rows=rows, widths=widths, kind=kind),
        grid=(4,),
        out_shape=[jax.ShapeDtypeStruct((count, 8 * widths[0]), kept)] * results
        + [jax.ShapeDtypeStruct(shape, jnp.bfloat16) for shape in shapes],
        in_specs=[pl.BlockSpec(memory_space=pltpu.SMEM)] * 2
        + [pl.BlockSpec(x.shape, lambda z: (0, 0))]
        + [pl.BlockSpec(memory_space=pl.ANY)] * 8,
        out_specs=[pl.BlockSpec((count, 2 * widths[0]), lambda z: (0, z))] * results
        + [pl.BlockSpec(memory_space=pl.ANY)] * len(widths),
        scratch_shapes=[pltpu.VMEM(shape, jnp.bfloat16) for shape in shapes]
        + [pltpu.SemaphoreType.DMA((64 * len(widths),)), pltpu.SemaphoreType.DMA((4 * len(widths),))],
        compiler_params=pltpu.CompilerParams(vmem_limit_bytes=VMEM_BYTES),
        cost_estimate=SMALL,
        name="gathered",
    )(place["rows"], place["cols"], x, *values)


def product_kernel(left, right, out, *, turned):
    if turned:
        result = lax.dot_general(left[...], right[...], NT, preferred_element_type=jnp.float32)
    else:
        result = jnp.dot(left[...], right[...], preferred_element_type=jnp.float32)
    out[...] = result.astype(out.dtype)


def scaled_kernel(left, right, factor, out):
    result = lax.dot_general(left[...], right[...], NT, preferred_element_type=jnp.float32)
    out[...] = (result * factor[...].astype(jnp.float32)).astype(out.dtype)


def tiled(kernel, left, right, columns, kept, turned, *factors):
    count = left.shape[0]
    total = right.shape[0] if turned else right.shape[1]
    block = pl.BlockSpec((count, columns), lambda i: (0, i))
    if turned:
        right_spec = pl.BlockSpec((columns, right.shape[1]), lambda i: (i, 0))
    else:
        right_spec = pl.BlockSpec((right.shape[0], columns), lambda i: (0, i))
    return pl.pallas_call(
        kernel,
        grid=(total // columns,),
        out_shape=jax.ShapeDtypeStruct((count, total), kept),
        in_specs=[pl.BlockSpec(left.shape, lambda i: (0, 0)), right_spec] + [block] * len(factors),
        out_specs=block,
        compiler_params=pltpu.CompilerParams(vmem_limit_bytes=VMEM_BYTES),
        cost_estimate=SMALL,
        name="product",
    )(left, right, *factors)


def product(left, right):
    return tiled(partial(product_kernel, turned=False), left, right, 512, jnp.float32, False)


def product_turned(left, right, kept=jnp.float32):
    columns = 512 if right.shape[1] == 1024 else 256
    return tiled(partial(product_kernel, turned=True), left, right, columns, kept, True)


def product_scaled(left, right, factor):
    return tiled(scaled_kernel, left, right, 1024, jnp.bfloat16, True, factor)


def grad_kernel(row_of, y_of, *refs, rows, widths, sources, kinds):
    count = len(widths)
    lefts = max(sources) + 1
    refs = list(refs)
    x_refs = [refs.pop(0) for _ in range(lefts)]
    dy_refs = [refs.pop(0) for _ in range(count)]
    old_refs = [[refs.pop(0) for _ in range(FOLDS[kind].takes)] for kind in kinds]
    send, keep = refs.pop(0), refs.pop(0)
    new_refs = [[refs.pop(0) for _ in range(FOLDS[kind].gives)] for kind in kinds]
    turns = refs
    half = rows // 2

    @pl.when(pl.program_id(0) == 0)
    def turn():
        for x_ref, turned in zip(x_refs, turns):
            for place in range(4):
                start = pl.multiple_of(row_of[place] * rows, 128)
                turned[place * rows : (place + 1) * rows, :] = x_ref[:, pl.ds(start, rows)].T

    offset = 0
    for dy_ref, width, source in zip(dy_refs, widths, sources):
        turned = turns[source]
        sides = [
            dy_ref[:, pl.ds(pl.multiple_of(y_of[y_rel] * width, 128), width)] for y_rel in range(2)
        ]
        product = jnp.dot(
            turned[...], jnp.concatenate(sides, axis=1), preferred_element_type=jnp.float32
        ).astype(jnp.bfloat16)
        for c_rel, out in ((0, keep), (1, send)):
            for x_rel in range(2):
                for ab in range(2):
                    first = (c_rel * 2 + x_rel) * rows + ab * half
                    for y_rel in range(2):
                        out[ab, x_rel, y_rel, 0, :, offset : offset + width] = product[
                            first : first + half, y_rel * width : (y_rel + 1) * width
                        ]
        offset += width
    for kind, old, new in zip(kinds, old_refs, new_refs):
        FOLDS[kind].kernel(*old, *new)


def fold_first(old_keep, old_came, a_send, a_keep, b_send, b_keep):
    for near in range(2):
        a_send[near] = old_keep[0, 1, near] + old_came[0, 1, near]
        a_keep[near] = old_keep[0, 0, near] + old_came[0, 0, near]
        b_send[near] = old_keep[1, near, 1] + old_came[1, near, 1]
        b_keep[near] = old_keep[1, near, 0] + old_came[1, near, 0]


def fold_second(a_keep, a_came, b_keep, b_came, a_out, a_held, b_out, b_held):
    a_out[...] = a_keep[1] + a_came[1]
    a_held[...] = a_keep[0] + a_came[0]
    b_out[...] = b_keep[1] + b_came[1]
    b_held[...] = b_keep[0] + b_came[0]


def fold_third(a_keep, a_came, b_keep, b_came, both):
    both[:, 0] = a_keep[...] + a_came[...]
    both[:, 1] = b_keep[...] + b_came[...]


class Part(NamedTuple):
    lead: tuple

    def shape(self, tail):
        return jax.ShapeDtypeStruct(self.lead + tail, jnp.bfloat16)

    def spec(self, tail):
        where = self.lead.index(4)
        block = tuple(1 if dim == where else size for dim, size in enumerate(self.lead))
        return pl.BlockSpec(
            block + tail, lambda z: (0,) * where + (z,) + (0,) * (len(block) + 1 - where)
        )


WHOLE, QUARTER, EIGHTH, TURNED = Part((2, 2, 2, 4)), Part((2, 4)), Part((4,)), Part((4, 2))


class Fold(NamedTuple):
    kernel: object
    takes: int
    takes_part: Part
    gives: int
    gives_part: Part


FOLDS = {
    1: Fold(fold_first, 2, WHOLE, 4, QUARTER),
    2: Fold(fold_second, 4, QUARTER, 4, EIGHTH),
    3: Fold(fold_third, 4, EIGHTH, 1, TURNED),
}


def weight_grad(xs, dys, place, rows, widths, starts, sources, olders):
    count = xs[0].shape[0]
    tail = (rows // 2, sum(widths))
    kinds = tuple(older.stage for older in olders)
    out_shape, out_specs = [WHOLE.shape(tail)] * 2, [WHOLE.spec(tail)] * 2
    old_specs, old_values = [], []
    for older, kind in zip(olders, kinds):
        fold = FOLDS[kind]
        old_tail = older.values[0].shape[-2:]
        old_specs += [fold.takes_part.spec(old_tail)] * fold.takes
        old_values += older.values
        out_shape += [fold.gives_part.shape(old_tail)] * fold.gives
        out_specs += [fold.gives_part.spec(old_tail)] * fold.gives
    outs = pl.pallas_call(
        partial(grad_kernel, rows=rows, widths=widths, sources=sources, kinds=kinds),
        grid=(4,),
        out_shape=out_shape,
        in_specs=[pl.BlockSpec(memory_space=pltpu.SMEM)] * 2
        + [pl.BlockSpec((count, 4 * rows), lambda z: (0, 0))] * len(xs)
        + [
            pl.BlockSpec((count, 2 * width), lambda z, s=start: (0, s + z))
            for width, start in zip(widths, starts)
        ]
        + old_specs,
        out_specs=out_specs,
        scratch_shapes=[pltpu.VMEM((4 * rows, count), jnp.bfloat16)] * len(xs),
        compiler_params=pltpu.CompilerParams(vmem_limit_bytes=VMEM_BYTES),
        cost_estimate=SMALL,
        name="weight_grad",
    )(place["rows"], place["cols"], *xs, *dys, *old_values)
    outs = list(outs)
    values = tuple(outs.pop(0) for _ in range(2))
    for older, kind in zip(olders, kinds):
        older.values = tuple(outs.pop(0) for _ in range(FOLDS[kind].gives))
    return values


class Scatter:
    def __init__(self, xs, dys, place, rows, widths, starts, sources, olders):
        self.values = weight_grad(xs, dys, place, rows, widths, starts, sources, olders)
        self.stage = 0

    def fold(self):
        fold = FOLDS[self.stage]
        outs = pl.pallas_call(
            fold.kernel,
            out_shape=[fold.gives_part.shape(self.values[0].shape[-2:])] * fold.gives,
            compiler_params=pltpu.CompilerParams(vmem_limit_bytes=VMEM_BYTES),
            cost_estimate=SMALL,
            name=fold.kernel.__name__,
        )(*self.values)
        self.values = tuple(outs)

    def advance(self, values):
        if self.stage == 0:
            send, keep = values
            new = (keep, hop(send, "core"))
        elif self.stage == 1:
            a_send, a_keep, b_send, b_keep = values
            new = (a_keep, hop(a_send, "x"), b_keep, hop(b_send, "y"))
        elif self.stage == 2:
            a_send, a_keep, b_send, b_keep = values
            new = (a_keep, hop(a_send, "y"), b_keep, hop(b_send, "x"))
        else:
            mine = lax.psum_scatter(
                values[0].reshape(-1, values[0].shape[-1]),
                "win",
                scatter_dimension=0,
                tiled=True,
                axis_index_groups=z_groups(),
            )
            new = mine.astype(jnp.float32)
        self.values = new
        self.stage += 1


class Total:
    def __init__(self, value, links):
        self.shape = value.shape
        self.size = value.size
        self.values = jnp.pad(value.reshape(-1), (0, -value.size % 1024)).reshape(-1, 128)
        self.links = list(links)

    def advance(self, values):
        self.values = values + hop(values, self.links.pop(0))

    def result(self):
        return self.values.reshape(-1)[: self.size].reshape(self.shape)


def together(jobs, state):
    held, state = lax.optimization_barrier(([job.values for job in jobs], state))
    for job, values in zip(jobs, held):
        job.advance(values)
    return state


def pair_table(extent):
    table_dims = (extent, extent, 2 * extent - 1)
    query_pos = lax.broadcasted_iota(jnp.int32, table_dims, 0)
    key_pos = lax.broadcasted_iota(jnp.int32, table_dims, 1)
    offset = lax.broadcasted_iota(jnp.int32, table_dims, 2)
    return (query_pos - key_pos + extent - 1 == offset).astype(jnp.float32)


def spatial_strip(table):
    side = 2 * WS - 1
    onehot = pair_table(WS).transpose(2, 1, 0).reshape(side, WS * WS)
    strip = jnp.dot(table.reshape(HEADS * side, side), onehot, precision=highest)
    strip = strip.reshape(HEADS, side, WS, WS).transpose(0, 2, 1, 3).reshape(HEADS, WS, side * WS)
    return jnp.pad(strip, ((0, 0), (0, 0), (0, WS)))


def spatial_strip_back(strip):
    side = 2 * WS - 1
    onehot = pair_table(WS).transpose(2, 1, 0).reshape(side, WS * WS)
    shaped = strip[:, :, : side * WS].reshape(HEADS, WS, side, WS).transpose(0, 2, 1, 3)
    flat = shaped.reshape(HEADS * side, WS * WS)
    return lax.dot_general(flat, onehot, NT, precision=highest).reshape(HEADS, side, side)


def joint_onehot():
    span = 2 * HS - 1
    table_dims = (span * span, HS**4)
    offset = lax.broadcasted_iota(jnp.int32, table_dims, 0)
    pair = lax.broadcasted_iota(jnp.int32, table_dims, 1)
    key_row, key_col = pair // HS**3, pair // HS**2 % HS
    query_row, query_col = pair // HS % HS, pair % HS
    wanted = (query_row - key_row + HS - 1) * span + query_col - key_col + HS - 1
    return (offset == wanted).astype(jnp.float32)


def joint_strip(table):
    frames = 2 * FR - 1
    places = HS * HS
    strip = jnp.dot(table.reshape(HEADS * frames, -1), joint_onehot(), precision=highest)
    strip = strip.reshape(HEADS, frames, places, places).transpose(0, 2, 1, 3)
    return jnp.pad(strip.reshape(HEADS, places, frames * places), ((0, 0), (0, 0), (0, places)))


def joint_strip_back(strip):
    frames, span, lanes = 2 * FR - 1, 2 * HS - 1, 2 * HS * HS
    shaped = strip.reshape(HEADS, HS, frames, lanes).transpose(0, 2, 1, 3)
    table_dims = (span * span, HS * lanes)
    offset = lax.broadcasted_iota(jnp.int32, table_dims, 0)
    pair = lax.broadcasted_iota(jnp.int32, table_dims, 1)
    wanted = pair // HS % (2 * HS) * span + pair % HS - pair // lanes + HS - 1
    onehot = ((offset == wanted) & (pair // HS % (2 * HS) < span)).astype(jnp.float32)
    flat = shaped.reshape(HEADS * frames, HS * lanes)
    grad = lax.dot_general(flat, onehot, NT, precision=highest)
    return grad.reshape(HEADS, frames, span, span)


def head_lanes(which):
    lane = lax.broadcasted_iota(jnp.int32, (1, 128), 1)
    return (lane // 64 == which).astype(jnp.float32)


def attend_kernel(q_ref, k_ref, v_ref, strip_ref, mask_ref, out_ref, probs_ref, bias, *, wins, length):
    rows, lanes = strip_ref.shape[1:]
    blocks = length // rows
    masks = mask_ref.shape[0]
    for head in range(2):
        strip = strip_ref[head]
        for block in range(blocks):
            offset = (blocks - 1 - block) * rows
            turned = strip if offset == 0 else pltpu.roll(strip, lanes - offset, 1)
            bias[block * rows : (block + 1) * rows, :] = turned[:, :length]
        chosen = head_lanes(head)
        low = chosen.astype(jnp.bfloat16)
        for win in range(wins):
            here = slice(win * length, (win + 1) * length)
            queries = q_ref[here, :] * jnp.bfloat16(0.125)
            scores = lax.dot_general(k_ref[here, :] * low, queries, NT, preferred_element_type=jnp.float32)
            scores = jnp.where(mask_ref[win % masks] > 0.0, scores + bias[...], masked_score)
            raised = jnp.exp(scores - jnp.max(scores, axis=0, keepdims=True))
            probs = raised * (1.0 / jnp.sum(raised, axis=0, keepdims=True))
            probs = probs.astype(jnp.bfloat16)
            probs_ref[head, win] = probs
            mixed = lax.dot_general(probs, v_ref[here, :] * low, TN, preferred_element_type=jnp.float32)
            if head == 0:
                out_ref[here, :] = mixed.astype(jnp.bfloat16)
            else:
                out_ref[here, :] = out_ref[here, :] + mixed.astype(jnp.bfloat16)


def attend(qkv, strip, allowed, wins, length):
    count, triple = qkv.shape
    width = triple // 3
    rows, lanes = strip.shape[1:]
    return pl.pallas_call(
        partial(attend_kernel, wins=wins, length=length),
        grid=(HEADS // 2,),
        out_shape=[
            jax.ShapeDtypeStruct((count, width), jnp.bfloat16),
            jax.ShapeDtypeStruct((HEADS, wins, length, length), jnp.bfloat16),
        ],
        in_specs=[
            pl.BlockSpec((count, 128), lambda h: (0, h)),
            pl.BlockSpec((count, 128), lambda h: (0, HEADS // 2 + h)),
            pl.BlockSpec((count, 128), lambda h: (0, HEADS + h)),
            pl.BlockSpec((2, rows, lanes), lambda h: (h, 0, 0)),
            pl.BlockSpec(allowed.shape, lambda h: (0, 0, 0)),
        ],
        out_specs=[
            pl.BlockSpec((count, 128), lambda h: (0, h)),
            pl.BlockSpec((2, wins, length, length), lambda h: (h, 0, 0, 0)),
        ],
        scratch_shapes=[pltpu.VMEM((length, length), jnp.float32)],
        compiler_params=pltpu.CompilerParams(vmem_limit_bytes=VMEM_BYTES),
        cost_estimate=SMALL,
        name="attend",
    )(qkv, qkv, qkv, strip, allowed)


def attend_back_kernel(
    q_ref, k_ref, v_ref, g_ref, probs_ref, out_ref, strip_ref, total, *, wins, length, rows
):
    blocks = length // rows
    width = out_ref.shape[1] // 3
    step = pl.program_id(0)
    grads = [[None] * 3 for _ in range(wins)]
    total[...] = jnp.zeros_like(total)
    for head in range(2):
        chosen = head_lanes(head)
        low = chosen.astype(jnp.bfloat16)
        for win in range(wins):
            here = slice(win * length, (win + 1) * length)
            queries = q_ref[here, :] * jnp.bfloat16(0.125)
            key_rows = k_ref[here, :]
            outer = g_ref[here, :]
            probs = probs_ref[head, win]
            grad_probs = lax.dot_general(v_ref[here, :] * low, outer, NT, preferred_element_type=jnp.float32)
            wide = probs.astype(jnp.float32)
            inner = jnp.sum(wide * grad_probs, axis=0, keepdims=True)
            grad_scores = (wide * (grad_probs - inner)).astype(jnp.bfloat16)
            if win == 0:
                total[:, :length] = grad_scores.astype(jnp.float32)
            else:
                total[:, :length] = total[:, :length] + grad_scores.astype(jnp.float32)
            new = (
                lax.dot_general(grad_scores, key_rows, TN, preferred_element_type=jnp.float32) * 0.125,
                jnp.dot(grad_scores, queries, preferred_element_type=jnp.float32),
                jnp.dot(probs, outer, preferred_element_type=jnp.float32),
            )
            for kind in range(3):
                column = pl.multiple_of(step * 128 + kind * width, 128)
                if head == 0:
                    out_ref[here, pl.ds(column, 128)] = (new[kind] * chosen).astype(jnp.bfloat16)
                else:
                    out_ref[here, pl.ds(column, 128)] = out_ref[here, pl.ds(column, 128)] + (
                        new[kind] * chosen
                    ).astype(jnp.bfloat16)
        strip = total[:rows, :] if blocks == 1 else pltpu.roll(total[:rows, :], (blocks - 1) * rows, 1)
        for block in range(1, blocks):
            offset = (blocks - 1 - block) * rows
            piece = total[block * rows : (block + 1) * rows, :]
            strip = strip + (piece if offset == 0 else pltpu.roll(piece, offset, 1))
        if strip_ref.shape[1] == rows:
            strip_ref[head] = strip
            continue
        lane = lax.broadcasted_iota(jnp.int32, (1, 128), 1)
        for offset in range(strip_ref.shape[2] // 128):
            odd = offset % 2
            there = slice(offset // 2 * 128, offset // 2 * 128 + 128)
            summed = None
            for row in range(HS):
                piece = jnp.where(lane // 64 == odd, strip[row * HS : (row + 1) * HS, there], 0.0)
                shift = (64 * odd + (HS - 1 - row) * HS) % 128
                piece = piece if shift == 0 else pltpu.roll(piece, shift, 1)
                summed = piece if summed is None else summed + piece
            strip_ref[head, :, offset * 128 : (offset + 1) * 128] = summed


def attend_back(qkv, probs, grad_out, wins, length, rows, lanes, strip):
    count, triple = qkv.shape
    return pl.pallas_call(
        partial(attend_back_kernel, wins=wins, length=length, rows=rows),
        grid=(HEADS // 2,),
        out_shape=[
            jax.ShapeDtypeStruct((count, triple), jnp.bfloat16),
            jax.ShapeDtypeStruct((HEADS,) + strip, jnp.float32),
        ],
        in_specs=[
            pl.BlockSpec((count, 128), lambda h: (0, h)),
            pl.BlockSpec((count, 128), lambda h: (0, HEADS // 2 + h)),
            pl.BlockSpec((count, 128), lambda h: (0, HEADS + h)),
            pl.BlockSpec((count, 128), lambda h: (0, h)),
            pl.BlockSpec((2, wins, length, length), lambda h: (h, 0, 0, 0)),
        ],
        out_specs=[
            pl.BlockSpec((count, triple), lambda h: (0, 0)),
            pl.BlockSpec((2,) + strip, lambda h: (h, 0, 0)),
        ],
        scratch_shapes=[pltpu.VMEM((length, lanes), jnp.float32)],
        compiler_params=pltpu.CompilerParams(vmem_limit_bytes=VMEM_BYTES),
        cost_estimate=SMALL,
        name="attend_back",
    )(qkv, qkv, qkv, grad_out, probs)


def plain_norm(values):
    center = values - jnp.mean(values, axis=-1, keepdims=True)
    spread = jnp.mean(center * center, axis=-1, keepdims=True)
    scale = lax.rsqrt(spread + epsilon)
    return center * scale, scale


def modulated_norm(values, shift_vec, scale_vec):
    return (plain_norm(values)[0] * (1.0 + scale_vec) + shift_vec).astype(jnp.bfloat16)


def norm_back(grad_in, values, scale_vec):
    unit, scale = plain_norm(values)
    inner = grad_in * (1.0 + scale_vec)
    mean_one = jnp.mean(inner, axis=-1, keepdims=True)
    mean_two = jnp.mean(inner * unit, axis=-1, keepdims=True)
    grad = scale * (inner - mean_one - unit * mean_two)
    return grad, jnp.sum(grad_in, axis=0), jnp.sum(grad_in * unit, axis=0)


def gelu_both(upward):
    half = 0.5 * (1.0 + lax.erf(upward * 0.7071067811865476))
    density = 0.3989422804014327 * jnp.exp(-0.5 * upward * upward)
    return (upward * half).astype(jnp.bfloat16), (half + upward * density).astype(jnp.bfloat16)


def joint_group(rows):
    split = rows.reshape(FR * HS, 2, HS, rows.shape[-1])
    return split.transpose(1, 0, 2, 3).reshape(rows.shape)


def joint_ungroup(rows):
    split = rows.reshape(2, FR * HS, HS, rows.shape[-1])
    return split.transpose(1, 0, 2, 3).reshape(rows.shape)


def window_group(flat_rows):
    return flat_rows.reshape(SLOTS, WS * WS, flat_rows.shape[-1])


def split_halves(half_rows, own_half):
    pair_windows = half_rows.shape[0]
    filler = jnp.zeros((2 * SLOTS - pair_windows,) + half_rows.shape[1:], half_rows.dtype)
    padded = jnp.concatenate([half_rows, filler], axis=0)
    keep_part = lax.dynamic_slice_in_dim(padded, own_half * SLOTS, SLOTS, 0)
    send_part = lax.dynamic_slice_in_dim(padded, (1 - own_half) * SLOTS, SLOTS, 0)
    return (keep_part, send_part)


def join_windows(keep_part, came_part, own_half):
    upper_half = jnp.where(own_half == 0, keep_part, came_part)
    lower_half = jnp.where(own_half == 0, came_part, keep_part)
    joined = jnp.concatenate([upper_half, lower_half], axis=1)
    return joined.reshape(-1, joined.shape[-1])


def split_windows(win_rows, own_half):
    grouped = window_group(win_rows)
    half_len = grouped.shape[1] // 2
    upper_half = grouped[:, :half_len]
    lower_half = grouped[:, half_len:]
    keep_part = jnp.where(own_half == 0, upper_half, lower_half)
    send_part = jnp.where(own_half == 0, lower_half, upper_half)
    return (keep_part, send_part)


def join_halves(keep_part, came_part, own_half, pair_windows):
    leading = jnp.where(own_half == 0, keep_part, came_part)
    trailing = jnp.where(own_half == 0, came_part, keep_part)
    joined = jnp.concatenate([leading, trailing], axis=0)[:pair_windows]
    return joined.reshape(-1, joined.shape[-1])


def from_pair(value):
    pairs = [(i, i ^ 1) for i in range(lax.axis_size("win"))]
    return lax.ppermute(value, "win", pairs)


def leave_windows(win_rows, own_half, pair_windows):
    keep_part, send_part = split_windows(win_rows, own_half)
    came_part = from_pair(send_part.astype(jnp.bfloat16)).astype(send_part.dtype)
    return join_halves(keep_part, came_part, own_half, pair_windows)


def enter_windows(flat_rows, own_half, pair_windows):
    half_rows = flat_rows.reshape(pair_windows, -1, flat_rows.shape[-1])
    keep_part, send_part = split_halves(half_rows, own_half)
    came_part = from_pair(send_part.astype(jnp.bfloat16)).astype(send_part.dtype)
    return join_windows(keep_part, came_part, own_half)


class Weights:
    def __init__(self, masters, place, quick):
        self.quick = quick
        low = [master.astype(jnp.bfloat16) for master in masters]
        self.place = place
        if quick:
            shards = []
            for block in range(2):
                qkv, out, up, down = low[4 * block : 4 * block + 4]
                shards += [jnp.concatenate([qkv, out], axis=1), up, down]
            self.widths = [(384, 128), (512,), (128,)] * 2
            self.jobs = [Gather(shard) for shard in shards]
        else:
            self.full = [
                lax.all_gather(lax.all_gather(shard, "win", axis=1, tiled=True), "clip", axis=0, tiled=True)
                for shard in low
            ]
            self.full = [tuple(self.full[0:2]), (self.full[2],), (self.full[3],)] + [
                tuple(self.full[4:6]),
                (self.full[6],),
                (self.full[7],),
            ]

    def go(self, moves, state, after=()):
        if not self.quick:
            return state
        jobs = [(self.jobs[unit], move) for unit, move in moves]
        known = [(job, job.needs(move)) for job, move in jobs if job.needs(move) in job.held]
        known += [(self.jobs[unit], name) for unit, name in after]
        held, state = lax.optimization_barrier(([job.held[name] for job, name in known], state))
        for (job, name), values in zip(known, held):
            job.held[name] = values
        for job, move in jobs:
            job.go(move)
        return state

    def apply(self, unit, x, kind):
        if self.quick:
            job = self.jobs[unit]
            return gathered(job.values(), self.place, x, job.rows, self.widths[unit], kind)
        wholes = self.full[unit]
        result = jnp.dot(x, wholes[0], preferred_element_type=jnp.float32)
        if kind == "gelu":
            return *gelu_both(result), *wholes
        return result if kind == "wide" else result.astype(jnp.bfloat16), *wholes


def body(
    tokens,
    grad_output,
    clip_height,
    clip_width,
    modulation,
    sp_qkv,
    sp_out,
    sp_up,
    sp_down,
    sp_table,
    st_qkv,
    st_out,
    st_up,
    st_down,
    st_table,
    quick,
):
    model_width = tokens.shape[-1]
    half_len = tokens.shape[-2]
    pair_windows = PAIR_LOCS * FR
    shard_index = lax.axis_index("win")
    clip_index = lax.axis_index("clip")
    pair_index = shard_index // 2
    own_half = shard_index % 2
    own_core = clip_index % 2
    own_x = clip_index // 2
    row_places = [
        (own_x ^ x_rel) * 2 + (own_core ^ c_rel) for c_rel in range(2) for x_rel in range(2)
    ]
    place = {
        "rows": jnp.stack(row_places).astype(jnp.int32),
        "cols": jnp.stack([own_half, own_half ^ 1]).astype(jnp.int32),
    }
    weights = Weights(
        (sp_qkv, sp_out, sp_up, sp_down, st_qkv, st_out, st_up, st_down), place, quick
    )
    mod = modulation[0]

    location = pair_index
    token_ids = jnp.arange(WS * WS, dtype=jnp.int32)
    row_pos = location // LOC_W * WS + token_ids // WS
    col_pos = location % LOC_W * WS + token_ids % WS
    sp_valid = (row_pos < clip_height[0]) & (col_pos < clip_width[0])
    sp_allowed = (sp_valid[None, :, None] | jnp.eye(WS * WS, dtype=bool)[None]).astype(jnp.float32)
    joint_len = FR * HS * HS
    joint_ids = jnp.arange(joint_len, dtype=jnp.int32)
    joint_row = location // LOC_W * WS + own_half * HS + joint_ids // HS % HS
    joint_col = location % LOC_W * WS + jnp.arange(2, dtype=jnp.int32)[:, None] * HS + joint_ids[None] % HS
    st_valid = (joint_row[None] < clip_height[0]) & (joint_col < clip_width[0])
    st_allowed = (st_valid[:, :, None] | jnp.eye(joint_len, dtype=bool)[None]).astype(jnp.float32)

    half_tokens = tokens.reshape(pair_windows, half_len, model_width)
    win_input = enter_windows(half_tokens, own_half, pair_windows).astype(jnp.float32)
    attn_in_a = modulated_norm(win_input, mod[0], mod[1])

    go = weights.go
    state = go([(0, "near")], (win_input, attn_in_a, sp_table))
    win_input, attn_in_a, sp_table = go([(0, "far"), (0, "core_near")], state)
    sp_strip = spatial_strip(sp_table)
    state = go([(1, "near")], (win_input, attn_in_a, sp_strip, sp_allowed))
    win_input, attn_in_a, sp_strip, sp_allowed = go([(0, "core_far")], state)
    qkv_a, w_qkv_a, w_out_a = weights.apply(0, attn_in_a, "narrow")
    win_input, qkv_a, w_out_a = go([(1, "far")], (win_input, qkv_a, w_out_a))
    win_input, qkv_a, w_out_a = go([(2, "near")], (win_input, qkv_a, w_out_a))
    attn_out_a, probs_a = attend(qkv_a, sp_strip, sp_allowed, SLOTS, WS * WS)
    win_input, attn_out_a, w_out_a = go([(1, "core_near")], (win_input, attn_out_a, w_out_a))
    mixed_a = product(attn_out_a, w_out_a)
    win_middle = win_input + mod[2] * mixed_a
    keep_part, send_part = split_windows(win_middle, own_half)
    send_part = send_part.astype(jnp.bfloat16)
    keep_part, send_part, st_table = go([(1, "core_far")], (keep_part, send_part, st_table))
    came_part = from_pair(send_part)
    keep_part, st_table = go([(2, "far")], (keep_part, st_table))
    st_strip = joint_strip(st_table)
    keep_part, came_part, st_strip, st_allowed = lax.optimization_barrier(
        (keep_part, came_part, st_strip, st_allowed)
    )
    middle_a = joint_group(join_halves(keep_part, came_part.astype(jnp.float32), own_half, pair_windows))
    mlp_in_a = modulated_norm(middle_a, mod[3], mod[4])

    middle_a, mlp_in_a = go([(3, "near")], (middle_a, mlp_in_a))
    hidden_a, slope_a, w_up_a = weights.apply(1, mlp_in_a, "gelu")
    middle_a, hidden_a, slope_a = go([(2, "core_near"), (2, "core_far")], (middle_a, hidden_a, slope_a))
    middle_a, hidden_a, slope_a = go([(4, "near")], (middle_a, hidden_a, slope_a))
    downward_a, w_down_a = weights.apply(2, hidden_a, "wide")
    middle_a, downward_a = go([(3, "far")], (middle_a, downward_a))
    middle_a, downward_a = go([(3, "core_near")], (middle_a, downward_a))
    first_out = middle_a + mod[5] * downward_a
    attn_in_b = modulated_norm(first_out, mod[6], mod[7])

    first_out, attn_in_b = go([(3, "core_far")], (first_out, attn_in_b))
    first_out, attn_in_b = go([(4, "far")], (first_out, attn_in_b))
    qkv_b, w_qkv_b, w_out_b = weights.apply(3, attn_in_b, "narrow")
    first_out, qkv_b, w_out_b = go([(5, "near"), (4, "core_near")], (first_out, qkv_b, w_out_b))
    attn_out_b, probs_b = attend(qkv_b, st_strip, st_allowed, 2, joint_len)
    first_out, attn_out_b, w_out_b = go([(4, "core_far")], (first_out, attn_out_b, w_out_b))
    first_out, attn_out_b, w_out_b = go([(5, "far")], (first_out, attn_out_b, w_out_b))
    mixed_b = product(attn_out_b, w_out_b)
    middle_b = first_out + mod[8] * mixed_b
    mlp_in_b = modulated_norm(middle_b, mod[9], mod[10])
    hidden_b, slope_b, w_up_b = weights.apply(4, mlp_in_b, "gelu")
    middle_b, hidden_b, slope_b = go([(5, "core_near"), (5, "core_far")], (middle_b, hidden_b, slope_b))

    def start_grad(xs, dys, rows, widths, starts, sources, olders=()):
        if quick:
            return Scatter(xs, dys, place, rows, widths, starts, sources, olders)
        return Plain(xs, dys, widths, starts, sources)

    def rounds(jobs, state):
        if quick:
            return together(jobs, state)
        return state

    def hold(jobs, state):
        if not quick:
            return state
        state, held = lax.optimization_barrier((state, [job.values for job in jobs]))
        for job, values in zip(jobs, held):
            job.values = values
        return state

    def settle(jobs, state):
        state = hold(jobs, state)
        if quick:
            for job in jobs:
                job.fold()
        return state

    grad_out_b = joint_group(grad_output.reshape(-1, model_width)).astype(jnp.float32)
    grad_down_b = (mod[11] * grad_out_b).astype(jnp.bfloat16)
    d_st_down = start_grad([hidden_b], [grad_down_b], 1024, (128,), (0,), (0,))
    grad_down_b, hidden_b = rounds([d_st_down], (grad_down_b, hidden_b))
    downward_b, w_down_b = weights.apply(5, hidden_b, "wide")
    grad_up_b = product_scaled(grad_down_b, w_down_b, slope_b)
    d_st_up = start_grad([mlp_in_b], [grad_up_b], 256, (512,), (0,), (0,), [d_st_down])
    grad_up_b, downward_b = rounds([d_st_up, d_st_down], (grad_up_b, downward_b))
    out_rows = middle_b + mod[11] * downward_b
    out_tokens = joint_ungroup(out_rows).reshape(tokens.shape)
    grad_gate_mb = jnp.sum(grad_out_b * downward_b, axis=0)
    grad_mlp_b = product_turned(grad_up_b, w_up_b)
    norm_grad, grad_shift_mb, grad_scale_mb = norm_back(grad_mlp_b, middle_b, mod[10])
    grad_middle_b = grad_out_b + norm_grad
    grad_mixed_b = (mod[8] * grad_middle_b).astype(jnp.bfloat16)
    grad_gate_ab = jnp.sum(grad_middle_b * mixed_b, axis=0)
    state = (grad_middle_b, grad_mixed_b)
    state = settle([d_st_up, d_st_down], state)
    grad_middle_b, grad_mixed_b = rounds([d_st_up, d_st_down], state)
    grad_attn_b = product_turned(grad_mixed_b, w_out_b, jnp.bfloat16)
    grad_qkv_b, strip_grad_b = attend_back(
        qkv_b, probs_b, grad_attn_b, 2, joint_len, *st_strip.shape[1:], (HS, 128 * (2 * FR - 1))
    )
    grad_middle_b, grad_qkv_b, strip_grad_b = hold(
        [d_st_down], (grad_middle_b, grad_qkv_b, strip_grad_b)
    )
    d_st_attn = start_grad(
        [attn_in_b, attn_out_b],
        [grad_qkv_b, grad_qkv_b, grad_mixed_b],
        256,
        (256, 128, 128),
        (0, 8, 0),
        (0, 0, 1),
        [d_st_down],
    )
    state = hold([d_st_attn], (grad_middle_b, grad_qkv_b, strip_grad_b))
    state = settle([d_st_up], state)
    grad_middle_b, grad_qkv_b, strip_grad_b = rounds([d_st_attn, d_st_up, d_st_down], state)
    grad_in_b = product_turned(grad_qkv_b, w_qkv_b)
    norm_grad, grad_shift_ab, grad_scale_ab = norm_back(grad_in_b, first_out, mod[7])
    grad_first = grad_middle_b + norm_grad
    grad_down_a = (mod[5] * grad_first).astype(jnp.bfloat16)
    grad_gate_ma = jnp.sum(grad_first * downward_a, axis=0)
    grad_first, grad_down_a = hold([d_st_attn, d_st_up], (grad_first, grad_down_a))
    d_sp_down = start_grad(
        [hidden_a], [grad_down_a], 1024, (128,), (0,), (0,), [d_st_attn, d_st_up]
    )
    grad_first, grad_down_a = rounds([d_sp_down, d_st_attn, d_st_up], (grad_first, grad_down_a))
    grad_up_a = product_scaled(grad_down_a, w_down_a, slope_a)
    grad_first, grad_up_a = hold([d_sp_down], (grad_first, grad_up_a))
    d_sp_up = start_grad([mlp_in_a], [grad_up_a], 256, (512,), (0,), (0,), [d_sp_down])
    grad_first, grad_up_a = hold([d_sp_up], (grad_first, grad_up_a))
    grad_first, grad_up_a = settle([d_st_attn], (grad_first, grad_up_a))
    grad_first, grad_up_a = rounds([d_sp_up, d_st_attn], (grad_first, grad_up_a))
    grad_mlp_a = product_turned(grad_up_a, w_up_a)
    norm_grad, grad_shift_ma, grad_scale_ma = norm_back(grad_mlp_a, middle_a, mod[4])
    grad_middle_a = joint_ungroup(grad_first + norm_grad)
    half_rows = grad_middle_a.reshape(pair_windows, -1, model_width)
    keep_part, send_part = split_halves(half_rows, own_half)
    send_part = send_part.astype(jnp.bfloat16)
    keep_part, send_part, strip_grad_b = hold(
        [d_sp_up, d_st_attn], (keep_part, send_part, strip_grad_b)
    )
    came_part = from_pair(send_part)
    strip_grad_b = rounds([d_sp_down], strip_grad_b)
    if quick:
        d_st_attn.fold()
        d_sp_up.fold()
    rounds([d_st_attn], ())
    st_sum = joint_strip_back(strip_grad_b)
    keep_part, came_part, st_sum = lax.optimization_barrier((keep_part, came_part, st_sum))
    grad_win = join_windows(keep_part, came_part.astype(jnp.float32), own_half)
    grad_mixed_a = (mod[2] * grad_win).astype(jnp.bfloat16)
    grad_gate_aa = jnp.sum(grad_win * mixed_a, axis=0)
    grad_win, grad_mixed_a = rounds([d_sp_up], (grad_win, grad_mixed_a))
    grad_attn_a = product_turned(grad_mixed_a, w_out_a, jnp.bfloat16)
    grad_qkv_a, strip_grad_a = attend_back(
        qkv_a, probs_a, grad_attn_a, SLOTS, WS * WS, *sp_strip.shape[1:], sp_strip.shape[1:]
    )
    grad_win, grad_qkv_a, strip_grad_a = settle([d_sp_down], (grad_win, grad_qkv_a, strip_grad_a))
    grad_win, grad_qkv_a, strip_grad_a = rounds([d_sp_down], (grad_win, grad_qkv_a, strip_grad_a))
    d_sp_attn = start_grad(
        [attn_in_a, attn_out_a], [grad_qkv_a, grad_mixed_a], 256, (384, 128), (0, 0), (0, 1)
    )
    state = hold([d_sp_attn, d_sp_up, d_sp_down], (grad_win, grad_qkv_a, strip_grad_a, st_sum))
    if quick:
        d_sp_up.fold()
        d_sp_down.fold()
    grad_win, grad_qkv_a, strip_grad_a, st_sum = rounds([d_sp_attn, d_sp_up, d_sp_down], state)
    grad_in_a = product_turned(grad_qkv_a, w_qkv_a)
    state = (grad_win, grad_in_a, strip_grad_a, st_sum)
    state = settle([d_sp_attn, d_sp_up], state)
    grad_win, grad_in_a, strip_grad_a, st_sum = rounds([d_sp_attn, d_sp_up], state)
    norm_grad, grad_shift_aa, grad_scale_aa = norm_back(grad_in_a, win_input, mod[1])
    mod_rows = [
        grad_shift_aa,
        grad_scale_aa,
        grad_gate_aa,
        grad_shift_ma,
        grad_scale_ma,
        grad_gate_ma,
        grad_shift_ab,
        grad_scale_ab,
        grad_gate_ab,
        grad_shift_mb,
        grad_scale_mb,
        grad_gate_mb,
    ]
    win_sum = grad_win + norm_grad
    keep_part, send_part = split_windows(win_sum, own_half)
    send_part = send_part.astype(jnp.bfloat16)
    sp_sum = spatial_strip_back(strip_grad_a)
    tables = jnp.concatenate([sp_sum.reshape(-1), st_sum.reshape(-1)])
    table_total = Total(tables, ("core", "z1", "z0", "y", "x"))
    mod_total = Total(jnp.stack(mod_rows, axis=0), ("z1", "z0", "y"))
    keep_part, send_part = settle([d_sp_attn], (keep_part, send_part))
    keep_part, send_part = rounds([d_sp_attn, table_total, mod_total], (keep_part, send_part))
    keep_part, send_part = settle([d_sp_attn], (keep_part, send_part))
    keep_part, send_part = rounds([d_sp_attn, table_total, mod_total], (keep_part, send_part))
    came_part = from_pair(send_part)
    rounds([table_total, mod_total], ())
    rounds([table_total], ())
    rounds([table_total], ())
    came_part = came_part.astype(jnp.float32)
    grad_tokens = join_halves(keep_part, came_part, own_half, pair_windows).reshape(tokens.shape)
    if quick:
        grad_modulation = mod_total.result()[None]
        table_sums = table_total.result()
    else:
        grad_modulation = lax.psum(jnp.stack(mod_rows, axis=0), "win")[None]
        table_sums = lax.psum(table_total.result(), ("clip", "win"))
    grad_sp_table = table_sums[: sp_table.size].reshape(sp_table.shape)
    grad_st_table = table_sums[sp_table.size :].reshape(st_table.shape)
    wide = d_st_attn.values
    wide_a = d_sp_attn.values
    out_width = wide.shape[1] // 4
    return (
        out_tokens,
        grad_tokens,
        grad_modulation,
        wide_a[:, : 3 * out_width],
        wide_a[:, 3 * out_width :],
        d_sp_up.values,
        d_sp_down.values,
        grad_sp_table,
        wide[:, : 2 * out_width],
        wide[:, 2 * out_width : 3 * out_width],
        wide[:, 3 * out_width :],
        d_st_up.values,
        d_st_down.values,
        grad_st_table,
    )


class Plain:
    def __init__(self, xs, dys, widths, starts, sources):
        grads = []
        for dy, width, start, source in zip(dys, widths, starts, sources):
            x = xs[source]
            part = dy[:, start * 2 * width : start * 2 * width + 8 * width]
            full = lax.dot_general(x, part, TN, preferred_element_type=jnp.float32)
            full = lax.psum_scatter(
                full.astype(jnp.bfloat16), "clip", scatter_dimension=0, tiled=True
            )
            grads.append(lax.psum_scatter(full, "win", scatter_dimension=1, tiled=True))
        self.values = jnp.concatenate(grads, axis=1).astype(jnp.float32)


def solution(mesh):
    grid = P("clip", "win")
    whole = P("clip", "win", None, None, None, None)
    in_specs = (whole, whole, P("clip"), P("clip"), P("clip", None, None)) + ((grid,) * 4 + (P(),)) * 2
    out_specs = (whole, whole, P("clip", None, None)) + (grid,) * 4 + (P(),) + (grid,) * 5 + (P(),)
    quick = mesh.shape["clip"] == 4 and mesh.shape["win"] == 8
    return jax.shard_map(
        partial(body, quick=quick), mesh=mesh, in_specs=in_specs, out_specs=out_specs, check_vma=False
    )
```

```python
from functools import partial
from typing import NamedTuple

import jax
import jax.numpy as jnp
import numpy as np
from jax import lax
from jax.experimental import pallas as pl
from jax.experimental.pallas import tpu as pltpu
from jax.sharding import PartitionSpec as P

HEADS = 16
WS = 16
FR = 5
LOC_W = 4
PAIR_LOCS = 1
HS = 8
SLOTS = 3
VMEM_BYTES = 56 * 1024 * 1024

SMALL = pl.CostEstimate(flops=1, bytes_accessed=1, transcendentals=0)

epsilon = 1e-06
masked_score = -1000000000.0
highest = lax.Precision.HIGHEST
NT = (((1,), (1,)), ((), ()))
TN = (((0,), (0,)), ((), ()))


BITS = {"core": ("clip", 1), "x": ("clip", 2), "y": ("win", 1), "z0": ("win", 2), "z1": ("win", 4)}


def hop(value, link):
    axis, mask = BITS[link]
    return lax.ppermute(value, axis, [(i, i ^ mask) for i in range(lax.axis_size(axis))])


def z_groups():
    size = lax.axis_size("win")
    return [list(range(start, size, 2)) for start in range(2)]


class Gather:
    def __init__(self, halves, rows, early):
        self.rows = rows
        self.early = early
        axis = halves.ndim - 2
        grown = lax.all_gather(halves, "win", axis=axis, tiled=False, axis_index_groups=z_groups())
        self.held = {"grown": (grown,)}

    def needs(self, move):
        if move == "far" and self.early:
            return "grown"
        return {"near": "grown", "far": "near", "core_near": "own", "core_far": "away"}[move]

    def go(self, move):
        values = self.held[self.needs(move)]
        if move == "near":
            (grown,) = values
            a0, b0 = grown[0], grown[1]
            self.held["near"] = (a0, hop(a0, "y"), b0, hop(b0, "x"))
        elif move == "far":
            if self.early:
                a1, b1 = values[0][0], values[0][1]
            else:
                a0, a_came, b0, b_came = values
                a1, b1 = jnp.stack([a0, a_came]), jnp.stack([b0, b_came])
            self.held["own"] = (a1, b1)
            self.held["away"] = (hop(a1, "x"), hop(b1, "y"))
        else:
            self.held[move] = tuple(hop(value, "core") for value in values)

    def values(self):
        pairs = [self.held[name] for name in ("own", "away", "core_near", "core_far")]
        return [pair[0] for pair in pairs] + [pair[1] for pair in pairs]


def gathered_kernel(row_of, y_of, x_ref, *refs, rows, widths, kind):
    count = len(widths)
    results = 2 if kind == "gelu" else 1
    pieces, refs = refs[:8], refs[8:]
    outs, wholes, held = refs[:results], refs[results : results + count], refs[results + count : -2]
    in_sems, out_sems = refs[-2:]
    half = rows // 2
    step = pl.program_id(0)

    def arrivals(z):
        copies = []
        for part in range(2):
            for c_rel in range(2):
                for x_rel in range(2):
                    row = row_of[c_rel * 2 + x_rel] * rows + part * half
                    row = pl.multiple_of(row, half)
                    for y_rel in range(2):
                        far, near = (x_rel, y_rel) if part == 0 else (y_rel, x_rel)
                        source = pieces[part * 4 + c_rel * 2 + far]
                        start = 0
                        for matrix, width in zip(held, widths):
                            col = pl.multiple_of((z * 2 + y_of[y_rel]) * width, 128)
                            copies.append(
                                pltpu.make_async_copy(
                                    source.at[near, z, :, pl.ds(start, width)],
                                    matrix.at[pl.ds(row, half), pl.ds(col, width)],
                                    in_sems.at[z * 16 * count + len(copies)],
                                )
                            )
                            start += width
        return copies

    def departures(z):
        copies = []
        for which, width in enumerate(widths):
            there = pl.ds(pl.multiple_of(z * 2 * width, 128), 2 * width)
            copies.append(
                pltpu.make_async_copy(
                    held[which].at[:, there], wholes[which].at[:, there], out_sems.at[z * count + which]
                )
            )
        return copies

    @pl.when(step == 0)
    def begin():
        for z in range(4):
            for copy in arrivals(z):
                copy.start()

    for copy in arrivals(step):
        copy.wait()
    for copy in departures(step):
        copy.start()
    wide = 2 * widths[0]
    chunk = 256 if kind == "gelu" else wide
    for first in range(0, wide, chunk):
        col = pl.multiple_of(step * wide + first, 128)
        there = slice(first, first + chunk)
        result = jnp.dot(
            x_ref[...], held[0][:, pl.ds(col, chunk)], preferred_element_type=jnp.float32
        )
        if kind == "gelu":
            outs[0][:, there], outs[1][:, there] = gelu_both(result)
        else:
            outs[0][:, there] = result.astype(outs[0].dtype)

    @pl.when(step == 3)
    def end():
        for z in range(4):
            for copy in departures(z):
                copy.wait()


def gathered(values, place, x, rows, widths, kind):
    shapes = [(4 * rows, 8 * width) for width in widths]
    results = 2 if kind == "gelu" else 1
    kept = jnp.float32 if kind == "wide" else jnp.bfloat16
    count = x.shape[0]
    return pl.pallas_call(
        partial(gathered_kernel, rows=rows, widths=widths, kind=kind),
        grid=(4,),
        out_shape=[jax.ShapeDtypeStruct((count, 8 * widths[0]), kept)] * results
        + [jax.ShapeDtypeStruct(shape, jnp.bfloat16) for shape in shapes],
        in_specs=[pl.BlockSpec(memory_space=pltpu.SMEM)] * 2
        + [pl.BlockSpec(x.shape, lambda z: (0, 0))]
        + [pl.BlockSpec(memory_space=pl.ANY)] * 8,
        out_specs=[pl.BlockSpec((count, 2 * widths[0]), lambda z: (0, z))] * results
        + [pl.BlockSpec(memory_space=pl.ANY)] * len(widths),
        scratch_shapes=[pltpu.VMEM(shape, jnp.bfloat16) for shape in shapes]
        + [pltpu.SemaphoreType.DMA((64 * len(widths),)), pltpu.SemaphoreType.DMA((4 * len(widths),))],
        compiler_params=pltpu.CompilerParams(vmem_limit_bytes=VMEM_BYTES),
        cost_estimate=SMALL,
        name="gathered",
    )(place["rows"], place["cols"], x, *values)


def product_kernel(left, right, out, *, turned):
    if turned:
        result = lax.dot_general(left[...], right[...], NT, preferred_element_type=jnp.float32)
    else:
        result = jnp.dot(left[...], right[...], preferred_element_type=jnp.float32)
    out[...] = result.astype(out.dtype)


def scaled_kernel(left, right, factor, out):
    result = lax.dot_general(left[...], right[...], NT, preferred_element_type=jnp.float32)
    out[...] = (result * factor[...].astype(jnp.float32)).astype(out.dtype)


def tiled(kernel, left, right, columns, kept, turned, *factors):
    count = left.shape[0]
    total = right.shape[0] if turned else right.shape[1]
    block = pl.BlockSpec((count, columns), lambda i: (0, i))
    if turned:
        right_spec = pl.BlockSpec((columns, right.shape[1]), lambda i: (i, 0))
    else:
        right_spec = pl.BlockSpec((right.shape[0], columns), lambda i: (0, i))
    return pl.pallas_call(
        kernel,
        grid=(total // columns,),
        out_shape=jax.ShapeDtypeStruct((count, total), kept),
        in_specs=[pl.BlockSpec(left.shape, lambda i: (0, 0)), right_spec] + [block] * len(factors),
        out_specs=block,
        compiler_params=pltpu.CompilerParams(vmem_limit_bytes=VMEM_BYTES),
        cost_estimate=SMALL,
        name="product",
    )(left, right, *factors)


def product(left, right):
    return tiled(partial(product_kernel, turned=False), left, right, 512, jnp.float32, False)


def product_turned(left, right, kept=jnp.float32):
    columns = 512 if right.shape[1] == 1024 else 256
    return tiled(partial(product_kernel, turned=True), left, right, columns, kept, True)


def product_scaled(left, right, factor):
    return tiled(scaled_kernel, left, right, 1024, jnp.bfloat16, True, factor)


def grad_kernel(row_of, y_of, *refs, rows, widths, sources, kinds):
    count = len(widths)
    lefts = max(sources) + 1
    refs = list(refs)
    x_refs = [refs.pop(0) for _ in range(lefts)]
    dy_refs = [refs.pop(0) for _ in range(count)]
    old_refs = [[refs.pop(0) for _ in range(FOLDS[kind].takes)] for kind in kinds]
    send, keep = refs.pop(0), refs.pop(0)
    new_refs = [[refs.pop(0) for _ in range(FOLDS[kind].gives)] for kind in kinds]
    turns = refs
    half = rows // 2

    @pl.when(pl.program_id(0) == 0)
    def turn():
        for x_ref, turned in zip(x_refs, turns):
            for place in range(4):
                start = pl.multiple_of(row_of[place] * rows, 128)
                turned[place * rows : (place + 1) * rows, :] = x_ref[:, pl.ds(start, rows)].T

    offset = 0
    for dy_ref, width, source in zip(dy_refs, widths, sources):
        turned = turns[source]
        sides = [
            dy_ref[:, pl.ds(pl.multiple_of(y_of[y_rel] * width, 128), width)] for y_rel in range(2)
        ]
        product = jnp.dot(
            turned[...], jnp.concatenate(sides, axis=1), preferred_element_type=jnp.float32
        ).astype(jnp.bfloat16)
        for c_rel, out in ((0, keep), (1, send)):
            for x_rel in range(2):
                for ab in range(2):
                    first = (c_rel * 2 + x_rel) * rows + ab * half
                    for y_rel in range(2):
                        out[ab, x_rel, y_rel, 0, :, offset : offset + width] = product[
                            first : first + half, y_rel * width : (y_rel + 1) * width
                        ]
        offset += width
    for kind, old, new in zip(kinds, old_refs, new_refs):
        FOLDS[kind].kernel(*old, *new)


def fold_first(old_keep, old_came, a_send, a_keep, b_send, b_keep):
    for near in range(2):
        a_send[near] = old_keep[0, 1, near] + old_came[0, 1, near]
        a_keep[near] = old_keep[0, 0, near] + old_came[0, 0, near]
        b_send[near] = old_keep[1, near, 1] + old_came[1, near, 1]
        b_keep[near] = old_keep[1, near, 0] + old_came[1, near, 0]


def fold_second(a_keep, a_came, b_keep, b_came, a_out, a_held, b_out, b_held):
    a_out[...] = a_keep[1] + a_came[1]
    a_held[...] = a_keep[0] + a_came[0]
    b_out[...] = b_keep[1] + b_came[1]
    b_held[...] = b_keep[0] + b_came[0]


def fold_third(a_keep, a_came, b_keep, b_came, both):
    both[:, 0] = a_keep[...] + a_came[...]
    both[:, 1] = b_keep[...] + b_came[...]


class Part(NamedTuple):
    lead: tuple

    def shape(self, tail):
        return jax.ShapeDtypeStruct(self.lead + tail, jnp.bfloat16)

    def spec(self, tail):
        where = self.lead.index(4)
        block = tuple(1 if dim == where else size for dim, size in enumerate(self.lead))
        return pl.BlockSpec(
            block + tail, lambda z: (0,) * where + (z,) + (0,) * (len(block) + 1 - where)
        )


WHOLE, QUARTER, EIGHTH, TURNED = Part((2, 2, 2, 4)), Part((2, 4)), Part((4,)), Part((4, 2))


class Fold(NamedTuple):
    kernel: object
    takes: int
    takes_part: Part
    gives: int
    gives_part: Part


FOLDS = {
    1: Fold(fold_first, 2, WHOLE, 4, QUARTER),
    2: Fold(fold_second, 4, QUARTER, 4, EIGHTH),
    3: Fold(fold_third, 4, EIGHTH, 1, TURNED),
}


def weight_grad(xs, dys, place, rows, widths, starts, sources, olders):
    count = xs[0].shape[0]
    tail = (rows // 2, sum(widths))
    kinds = tuple(older.stage for older in olders)
    out_shape, out_specs = [WHOLE.shape(tail)] * 2, [WHOLE.spec(tail)] * 2
    old_specs, old_values = [], []
    for older, kind in zip(olders, kinds):
        fold = FOLDS[kind]
        old_tail = older.values[0].shape[-2:]
        old_specs += [fold.takes_part.spec(old_tail)] * fold.takes
        old_values += older.values
        out_shape += [fold.gives_part.shape(old_tail)] * fold.gives
        out_specs += [fold.gives_part.spec(old_tail)] * fold.gives
    outs = pl.pallas_call(
        partial(grad_kernel, rows=rows, widths=widths, sources=sources, kinds=kinds),
        grid=(4,),
        out_shape=out_shape,
        in_specs=[pl.BlockSpec(memory_space=pltpu.SMEM)] * 2
        + [pl.BlockSpec((count, 4 * rows), lambda z: (0, 0))] * len(xs)
        + [
            pl.BlockSpec((count, 2 * width), lambda z, s=start: (0, s + z))
            for width, start in zip(widths, starts)
        ]
        + old_specs,
        out_specs=out_specs,
        scratch_shapes=[pltpu.VMEM((4 * rows, count), jnp.bfloat16)] * len(xs),
        compiler_params=pltpu.CompilerParams(vmem_limit_bytes=VMEM_BYTES),
        cost_estimate=SMALL,
        name="weight_grad",
    )(place["rows"], place["cols"], *xs, *dys, *old_values)
    outs = list(outs)
    values = tuple(outs.pop(0) for _ in range(2))
    for older, kind in zip(olders, kinds):
        older.values = tuple(outs.pop(0) for _ in range(FOLDS[kind].gives))
    return values


class Scatter:
    def __init__(self, xs, dys, place, rows, widths, starts, sources, olders):
        self.values = weight_grad(xs, dys, place, rows, widths, starts, sources, olders)
        self.stage = 0

    def fold(self):
        fold = FOLDS[self.stage]
        outs = pl.pallas_call(
            fold.kernel,
            out_shape=[fold.gives_part.shape(self.values[0].shape[-2:])] * fold.gives,
            compiler_params=pltpu.CompilerParams(vmem_limit_bytes=VMEM_BYTES),
            cost_estimate=SMALL,
            name=fold.kernel.__name__,
        )(*self.values)
        self.values = tuple(outs)

    def advance(self, values):
        if self.stage == 0:
            send, keep = values
            new = (keep, hop(send, "core"))
        elif self.stage == 1:
            a_send, a_keep, b_send, b_keep = values
            new = (a_keep, hop(a_send, "x"), b_keep, hop(b_send, "y"))
        elif self.stage == 2:
            a_send, a_keep, b_send, b_keep = values
            new = (a_keep, hop(a_send, "y"), b_keep, hop(b_send, "x"))
        else:
            mine = lax.psum_scatter(
                values[0].reshape(-1, values[0].shape[-1]),
                "win",
                scatter_dimension=0,
                tiled=True,
                axis_index_groups=z_groups(),
            )
            new = mine.astype(jnp.float32)
        self.values = new
        self.stage += 1


class Total:
    def __init__(self, value, links):
        self.shape = value.shape
        self.size = value.size
        self.values = jnp.pad(value.reshape(-1), (0, -value.size % 1024)).reshape(-1, 128)
        self.links = list(links)

    def advance(self, values):
        self.values = values + hop(values, self.links.pop(0))

    def result(self):
        return self.values.reshape(-1)[: self.size].reshape(self.shape)


def together(jobs, state):
    held, state = lax.optimization_barrier(([job.values for job in jobs], state))
    for job, values in zip(jobs, held):
        job.advance(values)
    return state


def pair_table(extent):
    table_dims = (extent, extent, 2 * extent - 1)
    query_pos = lax.broadcasted_iota(jnp.int32, table_dims, 0)
    key_pos = lax.broadcasted_iota(jnp.int32, table_dims, 1)
    offset = lax.broadcasted_iota(jnp.int32, table_dims, 2)
    return (query_pos - key_pos + extent - 1 == offset).astype(jnp.float32)


def spatial_strip(table):
    side = 2 * WS - 1
    onehot = pair_table(WS).transpose(2, 1, 0).reshape(side, WS * WS)
    strip = jnp.dot(table.reshape(HEADS * side, side), onehot, precision=highest)
    strip = strip.reshape(HEADS, side, WS, WS).transpose(0, 2, 1, 3).reshape(HEADS, WS, side * WS)
    return jnp.pad(strip, ((0, 0), (0, 0), (0, WS)))


def spatial_strip_back(strip):
    side = 2 * WS - 1
    shaped = strip.reshape(HEADS, 2, WS, 2 * WS).transpose(0, 2, 1, 3)
    return shaped.reshape(HEADS, 2 * WS, 2 * WS)[:, :side, :side]


def joint_onehot():
    span = 2 * HS - 1
    place = np.arange(HS)
    apart = place[None, :] - place[:, None] + HS - 1
    wanted = apart[:, None, :, None] * span + apart[None, :, None, :]
    offset = np.arange(span * span)[:, None]
    return jnp.asarray((offset == wanted.reshape(1, -1)).astype(np.float32))


def joint_strip(table):
    frames = 2 * FR - 1
    places = HS * HS
    strip = jnp.dot(table.reshape(HEADS * frames, -1), joint_onehot(), precision=highest)
    strip = strip.reshape(HEADS, frames, places, places).transpose(0, 2, 1, 3)
    return jnp.pad(strip.reshape(HEADS, places, frames * places), ((0, 0), (0, 0), (0, places)))


def joint_strip_back(strip):
    span = 2 * HS - 1
    shaped = strip.reshape(HEADS, 2, 2 * FR - 1, HS, 2 * HS).transpose(0, 2, 3, 1, 4)
    return shaped.reshape(HEADS, 2 * FR - 1, 2 * HS, 2 * HS)[:, :, :span, :span]


def head_lanes(which):
    lane = lax.broadcasted_iota(jnp.int32, (1, 128), 1)
    return (lane // 64 == which).astype(jnp.float32)


def attend_kernel(q_ref, k_ref, v_ref, strip_ref, mask_ref, out_ref, probs_ref, bias, *, wins, length):
    rows, lanes = strip_ref.shape[1:]
    blocks = length // rows
    masks = mask_ref.shape[0]
    for head in range(2):
        strip = strip_ref[head]
        for block in range(blocks):
            offset = (blocks - 1 - block) * rows
            turned = strip if offset == 0 else pltpu.roll(strip, lanes - offset, 1)
            bias[block * rows : (block + 1) * rows, :] = turned[:, :length]
        chosen = head_lanes(head)
        low = chosen.astype(jnp.bfloat16)
        for win in range(wins):
            here = slice(win * length, (win + 1) * length)
            queries = q_ref[here, :] * jnp.bfloat16(0.125)
            scores = lax.dot_general(k_ref[here, :] * low, queries, NT, preferred_element_type=jnp.float32)
            scores = jnp.where(mask_ref[win % masks] > 0.0, scores + bias[...], masked_score)
            raised = jnp.exp(scores - jnp.max(scores, axis=0, keepdims=True))
            probs = raised * (1.0 / jnp.sum(raised, axis=0, keepdims=True))
            probs = probs.astype(jnp.bfloat16)
            probs_ref[head, win] = probs
            mixed = lax.dot_general(probs, v_ref[here, :] * low, TN, preferred_element_type=jnp.float32)
            if head == 0:
                out_ref[here, :] = mixed.astype(jnp.bfloat16)
            else:
                out_ref[here, :] = out_ref[here, :] + mixed.astype(jnp.bfloat16)


def attend(qkv, strip, allowed, wins, length):
    count, triple = qkv.shape
    width = triple // 3
    rows, lanes = strip.shape[1:]
    return pl.pallas_call(
        partial(attend_kernel, wins=wins, length=length),
        grid=(HEADS // 2,),
        out_shape=[
            jax.ShapeDtypeStruct((count, width), jnp.bfloat16),
            jax.ShapeDtypeStruct((HEADS, wins, length, length), jnp.bfloat16),
        ],
        in_specs=[
            pl.BlockSpec((count, 128), lambda h: (0, h)),
            pl.BlockSpec((count, 128), lambda h: (0, HEADS // 2 + h)),
            pl.BlockSpec((count, 128), lambda h: (0, HEADS + h)),
            pl.BlockSpec((2, rows, lanes), lambda h: (h, 0, 0)),
            pl.BlockSpec(allowed.shape, lambda h: (0, 0, 0)),
        ],
        out_specs=[
            pl.BlockSpec((count, 128), lambda h: (0, h)),
            pl.BlockSpec((2, wins, length, length), lambda h: (h, 0, 0, 0)),
        ],
        scratch_shapes=[pltpu.VMEM((length, length), jnp.float32)],
        compiler_params=pltpu.CompilerParams(vmem_limit_bytes=VMEM_BYTES),
        cost_estimate=SMALL,
        name="attend",
    )(qkv, qkv, qkv, strip, allowed)


def attend_back_kernel(
    q_ref, k_ref, v_ref, g_ref, probs_ref, out_ref, strip_ref, total, *, wins, length, rows
):
    blocks = length // rows
    width = out_ref.shape[1] // 3
    step = pl.program_id(0)
    grads = [[None] * 3 for _ in range(wins)]
    total[...] = jnp.zeros_like(total)
    for head in range(2):
        chosen = head_lanes(head)
        low = chosen.astype(jnp.bfloat16)
        for win in range(wins):
            here = slice(win * length, (win + 1) * length)
            queries = q_ref[here, :] * jnp.bfloat16(0.125)
            key_rows = k_ref[here, :]
            outer = g_ref[here, :]
            probs = probs_ref[head, win]
            grad_probs = lax.dot_general(v_ref[here, :] * low, outer, NT, preferred_element_type=jnp.float32)
            wide = probs.astype(jnp.float32)
            inner = jnp.sum(wide * grad_probs, axis=0, keepdims=True)
            grad_scores = (wide * (grad_probs - inner)).astype(jnp.bfloat16)
            if win == 0:
                total[:, :length] = grad_scores.astype(jnp.float32)
            else:
                total[:, :length] = total[:, :length] + grad_scores.astype(jnp.float32)
            new = (
                lax.dot_general(grad_scores, key_rows, TN, preferred_element_type=jnp.float32) * 0.125,
                jnp.dot(grad_scores, queries, preferred_element_type=jnp.float32),
                jnp.dot(probs, outer, preferred_element_type=jnp.float32),
            )
            for kind in range(3):
                column = pl.multiple_of(step * 128 + kind * width, 128)
                if head == 0:
                    out_ref[here, pl.ds(column, 128)] = (new[kind] * chosen).astype(jnp.bfloat16)
                else:
                    out_ref[here, pl.ds(column, 128)] = out_ref[here, pl.ds(column, 128)] + (
                        new[kind] * chosen
                    ).astype(jnp.bfloat16)
        strip = total[:rows, :] if blocks == 1 else pltpu.roll(total[:rows, :], (blocks - 1) * rows, 1)
        for block in range(1, blocks):
            offset = (blocks - 1 - block) * rows
            piece = total[block * rows : (block + 1) * rows, :]
            strip = strip + (piece if offset == 0 else pltpu.roll(piece, offset, 1))
        if rows > WS:
            strip = split_rows(strip)
        skew(strip, strip_ref, head)


def split_rows(strip):
    lane = lax.broadcasted_iota(jnp.int32, (1, 128), 1)
    groups = []
    for offset in range(2 * FR - 1):
        odd = offset % 2
        there = slice(offset // 2 * 128, offset // 2 * 128 + 128)
        summed = None
        for row in range(HS):
            piece = jnp.where(lane // 64 == odd, strip[row * HS : (row + 1) * HS, there], 0.0)
            shift = (64 * odd + (HS - 1 - row) * HS) % 128
            piece = piece if shift == 0 else pltpu.roll(piece, shift, 1)
            summed = piece if summed is None else summed + piece
        groups.append(summed)
    return jnp.concatenate(groups, axis=1)


def skew(strip, out_ref, head):
    columns, lanes = strip.shape
    lane = lax.broadcasted_iota(jnp.int32, (1, lanes), 1)
    for odd in range(2):
        part = jnp.where(lane // columns % 2 == odd, strip, 0.0)
        if odd:
            part = pltpu.roll(part, lanes - columns, 1)
        summed = part[columns - 1 :, :]
        for column in range(columns - 1):
            summed = summed + pltpu.roll(part[column : column + 1, :], columns - 1 - column, 1)
        out_ref[head, odd : odd + 1, :] = summed


def attend_back(qkv, probs, grad_out, wins, length, rows, lanes, strip):
    count, triple = qkv.shape
    return pl.pallas_call(
        partial(attend_back_kernel, wins=wins, length=length, rows=rows),
        grid=(HEADS // 2,),
        out_shape=[
            jax.ShapeDtypeStruct((count, triple), jnp.bfloat16),
            jax.ShapeDtypeStruct((HEADS,) + strip, jnp.float32),
        ],
        in_specs=[
            pl.BlockSpec((count, 128), lambda h: (0, h)),
            pl.BlockSpec((count, 128), lambda h: (0, HEADS // 2 + h)),
            pl.BlockSpec((count, 128), lambda h: (0, HEADS + h)),
            pl.BlockSpec((count, 128), lambda h: (0, h)),
            pl.BlockSpec((2, wins, length, length), lambda h: (h, 0, 0, 0)),
        ],
        out_specs=[
            pl.BlockSpec((count, triple), lambda h: (0, 0)),
            pl.BlockSpec((2,) + strip, lambda h: (h, 0, 0)),
        ],
        scratch_shapes=[pltpu.VMEM((length, lanes), jnp.float32)],
        compiler_params=pltpu.CompilerParams(vmem_limit_bytes=VMEM_BYTES),
        cost_estimate=SMALL,
        name="attend_back",
    )(qkv, qkv, qkv, grad_out, probs)


def plain_norm(values):
    center = values - jnp.mean(values, axis=-1, keepdims=True)
    spread = jnp.mean(center * center, axis=-1, keepdims=True)
    scale = lax.rsqrt(spread + epsilon)
    return center * scale, scale


def modulated_norm(values, shift_vec, scale_vec):
    return (plain_norm(values)[0] * (1.0 + scale_vec) + shift_vec).astype(jnp.bfloat16)


def row_call(kernel, wide, vectors, kept, sums, name):
    count, width = wide[0].shape
    block = pl.BlockSpec((count // 2, width), lambda i: (i, 0))
    whole = pl.BlockSpec((1, width), lambda i: (0, 0))
    out_shape = [jax.ShapeDtypeStruct((count, width), kind) for kind in kept]
    out_specs = [block] * len(kept)
    if sums:
        out_shape.append(jax.ShapeDtypeStruct((8, width), jnp.float32))
        out_specs.append(pl.BlockSpec((8, width), lambda i: (0, 0)))
    return pl.pallas_call(
        kernel,
        grid=(2,),
        out_shape=out_shape,
        in_specs=[block] * len(wide) + [whole] * len(vectors),
        out_specs=out_specs,
        compiler_params=pltpu.CompilerParams(vmem_limit_bytes=VMEM_BYTES),
        cost_estimate=SMALL,
        name=name,
    )(*wide, *[vector.reshape(1, width) for vector in vectors])


def residual_kernel(rows, branch, gate, shift, scale, out, unit):
    values = rows[...] + gate[...] * branch[...]
    out[...] = values
    unit[...] = modulated_norm(values, shift[...], scale[...])


def add_branch(rows, branch, gate, shift, scale):
    kept = (jnp.float32, jnp.bfloat16)
    return row_call(residual_kernel, [rows, branch], [gate, shift, scale], kept, False, "add_branch")


def norm_back_kernel(grad_in, values, grad_rows, *refs):
    if len(refs) == 6:
        branch, scale, gate, out, gated, sums = refs
    else:
        scale, out, sums = refs
    unit, rate = plain_norm(values[...])
    grads = grad_in[...]
    inner = grads * (1.0 + scale[...])
    mean_one = jnp.mean(inner, axis=-1, keepdims=True)
    mean_two = jnp.mean(inner * unit, axis=-1, keepdims=True)
    total = grad_rows[...] + rate * (inner - mean_one - unit * mean_two)
    out[...] = total

    @pl.when(pl.program_id(0) == 0)
    def clear():
        sums[...] = jnp.zeros_like(sums)

    sums[0:1, :] += jnp.sum(grads, axis=0, keepdims=True)
    sums[1:2, :] += jnp.sum(grads * unit, axis=0, keepdims=True)
    if len(refs) == 6:
        gated[...] = (gate[...] * total).astype(jnp.bfloat16)
        sums[2:3, :] += jnp.sum(total * branch[...], axis=0, keepdims=True)


def norm_back(grad_in, values, grad_rows, scale, branch=None, gate=None):
    if branch is None:
        kept = (jnp.float32,)
        return row_call(norm_back_kernel, [grad_in, values, grad_rows], [scale], kept, True, "norm_back")
    kept = (jnp.float32, jnp.bfloat16)
    wide = [grad_in, values, grad_rows, branch]
    return row_call(norm_back_kernel, wide, [scale, gate], kept, True, "norm_back")


def gelu_both(upward):
    half = 0.5 * (1.0 + lax.erf(upward * 0.7071067811865476))
    density = 0.3989422804014327 * jnp.exp(-0.5 * upward * upward)
    return (upward * half).astype(jnp.bfloat16), (half + upward * density).astype(jnp.bfloat16)


def joint_group(rows):
    split = rows.reshape(FR * HS, 2, HS, rows.shape[-1])
    return split.transpose(1, 0, 2, 3).reshape(rows.shape)


def joint_ungroup(rows):
    split = rows.reshape(2, FR * HS, HS, rows.shape[-1])
    return split.transpose(1, 0, 2, 3).reshape(rows.shape)


def window_group(flat_rows):
    return flat_rows.reshape(SLOTS, WS * WS, flat_rows.shape[-1])


def split_halves(half_rows, own_half):
    pair_windows = half_rows.shape[0]
    filler = jnp.zeros((2 * SLOTS - pair_windows,) + half_rows.shape[1:], half_rows.dtype)
    padded = jnp.concatenate([half_rows, filler], axis=0)
    keep_part = lax.dynamic_slice_in_dim(padded, own_half * SLOTS, SLOTS, 0)
    send_part = lax.dynamic_slice_in_dim(padded, (1 - own_half) * SLOTS, SLOTS, 0)
    return (keep_part, send_part)


def join_windows(keep_part, came_part, own_half):
    upper_half = jnp.where(own_half == 0, keep_part, came_part)
    lower_half = jnp.where(own_half == 0, came_part, keep_part)
    joined = jnp.concatenate([upper_half, lower_half], axis=1)
    return joined.reshape(-1, joined.shape[-1])


def split_windows(win_rows, own_half):
    grouped = window_group(win_rows)
    half_len = grouped.shape[1] // 2
    upper_half = grouped[:, :half_len]
    lower_half = grouped[:, half_len:]
    keep_part = jnp.where(own_half == 0, upper_half, lower_half)
    send_part = jnp.where(own_half == 0, lower_half, upper_half)
    return (keep_part, send_part)


def join_halves(keep_part, came_part, own_half, pair_windows):
    leading = jnp.where(own_half == 0, keep_part, came_part)
    trailing = jnp.where(own_half == 0, came_part, keep_part)
    joined = jnp.concatenate([leading, trailing], axis=0)[:pair_windows]
    return joined.reshape(-1, joined.shape[-1])


def from_pair(value):
    pairs = [(i, i ^ 1) for i in range(lax.axis_size("win"))]
    return lax.ppermute(value, "win", pairs)


class Weights:
    def __init__(self, masters, place, quick):
        self.quick = quick
        low = [master.astype(jnp.bfloat16) for master in masters]
        self.place = place
        if quick:
            shards = []
            for block in range(2):
                qkv, out, up, down = low[4 * block : 4 * block + 4]
                shards += [jnp.concatenate([qkv, out], axis=1), up, down]
            self.widths = [(384, 128), (512,), (128,)] * 2
            halves = [shard.reshape(2, shard.shape[0] // 2, -1) for shard in shards]
            self.jobs = [Gather(value, 2 * value.shape[1], False) for value in halves[:2]] + [None] * 4
            self.later = [(units, jnp.stack([halves[unit] for unit in units], axis=1)) for units in ((2, 5), (3, 4))]
        else:
            self.full = [
                lax.all_gather(lax.all_gather(shard, "win", axis=1, tiled=True), "clip", axis=0, tiled=True)
                for shard in low
            ]
            self.full = [tuple(self.full[0:2]), (self.full[2],), (self.full[3],)] + [
                tuple(self.full[4:6]),
                (self.full[6],),
                (self.full[7],),
            ]

    def go(self, moves, state, after=()):
        if not self.quick:
            return state
        jobs = [(self.jobs[unit], move) for unit, move in moves]
        jobs = [(job, move) for job, move in jobs if not (job.early and move == "near")]
        known = [(job, job.needs(move)) for job, move in jobs if job.needs(move) in job.held]
        known += [(self.jobs[unit], name) for unit, name in after]
        held, state = lax.optimization_barrier(([job.held[name] for job, name in known], state))
        for (job, name), values in zip(known, held):
            job.held[name] = values
        for job, move in jobs:
            job.go(move)
        return state

    def begin(self, state):
        if not self.quick:
            return state
        state, held = lax.optimization_barrier((state, [value for units, value in self.later]))
        for (units, unused), (a0, b0) in zip(self.later, held):
            a_came, b_came = hop(a0, "y"), hop(b0, "x")
            for place, unit in enumerate(units):
                near = [a0[place], a_came[place], b0[place], b_came[place]]
                halves = jnp.stack(near).reshape(2, 2, *near[0].shape)
                self.jobs[unit] = Gather(halves, 2 * near[0].shape[0], True)
        return state

    def apply(self, unit, x, kind):
        if self.quick:
            job = self.jobs[unit]
            return gathered(job.values(), self.place, x, job.rows, self.widths[unit], kind)
        wholes = self.full[unit]
        result = jnp.dot(x, wholes[0], preferred_element_type=jnp.float32)
        if kind == "gelu":
            return *gelu_both(result), *wholes
        return result if kind == "wide" else result.astype(jnp.bfloat16), *wholes


def body(
    tokens,
    grad_output,
    clip_height,
    clip_width,
    modulation,
    sp_qkv,
    sp_out,
    sp_up,
    sp_down,
    sp_table,
    st_qkv,
    st_out,
    st_up,
    st_down,
    st_table,
    quick,
):
    model_width = tokens.shape[-1]
    half_len = tokens.shape[-2]
    pair_windows = PAIR_LOCS * FR
    shard_index = lax.axis_index("win")
    clip_index = lax.axis_index("clip")
    pair_index = shard_index // 2
    own_half = shard_index % 2
    own_core = clip_index % 2
    own_x = clip_index // 2
    row_places = [
        (own_x ^ x_rel) * 2 + (own_core ^ c_rel) for c_rel in range(2) for x_rel in range(2)
    ]
    place = {
        "rows": jnp.stack(row_places).astype(jnp.int32),
        "cols": jnp.stack([own_half, own_half ^ 1]).astype(jnp.int32),
    }
    weights = Weights(
        (sp_qkv, sp_out, sp_up, sp_down, st_qkv, st_out, st_up, st_down), place, quick
    )
    mod = modulation[0]

    location = pair_index
    token_ids = jnp.arange(WS * WS, dtype=jnp.int32)
    row_pos = location // LOC_W * WS + token_ids // WS
    col_pos = location % LOC_W * WS + token_ids % WS
    sp_valid = (row_pos < clip_height[0]) & (col_pos < clip_width[0])
    sp_allowed = (sp_valid[None, :, None] | jnp.eye(WS * WS, dtype=bool)[None]).astype(jnp.float32)
    joint_len = FR * HS * HS
    joint_ids = jnp.arange(joint_len, dtype=jnp.int32)
    joint_row = location // LOC_W * WS + own_half * HS + joint_ids // HS % HS
    joint_col = location % LOC_W * WS + jnp.arange(2, dtype=jnp.int32)[:, None] * HS + joint_ids[None] % HS
    st_valid = (joint_row[None] < clip_height[0]) & (joint_col < clip_width[0])
    st_allowed = (st_valid[:, :, None] | jnp.eye(joint_len, dtype=bool)[None]).astype(jnp.float32)

    half_tokens = tokens.reshape(pair_windows, half_len, model_width)
    keep_part, send_part = split_halves(half_tokens, own_half)
    came_part = weights.begin(from_pair(send_part))
    came_part = weights.go([(0, "near")], came_part)
    win_input = join_windows(keep_part, came_part, own_half).astype(jnp.float32)
    attn_in_a = modulated_norm(win_input, mod[0], mod[1])

    go = weights.go
    state = (win_input, attn_in_a, sp_table)
    win_input, attn_in_a, sp_table = go([(0, "far"), (0, "core_near")], state)
    sp_strip = spatial_strip(sp_table)
    state = go([(1, "near")], (win_input, attn_in_a, sp_strip, sp_allowed))
    win_input, attn_in_a, sp_strip, sp_allowed = go([(0, "core_far")], state)
    qkv_a, w_qkv_a, w_out_a = weights.apply(0, attn_in_a, "narrow")
    win_input, qkv_a, w_out_a = go([(1, "far")], (win_input, qkv_a, w_out_a))
    win_input, qkv_a, w_out_a = go([(2, "near")], (win_input, qkv_a, w_out_a))
    attn_out_a, probs_a = attend(qkv_a, sp_strip, sp_allowed, SLOTS, WS * WS)
    win_input, attn_out_a, w_out_a = go([(1, "core_near")], (win_input, attn_out_a, w_out_a))
    mixed_a = product(attn_out_a, w_out_a)
    win_middle = win_input + mod[2] * mixed_a
    keep_part, send_part = split_windows(win_middle, own_half)
    send_part = send_part.astype(jnp.bfloat16)
    keep_part, send_part, st_table = go([(1, "core_far")], (keep_part, send_part, st_table))
    came_part = from_pair(send_part)
    keep_part, st_table = go([(2, "far"), (2, "core_near")], (keep_part, st_table))
    st_strip = joint_strip(st_table)
    keep_part, came_part, st_strip, st_allowed = lax.optimization_barrier(
        (keep_part, came_part, st_strip, st_allowed)
    )
    middle_a = joint_group(join_halves(keep_part, came_part.astype(jnp.float32), own_half, pair_windows))
    mlp_in_a = modulated_norm(middle_a, mod[3], mod[4])

    hidden_a, slope_a, w_up_a = weights.apply(1, mlp_in_a, "gelu")
    state = go([(2, "core_far")], (middle_a, hidden_a, slope_a))
    middle_a, hidden_a, slope_a = go([(3, "far")], state)
    downward_a, w_down_a = weights.apply(2, hidden_a, "wide")
    middle_a, downward_a = go([(3, "core_near")], (middle_a, downward_a))
    first_out, attn_in_b = add_branch(middle_a, downward_a, mod[5], mod[6], mod[7])

    first_out, attn_in_b = go([(3, "core_far")], (first_out, attn_in_b))
    first_out, attn_in_b = go([(4, "far")], (first_out, attn_in_b))
    qkv_b, w_qkv_b, w_out_b = weights.apply(3, attn_in_b, "narrow")
    first_out, qkv_b, w_out_b = go([(4, "core_near")], (first_out, qkv_b, w_out_b))
    attn_out_b, probs_b = attend(qkv_b, st_strip, st_allowed, 2, joint_len)
    first_out, attn_out_b, w_out_b = go([(4, "core_far")], (first_out, attn_out_b, w_out_b))
    first_out, attn_out_b, w_out_b = go([(5, "far")], (first_out, attn_out_b, w_out_b))
    mixed_b = product(attn_out_b, w_out_b)
    middle_b, mlp_in_b = add_branch(first_out, mixed_b, mod[8], mod[9], mod[10])
    hidden_b, slope_b, w_up_b = weights.apply(4, mlp_in_b, "gelu")
    middle_b, hidden_b, slope_b = go([(5, "core_near"), (5, "core_far")], (middle_b, hidden_b, slope_b))

    def start_grad(xs, dys, rows, widths, starts, sources, olders=()):
        if quick:
            return Scatter(xs, dys, place, rows, widths, starts, sources, olders)
        return Plain(xs, dys, widths, starts, sources)

    def rounds(jobs, state):
        if quick:
            return together(jobs, state)
        return state

    def hold(jobs, state):
        if not quick:
            return state
        state, held = lax.optimization_barrier((state, [job.values for job in jobs]))
        for job, values in zip(jobs, held):
            job.values = values
        return state

    def settle(jobs, state):
        state = hold(jobs, state)
        if quick:
            for job in jobs:
                job.fold()
        return state

    grad_out_b = joint_group(grad_output.reshape(-1, model_width)).astype(jnp.float32)
    grad_down_b = (mod[11] * grad_out_b).astype(jnp.bfloat16)
    d_st_down = start_grad([hidden_b], [grad_down_b], 1024, (128,), (0,), (0,))
    grad_down_b, hidden_b = rounds([d_st_down], (grad_down_b, hidden_b))
    downward_b, w_down_b = weights.apply(5, hidden_b, "wide")
    grad_up_b = product_scaled(grad_down_b, w_down_b, slope_b)
    d_st_up = start_grad([mlp_in_b], [grad_up_b], 256, (512,), (0,), (0,), [d_st_down])
    grad_up_b, downward_b = rounds([d_st_up, d_st_down], (grad_up_b, downward_b))
    out_rows = middle_b + mod[11] * downward_b
    out_tokens = joint_ungroup(out_rows).reshape(tokens.shape)
    grad_gate_mb = jnp.sum(grad_out_b * downward_b, axis=0)
    grad_mlp_b = product_turned(grad_up_b, w_up_b)
    grad_middle_b, grad_mixed_b, sums_mb = norm_back(
        grad_mlp_b, middle_b, grad_out_b, mod[10], mixed_b, mod[8]
    )
    state = (grad_middle_b, grad_mixed_b)
    state = settle([d_st_up, d_st_down], state)
    grad_middle_b, grad_mixed_b = rounds([d_st_up, d_st_down], state)
    grad_attn_b = product_turned(grad_mixed_b, w_out_b, jnp.bfloat16)
    grad_qkv_b, strip_grad_b = attend_back(
        qkv_b, probs_b, grad_attn_b, 2, joint_len, *st_strip.shape[1:], (2, 128 * (2 * FR - 1))
    )
    grad_middle_b, grad_qkv_b, strip_grad_b, grad_gate_mb = hold(
        [d_st_down], (grad_middle_b, grad_qkv_b, strip_grad_b, grad_gate_mb)
    )
    d_st_attn = start_grad(
        [attn_in_b, attn_out_b],
        [grad_qkv_b, grad_qkv_b, grad_mixed_b],
        256,
        (256, 128, 128),
        (0, 8, 0),
        (0, 0, 1),
        [d_st_down],
    )
    state = hold([d_st_attn], (grad_middle_b, grad_qkv_b, strip_grad_b))
    state = settle([d_st_up], state)
    grad_middle_b, grad_qkv_b, strip_grad_b = rounds([d_st_attn, d_st_up, d_st_down], state)
    grad_in_b = product_turned(grad_qkv_b, w_qkv_b)
    grad_first, grad_down_a, sums_ab = norm_back(
        grad_in_b, first_out, grad_middle_b, mod[7], downward_a, mod[5]
    )
    grad_first, grad_down_a = hold([d_st_attn, d_st_up], (grad_first, grad_down_a))
    d_sp_down = start_grad(
        [hidden_a], [grad_down_a], 1024, (128,), (0,), (0,), [d_st_attn, d_st_up]
    )
    grad_first, grad_down_a = rounds([d_sp_down, d_st_attn, d_st_up], (grad_first, grad_down_a))
    grad_up_a = product_scaled(grad_down_a, w_down_a, slope_a)
    grad_first, grad_up_a = hold([d_sp_down], (grad_first, grad_up_a))
    d_sp_up = start_grad([mlp_in_a], [grad_up_a], 256, (512,), (0,), (0,), [d_sp_down])
    grad_first, grad_up_a = hold([d_sp_up], (grad_first, grad_up_a))
    grad_first, grad_up_a = settle([d_st_attn], (grad_first, grad_up_a))
    grad_first, grad_up_a = hold([d_sp_up], (grad_first, grad_up_a))
    grad_first, grad_up_a = rounds([d_sp_up, d_st_attn], (grad_first, grad_up_a))
    grad_mlp_a = product_turned(grad_up_a, w_up_a)
    grad_middle_a, sums_ma = norm_back(grad_mlp_a, middle_a, grad_first, mod[4])
    grad_middle_a = joint_ungroup(grad_middle_a)
    half_rows = grad_middle_a.reshape(pair_windows, -1, model_width)
    keep_part, send_part = split_halves(half_rows, own_half)
    send_part = send_part.astype(jnp.bfloat16)
    keep_part, send_part = hold([d_sp_up, d_st_attn], (keep_part, send_part))
    came_part = from_pair(send_part)
    keep_part = rounds([d_sp_down], keep_part)
    if quick:
        d_st_attn.fold()
        d_sp_up.fold()
    keep_part, came_part = rounds([d_st_attn], (keep_part, came_part))
    grad_win = join_windows(keep_part, came_part.astype(jnp.float32), own_half)
    grad_mixed_a = (mod[2] * grad_win).astype(jnp.bfloat16)
    grad_gate_aa = jnp.sum(grad_win * mixed_a, axis=0)
    grad_win, grad_mixed_a = rounds([d_sp_up], (grad_win, grad_mixed_a))
    grad_attn_a = product_turned(grad_mixed_a, w_out_a, jnp.bfloat16)
    grad_qkv_a, strip_grad_a = attend_back(
        qkv_a, probs_a, grad_attn_a, SLOTS, WS * WS, *sp_strip.shape[1:], (2, 2 * WS * WS)
    )
    grad_win, grad_qkv_a, strip_grad_a = settle([d_sp_down], (grad_win, grad_qkv_a, strip_grad_a))
    grad_win, grad_qkv_a, strip_grad_a = hold([d_st_attn], (grad_win, grad_qkv_a, strip_grad_a))
    grad_win, grad_qkv_a, strip_grad_a = rounds([d_sp_down], (grad_win, grad_qkv_a, strip_grad_a))
    d_sp_attn = start_grad(
        [attn_in_a, attn_out_a], [grad_qkv_a, grad_mixed_a], 256, (384, 128), (0, 0), (0, 1)
    )
    state = hold([d_sp_attn, d_sp_up, d_sp_down], (grad_win, grad_qkv_a, strip_grad_a, strip_grad_b))
    if quick:
        d_sp_up.fold()
        d_sp_down.fold()
    grad_win, grad_qkv_a, strip_grad_a, strip_grad_b = state
    tables = jnp.concatenate([strip_grad_a, strip_grad_b], axis=2)
    table_total = Total(tables, ("core", "z1", "z0", "y", "x"))
    state = (grad_win, grad_qkv_a)
    state = rounds([d_sp_attn, d_sp_up, d_sp_down, table_total], state)
    state = settle([d_sp_attn, d_sp_up], state)
    grad_win, grad_qkv_a = rounds([d_sp_attn, d_sp_up, table_total], state)
    grad_in_a = product_turned(grad_qkv_a, w_qkv_a)
    win_sum, sums_aa = norm_back(grad_in_a, win_input, grad_win, mod[1])
    win_sum, sums_aa = settle([d_sp_attn], (win_sum, sums_aa))
    mod_rows = [
        sums_aa[0],
        sums_aa[1],
        grad_gate_aa,
        sums_ma[0],
        sums_ma[1],
        sums_ab[2],
        sums_ab[0],
        sums_ab[1],
        sums_mb[2],
        sums_mb[0],
        sums_mb[1],
        grad_gate_mb,
    ]
    mod_total = Total(jnp.stack(mod_rows, axis=0), ("z1", "z0", "y"))
    win_sum = rounds([d_sp_attn, table_total], win_sum)
    keep_part, send_part = split_windows(win_sum, own_half)
    send_part = send_part.astype(jnp.bfloat16)
    keep_part, send_part = settle([d_sp_attn], (keep_part, send_part))
    keep_part, send_part = rounds([d_sp_attn, table_total, mod_total], (keep_part, send_part))
    came_part = from_pair(send_part)
    rounds([table_total, mod_total], ())
    rounds([mod_total], ())
    came_part = came_part.astype(jnp.float32)
    grad_tokens = join_halves(keep_part, came_part, own_half, pair_windows).reshape(tokens.shape)
    if quick:
        grad_modulation = mod_total.result()[None]
        table_sums = table_total.result()
    else:
        grad_modulation = lax.psum(jnp.stack(mod_rows, axis=0), "win")[None]
        table_sums = lax.psum(table_total.result(), ("clip", "win"))
    grad_sp_table = spatial_strip_back(table_sums[:, :, : 2 * WS * WS])
    grad_st_table = joint_strip_back(table_sums[:, :, 2 * WS * WS :])
    wide = d_st_attn.values
    wide_a = d_sp_attn.values
    out_width = wide.shape[1] // 4
    return (
        out_tokens,
        grad_tokens,
        grad_modulation,
        wide_a[:, : 3 * out_width],
        wide_a[:, 3 * out_width :],
        d_sp_up.values,
        d_sp_down.values,
        grad_sp_table,
        wide[:, : 2 * out_width],
        wide[:, 2 * out_width : 3 * out_width],
        wide[:, 3 * out_width :],
        d_st_up.values,
        d_st_down.values,
        grad_st_table,
    )


class Plain:
    def __init__(self, xs, dys, widths, starts, sources):
        grads = []
        for dy, width, start, source in zip(dys, widths, starts, sources):
            x = xs[source]
            part = dy[:, start * 2 * width : start * 2 * width + 8 * width]
            full = lax.dot_general(x, part, TN, preferred_element_type=jnp.float32)
            full = lax.psum_scatter(
                full.astype(jnp.bfloat16), "clip", scatter_dimension=0, tiled=True
            )
            grads.append(lax.psum_scatter(full, "win", scatter_dimension=1, tiled=True))
        self.values = jnp.concatenate(grads, axis=1).astype(jnp.float32)


def solution(mesh):
    grid = P("clip", "win")
    whole = P("clip", "win", None, None, None, None)
    in_specs = (whole, whole, P("clip"), P("clip"), P("clip", None, None)) + ((grid,) * 4 + (P(),)) * 2
    out_specs = (whole, whole, P("clip", None, None)) + (grid,) * 4 + (P(),) + (grid,) * 5 + (P(),)
    quick = mesh.shape["clip"] == 4 and mesh.shape["win"] == 8
    return jax.shard_map(
        partial(body, quick=quick), mesh=mesh, in_specs=in_specs, out_specs=out_specs, check_vma=False
    )
```

```python
from functools import partial
from typing import NamedTuple

import jax
import jax.numpy as jnp
import numpy as np
from jax import lax
from jax.experimental import pallas as pl
from jax.experimental.pallas import tpu as pltpu
from jax.sharding import PartitionSpec as P

HEADS = 16
WS = 16
FR = 5
LOC_W = 4
PAIR_LOCS = 1
HS = 8
SLOTS = 3
MIB = 1024 * 1024

SMALL = pl.CostEstimate(flops=1, bytes_accessed=1, transcendentals=0)

epsilon = 1e-06
masked_score = -1000000000.0
highest = lax.Precision.HIGHEST
NT = (((1,), (1,)), ((), ()))
TN = (((0,), (0,)), ((), ()))


BITS = {"core": ("clip", 1), "x": ("clip", 2), "y": ("win", 1), "z0": ("win", 2), "z1": ("win", 4)}


def hop(value, link):
    axis, mask = BITS[link]
    return lax.ppermute(value, axis, [(i, i ^ mask) for i in range(lax.axis_size(axis))])


def z_groups():
    size = lax.axis_size("win")
    return [list(range(start, size, 2)) for start in range(2)]


class Gather:
    def __init__(self, halves, rows, early):
        self.rows = rows
        self.early = early
        axis = halves.ndim - 2
        grown = lax.all_gather(halves, "win", axis=axis, tiled=False, axis_index_groups=z_groups())
        self.held = {"grown": (grown,)}

    def needs(self, move):
        if move == "far" and self.early:
            return "grown"
        return {"near": "grown", "far": "near", "core_near": "own", "core_far": "away"}[move]

    def go(self, move):
        values = self.held[self.needs(move)]
        if move == "near":
            (grown,) = values
            a0, b0 = grown[0], grown[1]
            self.held["near"] = (a0, hop(a0, "y"), b0, hop(b0, "x"))
        elif move == "far":
            if self.early:
                a1, b1 = values[0][0], values[0][1]
            else:
                a0, a_came, b0, b_came = values
                a1, b1 = jnp.stack([a0, a_came]), jnp.stack([b0, b_came])
            self.held["own"] = (a1, b1)
            self.held["away"] = (hop(a1, "x"), hop(b1, "y"))
        else:
            self.held[move] = tuple(hop(value, "core") for value in values)

    def values(self):
        pairs = [self.held[name] for name in ("own", "away", "core_near", "core_far")]
        return [pair[0] for pair in pairs] + [pair[1] for pair in pairs]


def gathered_kernel(row_of, y_of, x_ref, *refs, rows, widths, kind):
    count = len(widths)
    results = 2 if kind == "gelu" else 1
    pieces, refs = refs[:8], refs[8:]
    outs, wholes, held = refs[:results], refs[results : results + count], refs[results + count : -2]
    in_sems, out_sems = refs[-2:]
    half = rows // 2
    step = pl.program_id(0)

    def arrivals(z):
        copies = []
        for part in range(2):
            for c_rel in range(2):
                for x_rel in range(2):
                    row = row_of[c_rel * 2 + x_rel] * rows + part * half
                    row = pl.multiple_of(row, half)
                    for y_rel in range(2):
                        far, near = (x_rel, y_rel) if part == 0 else (y_rel, x_rel)
                        source = pieces[part * 4 + c_rel * 2 + far]
                        start = 0
                        for matrix, width in zip(held, widths):
                            col = pl.multiple_of((z * 2 + y_of[y_rel]) * width, 128)
                            copies.append(
                                pltpu.make_async_copy(
                                    source.at[near, z, :, pl.ds(start, width)],
                                    matrix.at[pl.ds(row, half), pl.ds(col, width)],
                                    in_sems.at[z * 16 * count + len(copies)],
                                )
                            )
                            start += width
        return copies

    def departures(z):
        copies = []
        for which, width in enumerate(widths):
            there = pl.ds(pl.multiple_of(z * 2 * width, 128), 2 * width)
            copies.append(
                pltpu.make_async_copy(
                    held[which].at[:, there], wholes[which].at[:, there], out_sems.at[z * count + which]
                )
            )
        return copies

    @pl.when(step == 0)
    def begin():
        for z in range(4):
            for copy in arrivals(z):
                copy.start()

    for copy in arrivals(step):
        copy.wait()
    for copy in departures(step):
        copy.start()
    wide = 2 * widths[0]
    chunk = 256 if kind == "gelu" else wide
    for first in range(0, wide, chunk):
        col = pl.multiple_of(step * wide + first, 128)
        there = slice(first, first + chunk)
        result = jnp.dot(
            x_ref[...], held[0][:, pl.ds(col, chunk)], preferred_element_type=jnp.float32
        )
        if kind == "gelu":
            outs[0][:, there], outs[1][:, there] = gelu_both(result)
        else:
            outs[0][:, there] = result.astype(outs[0].dtype)

    @pl.when(step == 3)
    def end():
        for z in range(4):
            for copy in departures(z):
                copy.wait()


def gathered(values, place, x, rows, widths, kind):
    shapes = [(4 * rows, 8 * width) for width in widths]
    results = 2 if kind == "gelu" else 1
    kept = jnp.float32 if kind == "wide" else jnp.bfloat16
    count = x.shape[0]
    return pl.pallas_call(
        partial(gathered_kernel, rows=rows, widths=widths, kind=kind),
        grid=(4,),
        out_shape=[jax.ShapeDtypeStruct((count, 8 * widths[0]), kept)] * results
        + [jax.ShapeDtypeStruct(shape, jnp.bfloat16) for shape in shapes],
        in_specs=[pl.BlockSpec(memory_space=pltpu.SMEM)] * 2
        + [pl.BlockSpec(x.shape, lambda z: (0, 0))]
        + [pl.BlockSpec(memory_space=pl.ANY)] * 8,
        out_specs=[pl.BlockSpec((count, 2 * widths[0]), lambda z: (0, z))] * results
        + [pl.BlockSpec(memory_space=pl.ANY)] * len(widths),
        scratch_shapes=[pltpu.VMEM(shape, jnp.bfloat16) for shape in shapes]
        + [pltpu.SemaphoreType.DMA((64 * len(widths),)), pltpu.SemaphoreType.DMA((4 * len(widths),))],
        compiler_params=pltpu.CompilerParams(vmem_limit_bytes=56 * MIB),
        cost_estimate=SMALL,
        name="gathered",
    )(place["rows"], place["cols"], x, *values)


def product_kernel(left, right, out, *, turned):
    if turned:
        result = lax.dot_general(left[...], right[...], NT, preferred_element_type=jnp.float32)
    else:
        result = jnp.dot(left[...], right[...], preferred_element_type=jnp.float32)
    out[...] = result.astype(out.dtype)


def scaled_kernel(left, right, factor, out):
    result = lax.dot_general(left[...], right[...], NT, preferred_element_type=jnp.float32)
    out[...] = (result * factor[...].astype(jnp.float32)).astype(out.dtype)


def tiled(kernel, left, right, columns, kept, turned, *factors):
    count = left.shape[0]
    total = right.shape[0] if turned else right.shape[1]
    block = pl.BlockSpec((count, columns), lambda i: (0, i))
    if turned:
        right_spec = pl.BlockSpec((columns, right.shape[1]), lambda i: (i, 0))
    else:
        right_spec = pl.BlockSpec((right.shape[0], columns), lambda i: (0, i))
    return pl.pallas_call(
        kernel,
        grid=(total // columns,),
        out_shape=jax.ShapeDtypeStruct((count, total), kept),
        in_specs=[pl.BlockSpec(left.shape, lambda i: (0, 0)), right_spec] + [block] * len(factors),
        out_specs=block,
        compiler_params=pltpu.CompilerParams(vmem_limit_bytes=56 * MIB),
        cost_estimate=SMALL,
        name="product",
    )(left, right, *factors)


def product(left, right):
    return tiled(partial(product_kernel, turned=False), left, right, 512, jnp.float32, False)


def product_turned(left, right, kept=jnp.float32):
    columns = 512 if right.shape[1] == 1024 else 256
    return tiled(partial(product_kernel, turned=True), left, right, columns, kept, True)


def product_scaled(left, right, factor):
    return tiled(scaled_kernel, left, right, 1024, jnp.bfloat16, True, factor)


def grad_kernel(row_of, y_of, *refs, rows, widths, sources, kinds):
    count = len(widths)
    lefts = max(sources) + 1
    refs = list(refs)
    x_refs = [refs.pop(0) for _ in range(lefts)]
    dy_refs = [refs.pop(0) for _ in range(count)]
    old_refs = [[refs.pop(0) for _ in range(FOLDS[kind].takes)] for kind in kinds]
    send, keep = refs.pop(0), refs.pop(0)
    new_refs = [[refs.pop(0) for _ in range(FOLDS[kind].gives)] for kind in kinds]
    turns = refs
    half = rows // 2

    @pl.when(pl.program_id(0) == 0)
    def turn():
        for x_ref, turned in zip(x_refs, turns):
            for place in range(4):
                start = pl.multiple_of(row_of[place] * rows, 128)
                turned[place * rows : (place + 1) * rows, :] = x_ref[:, pl.ds(start, rows)].T

    offset = 0
    for dy_ref, width, source in zip(dy_refs, widths, sources):
        turned = turns[source]
        sides = [
            dy_ref[:, pl.ds(pl.multiple_of(y_of[y_rel] * width, 128), width)] for y_rel in range(2)
        ]
        product = jnp.dot(
            turned[...], jnp.concatenate(sides, axis=1), preferred_element_type=jnp.float32
        ).astype(jnp.bfloat16)
        for c_rel, out in ((0, keep), (1, send)):
            for x_rel in range(2):
                for ab in range(2):
                    first = (c_rel * 2 + x_rel) * rows + ab * half
                    for y_rel in range(2):
                        out[ab, x_rel, y_rel, 0, :, offset : offset + width] = product[
                            first : first + half, y_rel * width : (y_rel + 1) * width
                        ]
        offset += width
    for kind, old, new in zip(kinds, old_refs, new_refs):
        FOLDS[kind].kernel(*old, *new)


def fold_first(old_keep, old_came, a_send, a_keep, b_send, b_keep):
    for near in range(2):
        a_send[near] = old_keep[0, 1, near] + old_came[0, 1, near]
        a_keep[near] = old_keep[0, 0, near] + old_came[0, 0, near]
        b_send[near] = old_keep[1, near, 1] + old_came[1, near, 1]
        b_keep[near] = old_keep[1, near, 0] + old_came[1, near, 0]


def fold_second(a_keep, a_came, b_keep, b_came, a_out, a_held, b_out, b_held):
    a_out[...] = a_keep[1] + a_came[1]
    a_held[...] = a_keep[0] + a_came[0]
    b_out[...] = b_keep[1] + b_came[1]
    b_held[...] = b_keep[0] + b_came[0]


def fold_third(a_keep, a_came, b_keep, b_came, both):
    both[:, 0] = a_keep[...] + a_came[...]
    both[:, 1] = b_keep[...] + b_came[...]


class Part(NamedTuple):
    lead: tuple

    def shape(self, tail):
        return jax.ShapeDtypeStruct(self.lead + tail, jnp.bfloat16)

    def spec(self, tail):
        where = self.lead.index(4)
        block = tuple(1 if dim == where else size for dim, size in enumerate(self.lead))
        return pl.BlockSpec(
            block + tail, lambda z: (0,) * where + (z,) + (0,) * (len(block) + 1 - where)
        )


WHOLE, QUARTER, EIGHTH, TURNED = Part((2, 2, 2, 4)), Part((2, 4)), Part((4,)), Part((4, 2))


class Fold(NamedTuple):
    kernel: object
    takes: int
    takes_part: Part
    gives: int
    gives_part: Part


FOLDS = {
    1: Fold(fold_first, 2, WHOLE, 4, QUARTER),
    2: Fold(fold_second, 4, QUARTER, 4, EIGHTH),
    3: Fold(fold_third, 4, EIGHTH, 1, TURNED),
}


def weight_grad(xs, dys, place, rows, widths, starts, sources, olders):
    count = xs[0].shape[0]
    tail = (rows // 2, sum(widths))
    kinds = tuple(older.stage for older in olders)
    out_shape, out_specs = [WHOLE.shape(tail)] * 2, [WHOLE.spec(tail)] * 2
    old_specs, old_values = [], []
    for older, kind in zip(olders, kinds):
        fold = FOLDS[kind]
        old_tail = older.values[0].shape[-2:]
        old_specs += [fold.takes_part.spec(old_tail)] * fold.takes
        old_values += older.values
        out_shape += [fold.gives_part.shape(old_tail)] * fold.gives
        out_specs += [fold.gives_part.spec(old_tail)] * fold.gives
    outs = pl.pallas_call(
        partial(grad_kernel, rows=rows, widths=widths, sources=sources, kinds=kinds),
        grid=(4,),
        out_shape=out_shape,
        in_specs=[pl.BlockSpec(memory_space=pltpu.SMEM)] * 2
        + [pl.BlockSpec((count, 4 * rows), lambda z: (0, 0))] * len(xs)
        + [
            pl.BlockSpec((count, 2 * width), lambda z, s=start: (0, s + z))
            for width, start in zip(widths, starts)
        ]
        + old_specs,
        out_specs=out_specs,
        scratch_shapes=[pltpu.VMEM((4 * rows, count), jnp.bfloat16)] * len(xs),
        compiler_params=pltpu.CompilerParams(vmem_limit_bytes=56 * MIB),
        cost_estimate=SMALL,
        name="weight_grad",
    )(place["rows"], place["cols"], *xs, *dys, *old_values)
    outs = list(outs)
    values = tuple(outs.pop(0) for _ in range(2))
    for older, kind in zip(olders, kinds):
        older.values = tuple(outs.pop(0) for _ in range(FOLDS[kind].gives))
    return values


class Scatter:
    def __init__(self, xs, dys, place, rows, widths, starts, sources, olders):
        self.values = weight_grad(xs, dys, place, rows, widths, starts, sources, olders)
        self.stage = 0

    def fold(self):
        fold = FOLDS[self.stage]
        outs = pl.pallas_call(
            fold.kernel,
            out_shape=[fold.gives_part.shape(self.values[0].shape[-2:])] * fold.gives,
            compiler_params=pltpu.CompilerParams(vmem_limit_bytes=16 * MIB),
            cost_estimate=SMALL,
            name=fold.kernel.__name__,
        )(*self.values)
        self.values = tuple(outs)

    def advance(self, values):
        if self.stage == 0:
            send, keep = values
            new = (keep, hop(send, "core"))
        elif self.stage == 1:
            a_send, a_keep, b_send, b_keep = values
            new = (a_keep, hop(a_send, "x"), b_keep, hop(b_send, "y"))
        elif self.stage == 2:
            a_send, a_keep, b_send, b_keep = values
            new = (a_keep, hop(a_send, "y"), b_keep, hop(b_send, "x"))
        else:
            mine = lax.psum_scatter(
                values[0].reshape(-1, values[0].shape[-1]),
                "win",
                scatter_dimension=0,
                tiled=True,
                axis_index_groups=z_groups(),
            )
            new = mine.astype(jnp.float32)
        self.values = new
        self.stage += 1


class Total:
    def __init__(self, value, links):
        self.shape = value.shape
        self.size = value.size
        self.values = jnp.pad(value.reshape(-1), (0, -value.size % 1024)).reshape(-1, 128)
        self.links = list(links)

    def advance(self, values):
        self.values = values + hop(values, self.links.pop(0))

    def result(self):
        return self.values.reshape(-1)[: self.size].reshape(self.shape)


def together(jobs, state):
    held, state = lax.optimization_barrier(([job.values for job in jobs], state))
    for job, values in zip(jobs, held):
        job.advance(values)
    return state


def pair_table(extent):
    table_dims = (extent, extent, 2 * extent - 1)
    query_pos = lax.broadcasted_iota(jnp.int32, table_dims, 0)
    key_pos = lax.broadcasted_iota(jnp.int32, table_dims, 1)
    offset = lax.broadcasted_iota(jnp.int32, table_dims, 2)
    return (query_pos - key_pos + extent - 1 == offset).astype(jnp.float32)


def spatial_strip(table):
    side = 2 * WS - 1
    onehot = pair_table(WS).transpose(2, 1, 0).reshape(side, WS * WS)
    strip = jnp.dot(table.reshape(HEADS * side, side), onehot, precision=highest)
    strip = strip.reshape(HEADS, side, WS, WS).transpose(0, 2, 1, 3).reshape(HEADS, WS, side * WS)
    return jnp.pad(strip, ((0, 0), (0, 0), (0, WS)))


def spatial_strip_back(strip):
    side = 2 * WS - 1
    shaped = strip.reshape(HEADS, 2, WS, 2 * WS).transpose(0, 2, 1, 3)
    return shaped.reshape(HEADS, 2 * WS, 2 * WS)[:, :side, :side]


def joint_onehot():
    span = 2 * HS - 1
    place = np.arange(HS)
    apart = place[None, :] - place[:, None] + HS - 1
    wanted = apart[:, None, :, None] * span + apart[None, :, None, :]
    offset = np.arange(span * span)[:, None]
    return jnp.asarray((offset == wanted.reshape(1, -1)).astype(np.float32))


def joint_strip(table):
    frames = 2 * FR - 1
    places = HS * HS
    strip = jnp.dot(table.reshape(HEADS * frames, -1), joint_onehot(), precision=highest)
    strip = strip.reshape(HEADS, frames, places, places).transpose(0, 2, 1, 3)
    return jnp.pad(strip.reshape(HEADS, places, frames * places), ((0, 0), (0, 0), (0, places)))


def joint_strip_back(strip):
    span = 2 * HS - 1
    shaped = strip.reshape(HEADS, 2, 2 * FR - 1, HS, 2 * HS).transpose(0, 2, 3, 1, 4)
    return shaped.reshape(HEADS, 2 * FR - 1, 2 * HS, 2 * HS)[:, :, :span, :span]


def head_lanes(which):
    lane = lax.broadcasted_iota(jnp.int32, (1, 128), 1)
    return (lane // 64 == which).astype(jnp.float32)


def attend_kernel(q_ref, k_ref, v_ref, strip_ref, mask_ref, out_ref, probs_ref, bias, *, wins, length):
    rows, lanes = strip_ref.shape[1:]
    blocks = length // rows
    masks = mask_ref.shape[0]
    mixed = [None] * wins
    for head in range(2):
        strip = strip_ref[head]
        for block in range(blocks):
            offset = (blocks - 1 - block) * rows
            turned = strip if offset == 0 else pltpu.roll(strip, lanes - offset, 1)
            bias[block * rows : (block + 1) * rows, :] = turned[:, :length]
        low = head_lanes(head).astype(jnp.bfloat16)
        for win in range(wins):
            here = slice(win * length, (win + 1) * length)
            queries = q_ref[here, :] * jnp.bfloat16(0.125)
            scores = lax.dot_general(k_ref[here, :] * low, queries, NT, preferred_element_type=jnp.float32)
            scores = jnp.where(mask_ref[win % masks] > 0.0, scores + bias[...], masked_score)
            raised = jnp.exp(scores - jnp.max(scores, axis=0, keepdims=True))
            probs = raised * (1.0 / jnp.sum(raised, axis=0, keepdims=True))
            probs = probs.astype(jnp.bfloat16)
            probs_ref[head, win] = probs
            turned = (v_ref[here, :] * low).T
            part = jnp.dot(turned, probs, preferred_element_type=jnp.float32)
            mixed[win] = part if head == 0 else mixed[win] + part
    for win in range(wins):
        out_ref[win * length : (win + 1) * length, :] = mixed[win].T.astype(jnp.bfloat16)


def attend(qkv, strip, allowed, wins, length):
    count, triple = qkv.shape
    width = triple // 3
    rows, lanes = strip.shape[1:]
    return pl.pallas_call(
        partial(attend_kernel, wins=wins, length=length),
        grid=(HEADS // 2,),
        out_shape=[
            jax.ShapeDtypeStruct((count, width), jnp.bfloat16),
            jax.ShapeDtypeStruct((HEADS, wins, length, length), jnp.bfloat16),
        ],
        in_specs=[
            pl.BlockSpec((count, 128), lambda h: (0, h)),
            pl.BlockSpec((count, 128), lambda h: (0, HEADS // 2 + h)),
            pl.BlockSpec((count, 128), lambda h: (0, HEADS + h)),
            pl.BlockSpec((2, rows, lanes), lambda h: (h, 0, 0)),
            pl.BlockSpec(allowed.shape, lambda h: (0, 0, 0)),
        ],
        out_specs=[
            pl.BlockSpec((count, 128), lambda h: (0, h)),
            pl.BlockSpec((2, wins, length, length), lambda h: (h, 0, 0, 0)),
        ],
        scratch_shapes=[pltpu.VMEM((length, length), jnp.float32)],
        compiler_params=pltpu.CompilerParams(vmem_limit_bytes=56 * MIB),
        cost_estimate=SMALL,
        name="attend",
    )(qkv, qkv, qkv, strip, allowed)


def attend_back_kernel(
    q_ref, k_ref, v_ref, g_ref, probs_ref, out_ref, strip_ref, total, *, wins, length, rows
):
    blocks = length // rows
    width = out_ref.shape[1] // 3
    step = pl.program_id(0)
    query_grads = [None] * wins
    total[...] = jnp.zeros_like(total)
    for head in range(2):
        chosen = head_lanes(head)
        low = chosen.astype(jnp.bfloat16)
        for win in range(wins):
            here = slice(win * length, (win + 1) * length)
            queries = q_ref[here, :] * jnp.bfloat16(0.125)
            key_rows = k_ref[here, :]
            outer = g_ref[here, :]
            probs = probs_ref[head, win]
            grad_probs = lax.dot_general(v_ref[here, :] * low, outer, NT, preferred_element_type=jnp.float32)
            wide = probs.astype(jnp.float32)
            inner = jnp.sum(wide * grad_probs, axis=0, keepdims=True)
            grad_scores = (wide * (grad_probs - inner)).astype(jnp.bfloat16)
            if win == 0:
                total[:, :length] = grad_scores.astype(jnp.float32)
            else:
                total[:, :length] = total[:, :length] + grad_scores.astype(jnp.float32)
            part = jnp.dot((key_rows * low).T, grad_scores, preferred_element_type=jnp.float32)
            if head == 0:
                query_grads[win] = part
            else:
                column = pl.multiple_of(step * 128, 128)
                both = (query_grads[win] + part) * 0.125
                out_ref[here, pl.ds(column, 128)] = both.T.astype(jnp.bfloat16)
            new = (
                None,
                jnp.dot(grad_scores, queries, preferred_element_type=jnp.float32),
                jnp.dot(probs, outer, preferred_element_type=jnp.float32),
            )
            for kind in range(1, 3):
                column = pl.multiple_of(step * 128 + kind * width, 128)
                if head == 0:
                    out_ref[here, pl.ds(column, 128)] = (new[kind] * chosen).astype(jnp.bfloat16)
                else:
                    out_ref[here, pl.ds(column, 128)] = out_ref[here, pl.ds(column, 128)] + (
                        new[kind] * chosen
                    ).astype(jnp.bfloat16)
        strip = total[:rows, :] if blocks == 1 else pltpu.roll(total[:rows, :], (blocks - 1) * rows, 1)
        for block in range(1, blocks):
            offset = (blocks - 1 - block) * rows
            piece = total[block * rows : (block + 1) * rows, :]
            strip = strip + (piece if offset == 0 else pltpu.roll(piece, offset, 1))
        if rows > WS:
            strip = split_rows(strip)
        skew(strip, strip_ref, head)


def split_rows(strip):
    lane = lax.broadcasted_iota(jnp.int32, (1, 128), 1)
    groups = []
    for offset in range(2 * FR - 1):
        odd = offset % 2
        there = slice(offset // 2 * 128, offset // 2 * 128 + 128)
        summed = None
        for row in range(HS):
            piece = jnp.where(lane // 64 == odd, strip[row * HS : (row + 1) * HS, there], 0.0)
            shift = (64 * odd + (HS - 1 - row) * HS) % 128
            piece = piece if shift == 0 else pltpu.roll(piece, shift, 1)
            summed = piece if summed is None else summed + piece
        groups.append(summed)
    return jnp.concatenate(groups, axis=1)


def skew(strip, out_ref, head):
    columns, lanes = strip.shape
    lane = lax.broadcasted_iota(jnp.int32, (1, lanes), 1)
    for odd in range(2):
        part = jnp.where(lane // columns % 2 == odd, strip, 0.0)
        if odd:
            part = pltpu.roll(part, lanes - columns, 1)
        summed = part[columns - 1 :, :]
        for column in range(columns - 1):
            summed = summed + pltpu.roll(part[column : column + 1, :], columns - 1 - column, 1)
        out_ref[head, odd : odd + 1, :] = summed


def attend_back(qkv, probs, grad_out, wins, length, rows, lanes, strip):
    count, triple = qkv.shape
    return pl.pallas_call(
        partial(attend_back_kernel, wins=wins, length=length, rows=rows),
        grid=(HEADS // 2,),
        out_shape=[
            jax.ShapeDtypeStruct((count, triple), jnp.bfloat16),
            jax.ShapeDtypeStruct((HEADS,) + strip, jnp.float32),
        ],
        in_specs=[
            pl.BlockSpec((count, 128), lambda h: (0, h)),
            pl.BlockSpec((count, 128), lambda h: (0, HEADS // 2 + h)),
            pl.BlockSpec((count, 128), lambda h: (0, HEADS + h)),
            pl.BlockSpec((count, 128), lambda h: (0, h)),
            pl.BlockSpec((2, wins, length, length), lambda h: (h, 0, 0, 0)),
        ],
        out_specs=[
            pl.BlockSpec((count, triple), lambda h: (0, 0)),
            pl.BlockSpec((2,) + strip, lambda h: (h, 0, 0)),
        ],
        scratch_shapes=[pltpu.VMEM((length, lanes), jnp.float32)],
        compiler_params=pltpu.CompilerParams(vmem_limit_bytes=56 * MIB),
        cost_estimate=SMALL,
        name="attend_back",
    )(qkv, qkv, qkv, grad_out, probs)


def plain_norm(values):
    center = values - jnp.mean(values, axis=-1, keepdims=True)
    spread = jnp.mean(center * center, axis=-1, keepdims=True)
    scale = lax.rsqrt(spread + epsilon)
    return center * scale, scale


def modulated_norm(values, shift_vec, scale_vec):
    return (plain_norm(values)[0] * (1.0 + scale_vec) + shift_vec).astype(jnp.bfloat16)


def row_call(kernel, wide, vectors, kept, sums, name):
    count, width = wide[0].shape
    block = pl.BlockSpec((count // 2, width), lambda i: (i, 0))
    whole = pl.BlockSpec((1, width), lambda i: (0, 0))
    out_shape = [jax.ShapeDtypeStruct((count, width), kind) for kind in kept]
    out_specs = [block] * len(kept)
    if sums:
        out_shape.append(jax.ShapeDtypeStruct((8, width), jnp.float32))
        out_specs.append(pl.BlockSpec((8, width), lambda i: (0, 0)))
    return pl.pallas_call(
        kernel,
        grid=(2,),
        out_shape=out_shape,
        in_specs=[block] * len(wide) + [whole] * len(vectors),
        out_specs=out_specs,
        compiler_params=pltpu.CompilerParams(vmem_limit_bytes=56 * MIB),
        cost_estimate=SMALL,
        name=name,
    )(*wide, *[vector.reshape(1, width) for vector in vectors])


def residual_kernel(rows, branch, gate, shift, scale, out, unit):
    values = rows[...] + gate[...] * branch[...]
    out[...] = values
    unit[...] = modulated_norm(values, shift[...], scale[...])


def add_branch(rows, branch, gate, shift, scale):
    kept = (jnp.float32, jnp.bfloat16)
    return row_call(residual_kernel, [rows, branch], [gate, shift, scale], kept, False, "add_branch")


def norm_back_kernel(grad_in, values, grad_rows, *refs):
    if len(refs) == 6:
        branch, scale, gate, out, gated, sums = refs
    else:
        scale, out, sums = refs
    unit, rate = plain_norm(values[...])
    grads = grad_in[...]
    inner = grads * (1.0 + scale[...])
    mean_one = jnp.mean(inner, axis=-1, keepdims=True)
    mean_two = jnp.mean(inner * unit, axis=-1, keepdims=True)
    total = grad_rows[...] + rate * (inner - mean_one - unit * mean_two)
    out[...] = total

    @pl.when(pl.program_id(0) == 0)
    def clear():
        sums[...] = jnp.zeros_like(sums)

    sums[0:1, :] += jnp.sum(grads, axis=0, keepdims=True)
    sums[1:2, :] += jnp.sum(grads * unit, axis=0, keepdims=True)
    if len(refs) == 6:
        gated[...] = (gate[...] * total).astype(jnp.bfloat16)
        sums[2:3, :] += jnp.sum(total * branch[...], axis=0, keepdims=True)


def norm_back(grad_in, values, grad_rows, scale, branch=None, gate=None):
    if branch is None:
        kept = (jnp.float32,)
        return row_call(norm_back_kernel, [grad_in, values, grad_rows], [scale], kept, True, "norm_back")
    kept = (jnp.float32, jnp.bfloat16)
    wide = [grad_in, values, grad_rows, branch]
    return row_call(norm_back_kernel, wide, [scale, gate], kept, True, "norm_back")


def gelu_both(upward):
    half = 0.5 * (1.0 + lax.erf(upward * 0.7071067811865476))
    density = 0.3989422804014327 * jnp.exp(-0.5 * upward * upward)
    return (upward * half).astype(jnp.bfloat16), (half + upward * density).astype(jnp.bfloat16)


def joint_group(rows):
    split = rows.reshape(FR * HS, 2, HS, rows.shape[-1])
    return split.transpose(1, 0, 2, 3).reshape(rows.shape)


def joint_ungroup(rows):
    split = rows.reshape(2, FR * HS, HS, rows.shape[-1])
    return split.transpose(1, 0, 2, 3).reshape(rows.shape)


def window_group(flat_rows):
    return flat_rows.reshape(SLOTS, WS * WS, flat_rows.shape[-1])


def split_halves(half_rows, own_half):
    pair_windows = half_rows.shape[0]
    filler = jnp.zeros((2 * SLOTS - pair_windows,) + half_rows.shape[1:], half_rows.dtype)
    padded = jnp.concatenate([half_rows, filler], axis=0)
    keep_part = lax.dynamic_slice_in_dim(padded, own_half * SLOTS, SLOTS, 0)
    send_part = lax.dynamic_slice_in_dim(padded, (1 - own_half) * SLOTS, SLOTS, 0)
    return (keep_part, send_part)


def join_windows(keep_part, came_part, own_half):
    upper_half = jnp.where(own_half == 0, keep_part, came_part)
    lower_half = jnp.where(own_half == 0, came_part, keep_part)
    joined = jnp.concatenate([upper_half, lower_half], axis=1)
    return joined.reshape(-1, joined.shape[-1])


def split_windows(win_rows, own_half):
    grouped = window_group(win_rows)
    half_len = grouped.shape[1] // 2
    upper_half = grouped[:, :half_len]
    lower_half = grouped[:, half_len:]
    keep_part = jnp.where(own_half == 0, upper_half, lower_half)
    send_part = jnp.where(own_half == 0, lower_half, upper_half)
    return (keep_part, send_part)


def join_halves(keep_part, came_part, own_half, pair_windows):
    leading = jnp.where(own_half == 0, keep_part, came_part)
    trailing = jnp.where(own_half == 0, came_part, keep_part)
    joined = jnp.concatenate([leading, trailing], axis=0)[:pair_windows]
    return joined.reshape(-1, joined.shape[-1])


def from_pair(value):
    pairs = [(i, i ^ 1) for i in range(lax.axis_size("win"))]
    return lax.ppermute(value, "win", pairs)


class Weights:
    def __init__(self, masters, place, quick):
        self.quick = quick
        low = [master.astype(jnp.bfloat16) for master in masters]
        self.place = place
        if quick:
            shards = []
            for block in range(2):
                qkv, out, up, down = low[4 * block : 4 * block + 4]
                shards += [jnp.concatenate([qkv, out], axis=1), up, down]
            self.widths = [(384, 128), (512,), (128,)] * 2
            halves = [shard.reshape(2, shard.shape[0] // 2, -1) for shard in shards]
            self.jobs = [Gather(value, 2 * value.shape[1], False) for value in halves[:2]] + [None] * 4
            self.later = [(units, jnp.stack([halves[unit] for unit in units], axis=1)) for units in ((2, 5), (3, 4))]
        else:
            self.full = [
                lax.all_gather(lax.all_gather(shard, "win", axis=1, tiled=True), "clip", axis=0, tiled=True)
                for shard in low
            ]
            self.full = [tuple(self.full[0:2]), (self.full[2],), (self.full[3],)] + [
                tuple(self.full[4:6]),
                (self.full[6],),
                (self.full[7],),
            ]

    def go(self, moves, state, after=()):
        if not self.quick:
            return state
        jobs = [(self.jobs[unit], move) for unit, move in moves]
        jobs = [(job, move) for job, move in jobs if not (job.early and move == "near")]
        known = [(job, job.needs(move)) for job, move in jobs if job.needs(move) in job.held]
        known += [(self.jobs[unit], name) for unit, name in after]
        held, state = lax.optimization_barrier(([job.held[name] for job, name in known], state))
        for (job, name), values in zip(known, held):
            job.held[name] = values
        for job, move in jobs:
            job.go(move)
        return state

    def begin(self, state):
        if not self.quick:
            return state
        state, held = lax.optimization_barrier((state, [value for units, value in self.later]))
        for (units, unused), (a0, b0) in zip(self.later, held):
            a_came, b_came = hop(a0, "y"), hop(b0, "x")
            for place, unit in enumerate(units):
                near = [a0[place], a_came[place], b0[place], b_came[place]]
                halves = jnp.stack(near).reshape(2, 2, *near[0].shape)
                self.jobs[unit] = Gather(halves, 2 * near[0].shape[0], True)
        return state

    def apply(self, unit, x, kind):
        if self.quick:
            job = self.jobs[unit]
            return gathered(job.values(), self.place, x, job.rows, self.widths[unit], kind)
        wholes = self.full[unit]
        result = jnp.dot(x, wholes[0], preferred_element_type=jnp.float32)
        if kind == "gelu":
            return *gelu_both(result), *wholes
        return result if kind == "wide" else result.astype(jnp.bfloat16), *wholes


def body(
    tokens,
    grad_output,
    clip_height,
    clip_width,
    modulation,
    sp_qkv,
    sp_out,
    sp_up,
    sp_down,
    sp_table,
    st_qkv,
    st_out,
    st_up,
    st_down,
    st_table,
    quick,
):
    model_width = tokens.shape[-1]
    half_len = tokens.shape[-2]
    pair_windows = PAIR_LOCS * FR
    shard_index = lax.axis_index("win")
    clip_index = lax.axis_index("clip")
    pair_index = shard_index // 2
    own_half = shard_index % 2
    own_core = clip_index % 2
    own_x = clip_index // 2
    row_places = [
        (own_x ^ x_rel) * 2 + (own_core ^ c_rel) for c_rel in range(2) for x_rel in range(2)
    ]
    place = {
        "rows": jnp.stack(row_places).astype(jnp.int32),
        "cols": jnp.stack([own_half, own_half ^ 1]).astype(jnp.int32),
    }
    weights = Weights(
        (sp_qkv, sp_out, sp_up, sp_down, st_qkv, st_out, st_up, st_down), place, quick
    )
    mod = modulation[0]

    location = pair_index
    token_ids = jnp.arange(WS * WS, dtype=jnp.int32)
    row_pos = location // LOC_W * WS + token_ids // WS
    col_pos = location % LOC_W * WS + token_ids % WS
    sp_valid = (row_pos < clip_height[0]) & (col_pos < clip_width[0])
    sp_allowed = (sp_valid[None, :, None] | jnp.eye(WS * WS, dtype=bool)[None]).astype(jnp.float32)
    joint_len = FR * HS * HS
    joint_ids = jnp.arange(joint_len, dtype=jnp.int32)
    joint_row = location // LOC_W * WS + own_half * HS + joint_ids // HS % HS
    joint_col = location % LOC_W * WS + jnp.arange(2, dtype=jnp.int32)[:, None] * HS + joint_ids[None] % HS
    st_valid = (joint_row[None] < clip_height[0]) & (joint_col < clip_width[0])
    st_allowed = (st_valid[:, :, None] | jnp.eye(joint_len, dtype=bool)[None]).astype(jnp.float32)

    half_tokens = tokens.reshape(pair_windows, half_len, model_width)
    keep_part, send_part = split_halves(half_tokens, own_half)
    came_part = weights.begin(from_pair(send_part))
    came_part = weights.go([(0, "near")], came_part)
    win_input = join_windows(keep_part, came_part, own_half).astype(jnp.float32)
    attn_in_a = modulated_norm(win_input, mod[0], mod[1])

    go = weights.go
    state = (win_input, attn_in_a, sp_table)
    win_input, attn_in_a, sp_table = go([(0, "far"), (0, "core_near")], state)
    sp_strip = spatial_strip(sp_table)
    state = go([(1, "near")], (win_input, attn_in_a, sp_strip, sp_allowed))
    win_input, attn_in_a, sp_strip, sp_allowed = go([(0, "core_far")], state)
    qkv_a, w_qkv_a, w_out_a = weights.apply(0, attn_in_a, "narrow")
    win_input, qkv_a, w_out_a = go([(1, "far")], (win_input, qkv_a, w_out_a))
    win_input, qkv_a, w_out_a = go([(2, "near")], (win_input, qkv_a, w_out_a))
    attn_out_a, probs_a = attend(qkv_a, sp_strip, sp_allowed, SLOTS, WS * WS)
    win_input, attn_out_a, w_out_a = go([(1, "core_near")], (win_input, attn_out_a, w_out_a))
    mixed_a = product(attn_out_a, w_out_a)
    win_middle = win_input + mod[2] * mixed_a
    keep_part, send_part = split_windows(win_middle, own_half)
    send_part = send_part.astype(jnp.bfloat16)
    keep_part, send_part, st_table = go([(1, "core_far")], (keep_part, send_part, st_table))
    came_part = from_pair(send_part)
    keep_part, st_table = go([(2, "far"), (2, "core_near")], (keep_part, st_table))
    st_strip = joint_strip(st_table)
    keep_part, came_part, st_strip, st_allowed = lax.optimization_barrier(
        (keep_part, came_part, st_strip, st_allowed)
    )
    middle_a = joint_group(join_halves(keep_part, came_part.astype(jnp.float32), own_half, pair_windows))
    mlp_in_a = modulated_norm(middle_a, mod[3], mod[4])

    hidden_a, slope_a, w_up_a = weights.apply(1, mlp_in_a, "gelu")
    state = go([(2, "core_far")], (middle_a, hidden_a, slope_a))
    middle_a, hidden_a, slope_a = go([(3, "far")], state)
    downward_a, w_down_a = weights.apply(2, hidden_a, "wide")
    middle_a, downward_a = go([(3, "core_near")], (middle_a, downward_a))
    first_out, attn_in_b = add_branch(middle_a, downward_a, mod[5], mod[6], mod[7])

    first_out, attn_in_b = go([(3, "core_far")], (first_out, attn_in_b))
    first_out, attn_in_b = go([(4, "far")], (first_out, attn_in_b))
    qkv_b, w_qkv_b, w_out_b = weights.apply(3, attn_in_b, "narrow")
    first_out, qkv_b, w_out_b = go([(4, "core_near")], (first_out, qkv_b, w_out_b))
    attn_out_b, probs_b = attend(qkv_b, st_strip, st_allowed, 2, joint_len)
    first_out, attn_out_b, w_out_b = go([(4, "core_far")], (first_out, attn_out_b, w_out_b))
    first_out, attn_out_b, w_out_b = go([(5, "far")], (first_out, attn_out_b, w_out_b))
    mixed_b = product(attn_out_b, w_out_b)
    middle_b, mlp_in_b = add_branch(first_out, mixed_b, mod[8], mod[9], mod[10])
    hidden_b, slope_b, w_up_b = weights.apply(4, mlp_in_b, "gelu")
    middle_b, hidden_b, slope_b = go([(5, "core_near"), (5, "core_far")], (middle_b, hidden_b, slope_b))

    def start_grad(xs, dys, rows, widths, starts, sources, olders=()):
        if quick:
            return Scatter(xs, dys, place, rows, widths, starts, sources, olders)
        return Plain(xs, dys, widths, starts, sources)

    def rounds(jobs, state):
        if quick:
            return together(jobs, state)
        return state

    def hold(jobs, state):
        if not quick:
            return state
        state, held = lax.optimization_barrier((state, [job.values for job in jobs]))
        for job, values in zip(jobs, held):
            job.values = values
        return state

    def settle(jobs, state):
        state = hold(jobs, state)
        if quick:
            for job in jobs:
                job.fold()
        return state

    grad_out_b = joint_group(grad_output.reshape(-1, model_width)).astype(jnp.float32)
    grad_down_b = (mod[11] * grad_out_b).astype(jnp.bfloat16)
    d_st_down = start_grad([hidden_b], [grad_down_b], 1024, (128,), (0,), (0,))
    grad_down_b, hidden_b = rounds([d_st_down], (grad_down_b, hidden_b))
    downward_b, w_down_b = weights.apply(5, hidden_b, "wide")
    grad_up_b = product_scaled(grad_down_b, w_down_b, slope_b)
    d_st_up = start_grad([mlp_in_b], [grad_up_b], 256, (512,), (0,), (0,), [d_st_down])
    grad_up_b, downward_b = rounds([d_st_up, d_st_down], (grad_up_b, downward_b))
    out_rows = middle_b + mod[11] * downward_b
    out_tokens = joint_ungroup(out_rows).reshape(tokens.shape)
    grad_gate_mb = jnp.sum(grad_out_b * downward_b, axis=0)
    grad_mlp_b = product_turned(grad_up_b, w_up_b)
    grad_middle_b, grad_mixed_b, sums_mb = norm_back(
        grad_mlp_b, middle_b, grad_out_b, mod[10], mixed_b, mod[8]
    )
    state = (grad_middle_b, grad_mixed_b)
    state = settle([d_st_up, d_st_down], state)
    grad_middle_b, grad_mixed_b = rounds([d_st_up, d_st_down], state)
    grad_attn_b = product_turned(grad_mixed_b, w_out_b, jnp.bfloat16)
    grad_qkv_b, strip_grad_b = attend_back(
        qkv_b, probs_b, grad_attn_b, 2, joint_len, *st_strip.shape[1:], (2, 128 * (2 * FR - 1))
    )
    grad_middle_b, grad_qkv_b, strip_grad_b, grad_gate_mb = hold(
        [d_st_down], (grad_middle_b, grad_qkv_b, strip_grad_b, grad_gate_mb)
    )
    d_st_attn = start_grad(
        [attn_in_b, attn_out_b],
        [grad_qkv_b, grad_qkv_b, grad_mixed_b],
        256,
        (256, 128, 128),
        (0, 8, 0),
        (0, 0, 1),
        [d_st_down],
    )
    state = hold([d_st_attn], (grad_middle_b, grad_qkv_b, strip_grad_b))
    state = settle([d_st_up], state)
    grad_middle_b, grad_qkv_b, strip_grad_b = rounds([d_st_attn, d_st_up, d_st_down], state)
    grad_in_b = product_turned(grad_qkv_b, w_qkv_b)
    grad_first, grad_down_a, sums_ab = norm_back(
        grad_in_b, first_out, grad_middle_b, mod[7], downward_a, mod[5]
    )
    grad_first, grad_down_a = hold([d_st_attn, d_st_up], (grad_first, grad_down_a))
    d_sp_down = start_grad(
        [hidden_a], [grad_down_a], 1024, (128,), (0,), (0,), [d_st_attn, d_st_up]
    )
    grad_first, grad_down_a = rounds([d_sp_down, d_st_attn, d_st_up], (grad_first, grad_down_a))
    grad_up_a = product_scaled(grad_down_a, w_down_a, slope_a)
    grad_first, grad_up_a = hold([d_sp_down], (grad_first, grad_up_a))
    d_sp_up = start_grad([mlp_in_a], [grad_up_a], 256, (512,), (0,), (0,), [d_sp_down])
    grad_first, grad_up_a = hold([d_sp_up], (grad_first, grad_up_a))
    grad_first, grad_up_a = settle([d_st_attn], (grad_first, grad_up_a))
    grad_first, grad_up_a = hold([d_sp_up], (grad_first, grad_up_a))
    grad_first, grad_up_a = rounds([d_sp_up, d_st_attn], (grad_first, grad_up_a))
    grad_mlp_a = product_turned(grad_up_a, w_up_a)
    grad_middle_a, sums_ma = norm_back(grad_mlp_a, middle_a, grad_first, mod[4])
    grad_middle_a = joint_ungroup(grad_middle_a)
    half_rows = grad_middle_a.reshape(pair_windows, -1, model_width)
    keep_part, send_part = split_halves(half_rows, own_half)
    send_part = send_part.astype(jnp.bfloat16)
    keep_part, send_part = hold([d_sp_up, d_st_attn], (keep_part, send_part))
    came_part = from_pair(send_part)
    keep_part = rounds([d_sp_down], keep_part)
    if quick:
        d_st_attn.fold()
        d_sp_up.fold()
    keep_part, came_part = rounds([d_st_attn], (keep_part, came_part))
    grad_win = join_windows(keep_part, came_part.astype(jnp.float32), own_half)
    grad_mixed_a = (mod[2] * grad_win).astype(jnp.bfloat16)
    grad_gate_aa = jnp.sum(grad_win * mixed_a, axis=0)
    grad_win, grad_mixed_a = rounds([d_sp_up], (grad_win, grad_mixed_a))
    grad_attn_a = product_turned(grad_mixed_a, w_out_a, jnp.bfloat16)
    grad_qkv_a, strip_grad_a = attend_back(
        qkv_a, probs_a, grad_attn_a, SLOTS, WS * WS, *sp_strip.shape[1:], (2, 2 * WS * WS)
    )
    grad_win, grad_qkv_a, strip_grad_a = settle([d_sp_down], (grad_win, grad_qkv_a, strip_grad_a))
    grad_win, grad_qkv_a, strip_grad_a = hold([d_st_attn], (grad_win, grad_qkv_a, strip_grad_a))
    grad_win, grad_qkv_a, strip_grad_a = rounds([d_sp_down], (grad_win, grad_qkv_a, strip_grad_a))
    d_sp_attn = start_grad(
        [attn_in_a, attn_out_a], [grad_qkv_a, grad_mixed_a], 256, (384, 128), (0, 0), (0, 1)
    )
    state = hold([d_sp_attn, d_sp_up, d_sp_down], (grad_win, grad_qkv_a, strip_grad_a, strip_grad_b))
    if quick:
        d_sp_up.fold()
        d_sp_down.fold()
    grad_win, grad_qkv_a, strip_grad_a, strip_grad_b = state
    tables = jnp.concatenate([strip_grad_a, strip_grad_b], axis=2)
    table_total = Total(tables, ("core", "z1", "z0", "y", "x"))
    state = (grad_win, grad_qkv_a)
    state = rounds([d_sp_attn, d_sp_up, d_sp_down, table_total], state)
    state = settle([d_sp_attn, d_sp_up], state)
    grad_win, grad_qkv_a = rounds([d_sp_attn, d_sp_up, table_total], state)
    grad_in_a = product_turned(grad_qkv_a, w_qkv_a)
    win_sum, sums_aa = norm_back(grad_in_a, win_input, grad_win, mod[1])
    win_sum, sums_aa = settle([d_sp_attn], (win_sum, sums_aa))
    mod_rows = [
        sums_aa[0],
        sums_aa[1],
        grad_gate_aa,
        sums_ma[0],
        sums_ma[1],
        sums_ab[2],
        sums_ab[0],
        sums_ab[1],
        sums_mb[2],
        sums_mb[0],
        sums_mb[1],
        grad_gate_mb,
    ]
    mod_total = Total(jnp.stack(mod_rows, axis=0), ("z1", "z0", "y"))
    win_sum = rounds([d_sp_attn, table_total], win_sum)
    keep_part, send_part = split_windows(win_sum, own_half)
    send_part = send_part.astype(jnp.bfloat16)
    keep_part, send_part = settle([d_sp_attn], (keep_part, send_part))
    keep_part, send_part = rounds([d_sp_attn, table_total, mod_total], (keep_part, send_part))
    came_part = from_pair(send_part)
    rounds([table_total, mod_total], ())
    rounds([mod_total], ())
    came_part = came_part.astype(jnp.float32)
    grad_tokens = join_halves(keep_part, came_part, own_half, pair_windows).reshape(tokens.shape)
    if quick:
        grad_modulation = mod_total.result()[None]
        table_sums = table_total.result()
    else:
        grad_modulation = lax.psum(jnp.stack(mod_rows, axis=0), "win")[None]
        table_sums = lax.psum(table_total.result(), ("clip", "win"))
    grad_sp_table = spatial_strip_back(table_sums[:, :, : 2 * WS * WS])
    grad_st_table = joint_strip_back(table_sums[:, :, 2 * WS * WS :])
    wide = d_st_attn.values
    wide_a = d_sp_attn.values
    out_width = wide.shape[1] // 4
    return (
        out_tokens,
        grad_tokens,
        grad_modulation,
        wide_a[:, : 3 * out_width],
        wide_a[:, 3 * out_width :],
        d_sp_up.values,
        d_sp_down.values,
        grad_sp_table,
        wide[:, : 2 * out_width],
        wide[:, 2 * out_width : 3 * out_width],
        wide[:, 3 * out_width :],
        d_st_up.values,
        d_st_down.values,
        grad_st_table,
    )


class Plain:
    def __init__(self, xs, dys, widths, starts, sources):
        grads = []
        for dy, width, start, source in zip(dys, widths, starts, sources):
            x = xs[source]
            part = dy[:, start * 2 * width : start * 2 * width + 8 * width]
            full = lax.dot_general(x, part, TN, preferred_element_type=jnp.float32)
            full = lax.psum_scatter(
                full.astype(jnp.bfloat16), "clip", scatter_dimension=0, tiled=True
            )
            grads.append(lax.psum_scatter(full, "win", scatter_dimension=1, tiled=True))
        self.values = jnp.concatenate(grads, axis=1).astype(jnp.float32)


def solution(mesh):
    grid = P("clip", "win")
    whole = P("clip", "win", None, None, None, None)
    in_specs = (whole, whole, P("clip"), P("clip"), P("clip", None, None)) + ((grid,) * 4 + (P(),)) * 2
    out_specs = (whole, whole, P("clip", None, None)) + (grid,) * 4 + (P(),) + (grid,) * 5 + (P(),)
    quick = mesh.shape["clip"] == 4 and mesh.shape["win"] == 8
    return jax.shard_map(
        partial(body, quick=quick), mesh=mesh, in_specs=in_specs, out_specs=out_specs, check_vma=False
    )
```

```python
from functools import partial
from typing import NamedTuple

import jax
import jax.numpy as jnp
import numpy as np
from jax import lax
from jax.experimental import pallas as pl
from jax.experimental.pallas import tpu as pltpu
from jax.sharding import PartitionSpec as P

HEADS = 16
WS = 16
FR = 5
LOC_W = 4
PAIR_LOCS = 1
HS = 8
SLOTS = 3
MIB = 1024 * 1024

SMALL = pl.CostEstimate(flops=1, bytes_accessed=1, transcendentals=0)

epsilon = 1e-06
masked_score = -1000000000.0
highest = lax.Precision.HIGHEST
NT = (((1,), (1,)), ((), ()))
TN = (((0,), (0,)), ((), ()))


BITS = {"core": ("clip", 1), "x": ("clip", 2), "y": ("win", 1), "z0": ("win", 2), "z1": ("win", 4)}


def hop(value, link):
    axis, mask = BITS[link]
    return lax.ppermute(value, axis, [(i, i ^ mask) for i in range(lax.axis_size(axis))])


def z_groups():
    size = lax.axis_size("win")
    return [list(range(start, size, 2)) for start in range(2)]


class Gather:
    def __init__(self, halves, rows, early):
        self.rows = rows
        self.early = early
        axis = halves.ndim - 2
        grown = lax.all_gather(halves, "win", axis=axis, tiled=False, axis_index_groups=z_groups())
        self.held = {"grown": (grown,)}

    def needs(self, move):
        if move == "far" and self.early:
            return "grown"
        return {"near": "grown", "far": "near", "core_near": "own", "core_far": "away"}[move]

    def go(self, move):
        values = self.held[self.needs(move)]
        if move == "near":
            (grown,) = values
            a0, b0 = grown[0], grown[1]
            self.held["near"] = (a0, hop(a0, "y"), b0, hop(b0, "x"))
        elif move == "far":
            if self.early:
                a1, b1 = values[0][0], values[0][1]
            else:
                a0, a_came, b0, b_came = values
                a1, b1 = jnp.stack([a0, a_came]), jnp.stack([b0, b_came])
            self.held["own"] = (a1, b1)
            self.held["away"] = (hop(a1, "x"), hop(b1, "y"))
        else:
            self.held[move] = tuple(hop(value, "core") for value in values)

    def values(self):
        pairs = [self.held[name] for name in ("own", "away", "core_near", "core_far")]
        return [pair[0] for pair in pairs] + [pair[1] for pair in pairs]


def gathered_kernel(row_of, y_of, x_ref, *refs, rows, widths, kind):
    count = len(widths)
    results = 2 if kind == "gelu" else 1
    pieces, refs = refs[:8], refs[8:]
    outs, wholes, held = refs[:results], refs[results : results + count], refs[results + count : -2]
    in_sems, out_sems = refs[-2:]
    half = rows // 2
    step = pl.program_id(0)

    def arrivals(z):
        copies = []
        for part in range(2):
            for c_rel in range(2):
                for x_rel in range(2):
                    row = row_of[c_rel * 2 + x_rel] * rows + part * half
                    row = pl.multiple_of(row, half)
                    for y_rel in range(2):
                        far, near = (x_rel, y_rel) if part == 0 else (y_rel, x_rel)
                        source = pieces[part * 4 + c_rel * 2 + far]
                        start = 0
                        for matrix, width in zip(held, widths):
                            col = pl.multiple_of((z * 2 + y_of[y_rel]) * width, 128)
                            copies.append(
                                pltpu.make_async_copy(
                                    source.at[near, z, :, pl.ds(start, width)],
                                    matrix.at[pl.ds(row, half), pl.ds(col, width)],
                                    in_sems.at[z * 16 * count + len(copies)],
                                )
                            )
                            start += width
        return copies

    def departures(z):
        copies = []
        for which, width in enumerate(widths):
            there = pl.ds(pl.multiple_of(z * 2 * width, 128), 2 * width)
            copies.append(
                pltpu.make_async_copy(
                    held[which].at[:, there], wholes[which].at[:, there], out_sems.at[z * count + which]
                )
            )
        return copies

    @pl.when(step == 0)
    def begin():
        for z in range(4):
            for copy in arrivals(z):
                copy.start()

    for copy in arrivals(step):
        copy.wait()
    for copy in departures(step):
        copy.start()
    wide = 2 * widths[0]
    chunk = 256 if kind == "gelu" else wide
    for first in range(0, wide, chunk):
        col = pl.multiple_of(step * wide + first, 128)
        there = slice(first, first + chunk)
        result = jnp.dot(
            x_ref[...], held[0][:, pl.ds(col, chunk)], preferred_element_type=jnp.float32
        )
        if kind == "gelu":
            outs[0][:, there], outs[1][:, there] = gelu_both(result)
        else:
            outs[0][:, there] = result.astype(outs[0].dtype)

    @pl.when(step == 3)
    def end():
        for z in range(4):
            for copy in departures(z):
                copy.wait()


def gathered(values, place, x, rows, widths, kind):
    shapes = [(4 * rows, 8 * width) for width in widths]
    results = 2 if kind == "gelu" else 1
    kept = jnp.float32 if kind == "wide" else jnp.bfloat16
    count = x.shape[0]
    return pl.pallas_call(
        partial(gathered_kernel, rows=rows, widths=widths, kind=kind),
        grid=(4,),
        out_shape=[jax.ShapeDtypeStruct((count, 8 * widths[0]), kept)] * results
        + [jax.ShapeDtypeStruct(shape, jnp.bfloat16) for shape in shapes],
        in_specs=[pl.BlockSpec(memory_space=pltpu.SMEM)] * 2
        + [pl.BlockSpec(x.shape, lambda z: (0, 0))]
        + [pl.BlockSpec(memory_space=pl.ANY)] * 8,
        out_specs=[pl.BlockSpec((count, 2 * widths[0]), lambda z: (0, z))] * results
        + [pl.BlockSpec(memory_space=pl.ANY)] * len(widths),
        scratch_shapes=[pltpu.VMEM(shape, jnp.bfloat16) for shape in shapes]
        + [pltpu.SemaphoreType.DMA((64 * len(widths),)), pltpu.SemaphoreType.DMA((4 * len(widths),))],
        compiler_params=pltpu.CompilerParams(vmem_limit_bytes=56 * MIB),
        cost_estimate=SMALL,
        name="gathered",
    )(place["rows"], place["cols"], x, *values)


def product_kernel(left, right, out, *, turned):
    if turned:
        result = lax.dot_general(left[...], right[...], NT, preferred_element_type=jnp.float32)
    else:
        result = jnp.dot(left[...], right[...], preferred_element_type=jnp.float32)
    out[...] = result.astype(out.dtype)


def scaled_kernel(left, right, factor, out):
    result = lax.dot_general(left[...], right[...], NT, preferred_element_type=jnp.float32)
    out[...] = (result * factor[...].astype(jnp.float32)).astype(out.dtype)


def tiled(kernel, left, right, columns, kept, turned, *factors):
    count = left.shape[0]
    total = right.shape[0] if turned else right.shape[1]
    block = pl.BlockSpec((count, columns), lambda i: (0, i))
    if turned:
        right_spec = pl.BlockSpec((columns, right.shape[1]), lambda i: (i, 0))
    else:
        right_spec = pl.BlockSpec((right.shape[0], columns), lambda i: (0, i))
    return pl.pallas_call(
        kernel,
        grid=(total // columns,),
        out_shape=jax.ShapeDtypeStruct((count, total), kept),
        in_specs=[pl.BlockSpec(left.shape, lambda i: (0, 0)), right_spec] + [block] * len(factors),
        out_specs=block,
        compiler_params=pltpu.CompilerParams(vmem_limit_bytes=56 * MIB),
        cost_estimate=SMALL,
        name="product",
    )(left, right, *factors)


def product(left, right):
    return tiled(partial(product_kernel, turned=False), left, right, 512, jnp.float32, False)


def product_turned(left, right, kept=jnp.float32):
    columns = 512 if right.shape[1] == 1024 else 256
    return tiled(partial(product_kernel, turned=True), left, right, columns, kept, True)


def product_scaled(left, right, factor):
    return tiled(scaled_kernel, left, right, 1024, jnp.bfloat16, True, factor)


def grad_kernel(row_of, y_of, *refs, rows, widths, sources, kinds):
    count = len(widths)
    lefts = max(sources) + 1
    refs = list(refs)
    x_refs = [refs.pop(0) for _ in range(lefts)]
    dy_refs = [refs.pop(0) for _ in range(count)]
    old_refs = [[refs.pop(0) for _ in range(FOLDS[kind].takes)] for kind in kinds]
    send, keep = refs.pop(0), refs.pop(0)
    new_refs = [[refs.pop(0) for _ in range(FOLDS[kind].gives)] for kind in kinds]
    turns = refs
    half = rows // 2

    @pl.when(pl.program_id(0) == 0)
    def turn():
        for x_ref, turned in zip(x_refs, turns):
            for place in range(4):
                start = pl.multiple_of(row_of[place] * rows, 128)
                turned[place * rows : (place + 1) * rows, :] = x_ref[:, pl.ds(start, rows)].T

    offset = 0
    for dy_ref, width, source in zip(dy_refs, widths, sources):
        turned = turns[source]
        sides = [
            dy_ref[:, pl.ds(pl.multiple_of(y_of[y_rel] * width, 128), width)] for y_rel in range(2)
        ]
        product = jnp.dot(
            turned[...], jnp.concatenate(sides, axis=1), preferred_element_type=jnp.float32
        ).astype(jnp.bfloat16)
        for c_rel, out in ((0, keep), (1, send)):
            for x_rel in range(2):
                for ab in range(2):
                    first = (c_rel * 2 + x_rel) * rows + ab * half
                    for y_rel in range(2):
                        out[ab, x_rel, y_rel, 0, :, offset : offset + width] = product[
                            first : first + half, y_rel * width : (y_rel + 1) * width
                        ]
        offset += width
    for kind, old, new in zip(kinds, old_refs, new_refs):
        FOLDS[kind].kernel(*old, *new)


def fold_first(old_keep, old_came, a_send, a_keep, b_send, b_keep):
    for near in range(2):
        a_send[near] = old_keep[0, 1, near] + old_came[0, 1, near]
        a_keep[near] = old_keep[0, 0, near] + old_came[0, 0, near]
        b_send[near] = old_keep[1, near, 1] + old_came[1, near, 1]
        b_keep[near] = old_keep[1, near, 0] + old_came[1, near, 0]


def fold_second(a_keep, a_came, b_keep, b_came, a_out, a_held, b_out, b_held):
    a_out[...] = a_keep[1] + a_came[1]
    a_held[...] = a_keep[0] + a_came[0]
    b_out[...] = b_keep[1] + b_came[1]
    b_held[...] = b_keep[0] + b_came[0]


def fold_third(a_keep, a_came, b_keep, b_came, both):
    both[:, 0] = a_keep[...] + a_came[...]
    both[:, 1] = b_keep[...] + b_came[...]


class Part(NamedTuple):
    lead: tuple

    def shape(self, tail):
        return jax.ShapeDtypeStruct(self.lead + tail, jnp.bfloat16)

    def spec(self, tail):
        where = self.lead.index(4)
        block = tuple(1 if dim == where else size for dim, size in enumerate(self.lead))
        return pl.BlockSpec(
            block + tail, lambda z: (0,) * where + (z,) + (0,) * (len(block) + 1 - where)
        )


WHOLE, QUARTER, EIGHTH, TURNED = Part((2, 2, 2, 4)), Part((2, 4)), Part((4,)), Part((4, 2))


class Fold(NamedTuple):
    kernel: object
    takes: int
    takes_part: Part
    gives: int
    gives_part: Part


FOLDS = {
    1: Fold(fold_first, 2, WHOLE, 4, QUARTER),
    2: Fold(fold_second, 4, QUARTER, 4, EIGHTH),
    3: Fold(fold_third, 4, EIGHTH, 1, TURNED),
}


def weight_grad(xs, dys, place, rows, widths, starts, sources, olders):
    count = xs[0].shape[0]
    tail = (rows // 2, sum(widths))
    kinds = tuple(older.stage for older in olders)
    out_shape, out_specs = [WHOLE.shape(tail)] * 2, [WHOLE.spec(tail)] * 2
    old_specs, old_values = [], []
    for older, kind in zip(olders, kinds):
        fold = FOLDS[kind]
        old_tail = older.values[0].shape[-2:]
        old_specs += [fold.takes_part.spec(old_tail)] * fold.takes
        old_values += older.values
        out_shape += [fold.gives_part.shape(old_tail)] * fold.gives
        out_specs += [fold.gives_part.spec(old_tail)] * fold.gives
    outs = pl.pallas_call(
        partial(grad_kernel, rows=rows, widths=widths, sources=sources, kinds=kinds),
        grid=(4,),
        out_shape=out_shape,
        in_specs=[pl.BlockSpec(memory_space=pltpu.SMEM)] * 2
        + [pl.BlockSpec((count, 4 * rows), lambda z: (0, 0))] * len(xs)
        + [
            pl.BlockSpec((count, 2 * width), lambda z, s=start: (0, s + z))
            for width, start in zip(widths, starts)
        ]
        + old_specs,
        out_specs=out_specs,
        scratch_shapes=[pltpu.VMEM((4 * rows, count), jnp.bfloat16)] * len(xs),
        compiler_params=pltpu.CompilerParams(vmem_limit_bytes=56 * MIB),
        cost_estimate=SMALL,
        name="weight_grad",
    )(place["rows"], place["cols"], *xs, *dys, *old_values)
    outs = list(outs)
    values = tuple(outs.pop(0) for _ in range(2))
    for older, kind in zip(olders, kinds):
        older.values = tuple(outs.pop(0) for _ in range(FOLDS[kind].gives))
    return values


class Scatter:
    def __init__(self, xs, dys, place, rows, widths, starts, sources, olders):
        self.values = weight_grad(xs, dys, place, rows, widths, starts, sources, olders)
        self.stage = 0

    def fold(self):
        fold = FOLDS[self.stage]
        outs = pl.pallas_call(
            fold.kernel,
            out_shape=[fold.gives_part.shape(self.values[0].shape[-2:])] * fold.gives,
            compiler_params=pltpu.CompilerParams(vmem_limit_bytes=16 * MIB),
            cost_estimate=SMALL,
            name=fold.kernel.__name__,
        )(*self.values)
        self.values = tuple(outs)

    def advance(self, values):
        if self.stage == 0:
            send, keep = values
            new = (keep, hop(send, "core"))
        elif self.stage == 1:
            a_send, a_keep, b_send, b_keep = values
            new = (a_keep, hop(a_send, "x"), b_keep, hop(b_send, "y"))
        elif self.stage == 2:
            a_send, a_keep, b_send, b_keep = values
            new = (a_keep, hop(a_send, "y"), b_keep, hop(b_send, "x"))
        else:
            mine = lax.psum_scatter(
                values[0].reshape(-1, values[0].shape[-1]),
                "win",
                scatter_dimension=0,
                tiled=True,
                axis_index_groups=z_groups(),
            )
            new = mine.astype(jnp.float32)
        self.values = new
        self.stage += 1


class Total:
    def __init__(self, value, links):
        self.shape = value.shape
        self.size = value.size
        self.values = jnp.pad(value.reshape(-1), (0, -value.size % 1024)).reshape(-1, 128)
        self.links = list(links)

    def advance(self, values):
        self.values = values + hop(values, self.links.pop(0))

    def result(self):
        return self.values.reshape(-1)[: self.size].reshape(self.shape)


def together(jobs, state):
    held, state = lax.optimization_barrier(([job.values for job in jobs], state))
    for job, values in zip(jobs, held):
        job.advance(values)
    return state


def pair_table(extent):
    table_dims = (extent, extent, 2 * extent - 1)
    query_pos = lax.broadcasted_iota(jnp.int32, table_dims, 0)
    key_pos = lax.broadcasted_iota(jnp.int32, table_dims, 1)
    offset = lax.broadcasted_iota(jnp.int32, table_dims, 2)
    return (query_pos - key_pos + extent - 1 == offset).astype(jnp.float32)


def spatial_strip(table):
    side = 2 * WS - 1
    onehot = pair_table(WS).transpose(2, 1, 0).reshape(side, WS * WS)
    strip = jnp.dot(table.reshape(HEADS * side, side), onehot, precision=highest)
    strip = strip.reshape(HEADS, side, WS, WS).transpose(0, 2, 1, 3).reshape(HEADS, WS, side * WS)
    return jnp.pad(strip, ((0, 0), (0, 0), (0, WS)))


def spatial_strip_back(strip):
    side = 2 * WS - 1
    shaped = strip.reshape(HEADS, 2, WS, 2 * WS).transpose(0, 2, 1, 3)
    return shaped.reshape(HEADS, 2 * WS, 2 * WS)[:, :side, :side]


def joint_onehot():
    span = 2 * HS - 1
    place = np.arange(HS)
    apart = place[None, :] - place[:, None] + HS - 1
    wanted = apart[:, None, :, None] * span + apart[None, :, None, :]
    offset = np.arange(span * span)[:, None]
    return jnp.asarray((offset == wanted.reshape(1, -1)).astype(np.float32))


def joint_strip(table):
    frames = 2 * FR - 1
    places = HS * HS
    strip = jnp.dot(table.reshape(HEADS * frames, -1), joint_onehot(), precision=highest)
    strip = strip.reshape(HEADS, frames, places, places).transpose(0, 2, 1, 3)
    return jnp.pad(strip.reshape(HEADS, places, frames * places), ((0, 0), (0, 0), (0, places)))


def joint_strip_back(strip):
    span = 2 * HS - 1
    shaped = strip.reshape(HEADS, 2, 2 * FR - 1, HS, 2 * HS).transpose(0, 2, 3, 1, 4)
    return shaped.reshape(HEADS, 2 * FR - 1, 2 * HS, 2 * HS)[:, :, :span, :span]


def head_lanes(which):
    lane = lax.broadcasted_iota(jnp.int32, (1, 128), 1)
    return (lane // 64 == which).astype(jnp.float32)


def attend_kernel(q_ref, k_ref, v_ref, strip_ref, mask_ref, out_ref, probs_ref, bias, *, wins, length):
    rows, lanes = strip_ref.shape[1:]
    blocks = length // rows
    masks = mask_ref.shape[0]
    mixed = [None] * wins
    value_cols = [v_ref[win * length : (win + 1) * length, :].T for win in range(wins)]
    for head in range(2):
        strip = strip_ref[head]
        for block in range(blocks):
            offset = (blocks - 1 - block) * rows
            turned = strip if offset == 0 else pltpu.roll(strip, lanes - offset, 1)
            bias[block * rows : (block + 1) * rows, :] = turned[:, :length]
        low = head_lanes(head).astype(jnp.bfloat16)
        for win in range(wins):
            here = slice(win * length, (win + 1) * length)
            queries = q_ref[here, :] * jnp.bfloat16(0.125)
            scores = lax.dot_general(k_ref[here, :] * low, queries, NT, preferred_element_type=jnp.float32)
            scores = jnp.where(mask_ref[win % masks] > 0.0, scores + bias[...], masked_score)
            raised = jnp.exp(scores - jnp.max(scores, axis=0, keepdims=True))
            probs = raised * (1.0 / jnp.sum(raised, axis=0, keepdims=True))
            probs = probs.astype(jnp.bfloat16)
            probs_ref[head, win] = probs
            own = value_cols[win][head * 64 : (head + 1) * 64, :]
            part = jnp.dot(own, probs, preferred_element_type=jnp.float32)
            mixed[win] = part if head == 0 else jnp.concatenate([mixed[win], part], axis=0)
    for win in range(wins):
        out_ref[win * length : (win + 1) * length, :] = mixed[win].T.astype(jnp.bfloat16)


def attend(qkv, strip, allowed, wins, length):
    count, triple = qkv.shape
    width = triple // 3
    rows, lanes = strip.shape[1:]
    return pl.pallas_call(
        partial(attend_kernel, wins=wins, length=length),
        grid=(HEADS // 2,),
        out_shape=[
            jax.ShapeDtypeStruct((count, width), jnp.bfloat16),
            jax.ShapeDtypeStruct((HEADS, wins, length, length), jnp.bfloat16),
        ],
        in_specs=[
            pl.BlockSpec((count, 128), lambda h: (0, h)),
            pl.BlockSpec((count, 128), lambda h: (0, HEADS // 2 + h)),
            pl.BlockSpec((count, 128), lambda h: (0, HEADS + h)),
            pl.BlockSpec((2, rows, lanes), lambda h: (h, 0, 0)),
            pl.BlockSpec(allowed.shape, lambda h: (0, 0, 0)),
        ],
        out_specs=[
            pl.BlockSpec((count, 128), lambda h: (0, h)),
            pl.BlockSpec((2, wins, length, length), lambda h: (h, 0, 0, 0)),
        ],
        scratch_shapes=[pltpu.VMEM((length, length), jnp.float32)],
        compiler_params=pltpu.CompilerParams(vmem_limit_bytes=56 * MIB),
        cost_estimate=SMALL,
        name="attend",
    )(qkv, qkv, qkv, strip, allowed)


def attend_back_kernel(
    q_ref, k_ref, v_ref, g_ref, probs_ref, out_ref, strip_ref, total, *, wins, length, rows
):
    blocks = length // rows
    width = out_ref.shape[1] // 3
    step = pl.program_id(0)
    query_grads = [None] * wins
    key_cols = [k_ref[win * length : (win + 1) * length, :].T for win in range(wins)]
    total[...] = jnp.zeros_like(total)
    for head in range(2):
        chosen = head_lanes(head)
        low = chosen.astype(jnp.bfloat16)
        for win in range(wins):
            here = slice(win * length, (win + 1) * length)
            queries = q_ref[here, :] * jnp.bfloat16(0.125)
            outer = g_ref[here, :]
            probs = probs_ref[head, win]
            grad_probs = lax.dot_general(v_ref[here, :] * low, outer, NT, preferred_element_type=jnp.float32)
            wide = probs.astype(jnp.float32)
            inner = jnp.sum(wide * grad_probs, axis=0, keepdims=True)
            grad_scores = (wide * (grad_probs - inner)).astype(jnp.bfloat16)
            if win == 0:
                total[:, :length] = grad_scores.astype(jnp.float32)
            else:
                total[:, :length] = total[:, :length] + grad_scores.astype(jnp.float32)
            own = key_cols[win][head * 64 : (head + 1) * 64, :]
            part = jnp.dot(own, grad_scores, preferred_element_type=jnp.float32)
            if head == 0:
                query_grads[win] = part
            else:
                column = pl.multiple_of(step * 128, 128)
                both = jnp.concatenate([query_grads[win], part], axis=0) * 0.125
                out_ref[here, pl.ds(column, 128)] = both.T.astype(jnp.bfloat16)
            new = (
                None,
                jnp.dot(grad_scores, queries, preferred_element_type=jnp.float32),
                jnp.dot(probs, outer, preferred_element_type=jnp.float32),
            )
            for kind in range(1, 3):
                column = pl.multiple_of(step * 128 + kind * width, 128)
                if head == 0:
                    out_ref[here, pl.ds(column, 128)] = (new[kind] * chosen).astype(jnp.bfloat16)
                else:
                    out_ref[here, pl.ds(column, 128)] = out_ref[here, pl.ds(column, 128)] + (
                        new[kind] * chosen
                    ).astype(jnp.bfloat16)
        strip = total[:rows, :] if blocks == 1 else pltpu.roll(total[:rows, :], (blocks - 1) * rows, 1)
        for block in range(1, blocks):
            offset = (blocks - 1 - block) * rows
            piece = total[block * rows : (block + 1) * rows, :]
            strip = strip + (piece if offset == 0 else pltpu.roll(piece, offset, 1))
        if rows > WS:
            strip = split_rows(strip)
        skew(strip, strip_ref, head)


def split_rows(strip):
    lane = lax.broadcasted_iota(jnp.int32, (1, 128), 1)
    groups = []
    for offset in range(2 * FR - 1):
        odd = offset % 2
        there = slice(offset // 2 * 128, offset // 2 * 128 + 128)
        summed = None
        for row in range(HS):
            piece = jnp.where(lane // 64 == odd, strip[row * HS : (row + 1) * HS, there], 0.0)
            shift = (64 * odd + (HS - 1 - row) * HS) % 128
            piece = piece if shift == 0 else pltpu.roll(piece, shift, 1)
            summed = piece if summed is None else summed + piece
        groups.append(summed)
    return jnp.concatenate(groups, axis=1)


def skew(strip, out_ref, head):
    columns, lanes = strip.shape
    lane = lax.broadcasted_iota(jnp.int32, (1, lanes), 1)
    for odd in range(2):
        part = jnp.where(lane // columns % 2 == odd, strip, 0.0)
        if odd:
            part = pltpu.roll(part, lanes - columns, 1)
        summed = part[columns - 1 :, :]
        for column in range(columns - 1):
            summed = summed + pltpu.roll(part[column : column + 1, :], columns - 1 - column, 1)
        out_ref[head, odd : odd + 1, :] = summed


def attend_back(qkv, probs, grad_out, wins, length, rows, lanes, strip):
    count, triple = qkv.shape
    return pl.pallas_call(
        partial(attend_back_kernel, wins=wins, length=length, rows=rows),
        grid=(HEADS // 2,),
        out_shape=[
            jax.ShapeDtypeStruct((count, triple), jnp.bfloat16),
            jax.ShapeDtypeStruct((HEADS,) + strip, jnp.float32),
        ],
        in_specs=[
            pl.BlockSpec((count, 128), lambda h: (0, h)),
            pl.BlockSpec((count, 128), lambda h: (0, HEADS // 2 + h)),
            pl.BlockSpec((count, 128), lambda h: (0, HEADS + h)),
            pl.BlockSpec((count, 128), lambda h: (0, h)),
            pl.BlockSpec((2, wins, length, length), lambda h: (h, 0, 0, 0)),
        ],
        out_specs=[
            pl.BlockSpec((count, triple), lambda h: (0, 0)),
            pl.BlockSpec((2,) + strip, lambda h: (h, 0, 0)),
        ],
        scratch_shapes=[pltpu.VMEM((length, lanes), jnp.float32)],
        compiler_params=pltpu.CompilerParams(vmem_limit_bytes=56 * MIB),
        cost_estimate=SMALL,
        name="attend_back",
    )(qkv, qkv, qkv, grad_out, probs)


def plain_norm(values):
    center = values - jnp.mean(values, axis=-1, keepdims=True)
    spread = jnp.mean(center * center, axis=-1, keepdims=True)
    scale = lax.rsqrt(spread + epsilon)
    return center * scale, scale


def modulated_norm(values, shift_vec, scale_vec):
    return (plain_norm(values)[0] * (1.0 + scale_vec) + shift_vec).astype(jnp.bfloat16)


def row_call(kernel, wide, vectors, kept, sums, name):
    count, width = wide[0].shape
    block = pl.BlockSpec((count // 2, width), lambda i: (i, 0))
    whole = pl.BlockSpec((1, width), lambda i: (0, 0))
    out_shape = [jax.ShapeDtypeStruct((count, width), kind) for kind in kept]
    out_specs = [block] * len(kept)
    if sums:
        out_shape.append(jax.ShapeDtypeStruct((8, width), jnp.float32))
        out_specs.append(pl.BlockSpec((8, width), lambda i: (0, 0)))
    return pl.pallas_call(
        kernel,
        grid=(2,),
        out_shape=out_shape,
        in_specs=[block] * len(wide) + [whole] * len(vectors),
        out_specs=out_specs,
        compiler_params=pltpu.CompilerParams(vmem_limit_bytes=56 * MIB),
        cost_estimate=SMALL,
        name=name,
    )(*wide, *[vector.reshape(1, width) for vector in vectors])


def residual_kernel(rows, branch, gate, shift, scale, out, unit):
    values = rows[...] + gate[...] * branch[...]
    out[...] = values
    unit[...] = modulated_norm(values, shift[...], scale[...])


def add_branch(rows, branch, gate, shift, scale):
    kept = (jnp.float32, jnp.bfloat16)
    return row_call(residual_kernel, [rows, branch], [gate, shift, scale], kept, False, "add_branch")


def norm_back_kernel(grad_in, values, grad_rows, *refs):
    if len(refs) == 6:
        branch, scale, gate, out, gated, sums = refs
    else:
        scale, out, sums = refs
    unit, rate = plain_norm(values[...])
    grads = grad_in[...]
    inner = grads * (1.0 + scale[...])
    mean_one = jnp.mean(inner, axis=-1, keepdims=True)
    mean_two = jnp.mean(inner * unit, axis=-1, keepdims=True)
    total = grad_rows[...] + rate * (inner - mean_one - unit * mean_two)
    out[...] = total

    @pl.when(pl.program_id(0) == 0)
    def clear():
        sums[...] = jnp.zeros_like(sums)

    sums[0:1, :] += jnp.sum(grads, axis=0, keepdims=True)
    sums[1:2, :] += jnp.sum(grads * unit, axis=0, keepdims=True)
    if len(refs) == 6:
        gated[...] = (gate[...] * total).astype(jnp.bfloat16)
        sums[2:3, :] += jnp.sum(total * branch[...], axis=0, keepdims=True)


def norm_back(grad_in, values, grad_rows, scale, branch=None, gate=None):
    if branch is None:
        kept = (jnp.float32,)
        return row_call(norm_back_kernel, [grad_in, values, grad_rows], [scale], kept, True, "norm_back")
    kept = (jnp.float32, jnp.bfloat16)
    wide = [grad_in, values, grad_rows, branch]
    return row_call(norm_back_kernel, wide, [scale, gate], kept, True, "norm_back")


def gelu_both(upward):
    half = 0.5 * (1.0 + lax.erf(upward * 0.7071067811865476))
    density = 0.3989422804014327 * jnp.exp(-0.5 * upward * upward)
    return (upward * half).astype(jnp.bfloat16), (half + upward * density).astype(jnp.bfloat16)


def joint_group(rows):
    split = rows.reshape(FR * HS, 2, HS, rows.shape[-1])
    return split.transpose(1, 0, 2, 3).reshape(rows.shape)


def joint_ungroup(rows):
    split = rows.reshape(2, FR * HS, HS, rows.shape[-1])
    return split.transpose(1, 0, 2, 3).reshape(rows.shape)


def window_group(flat_rows):
    return flat_rows.reshape(SLOTS, WS * WS, flat_rows.shape[-1])


def split_halves(half_rows, own_half):
    pair_windows = half_rows.shape[0]
    filler = jnp.zeros((2 * SLOTS - pair_windows,) + half_rows.shape[1:], half_rows.dtype)
    padded = jnp.concatenate([half_rows, filler], axis=0)
    keep_part = lax.dynamic_slice_in_dim(padded, own_half * SLOTS, SLOTS, 0)
    send_part = lax.dynamic_slice_in_dim(padded, (1 - own_half) * SLOTS, SLOTS, 0)
    return (keep_part, send_part)


def join_windows(keep_part, came_part, own_half):
    upper_half = jnp.where(own_half == 0, keep_part, came_part)
    lower_half = jnp.where(own_half == 0, came_part, keep_part)
    joined = jnp.concatenate([upper_half, lower_half], axis=1)
    return joined.reshape(-1, joined.shape[-1])


def split_windows(win_rows, own_half):
    grouped = window_group(win_rows)
    half_len = grouped.shape[1] // 2
    upper_half = grouped[:, :half_len]
    lower_half = grouped[:, half_len:]
    keep_part = jnp.where(own_half == 0, upper_half, lower_half)
    send_part = jnp.where(own_half == 0, lower_half, upper_half)
    return (keep_part, send_part)


def join_halves(keep_part, came_part, own_half, pair_windows):
    leading = jnp.where(own_half == 0, keep_part, came_part)
    trailing = jnp.where(own_half == 0, came_part, keep_part)
    joined = jnp.concatenate([leading, trailing], axis=0)[:pair_windows]
    return joined.reshape(-1, joined.shape[-1])


def from_pair(value):
    pairs = [(i, i ^ 1) for i in range(lax.axis_size("win"))]
    return lax.ppermute(value, "win", pairs)


class Weights:
    def __init__(self, masters, place, quick):
        self.quick = quick
        low = [master.astype(jnp.bfloat16) for master in masters]
        self.place = place
        if quick:
            shards = []
            for block in range(2):
                qkv, out, up, down = low[4 * block : 4 * block + 4]
                shards += [jnp.concatenate([qkv, out], axis=1), up, down]
            self.widths = [(384, 128), (512,), (128,)] * 2
            halves = [shard.reshape(2, shard.shape[0] // 2, -1) for shard in shards]
            self.jobs = [Gather(value, 2 * value.shape[1], False) for value in halves[:2]] + [None] * 4
            self.later = [(units, jnp.stack([halves[unit] for unit in units], axis=1)) for units in ((2, 5), (3, 4))]
        else:
            self.full = [
                lax.all_gather(lax.all_gather(shard, "win", axis=1, tiled=True), "clip", axis=0, tiled=True)
                for shard in low
            ]
            self.full = [tuple(self.full[0:2]), (self.full[2],), (self.full[3],)] + [
                tuple(self.full[4:6]),
                (self.full[6],),
                (self.full[7],),
            ]

    def go(self, moves, state, after=()):
        if not self.quick:
            return state
        jobs = [(self.jobs[unit], move) for unit, move in moves]
        jobs = [(job, move) for job, move in jobs if not (job.early and move == "near")]
        known = [(job, job.needs(move)) for job, move in jobs if job.needs(move) in job.held]
        known += [(self.jobs[unit], name) for unit, name in after]
        held, state = lax.optimization_barrier(([job.held[name] for job, name in known], state))
        for (job, name), values in zip(known, held):
            job.held[name] = values
        for job, move in jobs:
            job.go(move)
        return state

    def begin(self, state):
        if not self.quick:
            return state
        state, held = lax.optimization_barrier((state, [value for units, value in self.later]))
        for (units, unused), (a0, b0) in zip(self.later, held):
            a_came, b_came = hop(a0, "y"), hop(b0, "x")
            for place, unit in enumerate(units):
                near = [a0[place], a_came[place], b0[place], b_came[place]]
                halves = jnp.stack(near).reshape(2, 2, *near[0].shape)
                self.jobs[unit] = Gather(halves, 2 * near[0].shape[0], True)
        return state

    def apply(self, unit, x, kind):
        if self.quick:
            job = self.jobs[unit]
            return gathered(job.values(), self.place, x, job.rows, self.widths[unit], kind)
        wholes = self.full[unit]
        result = jnp.dot(x, wholes[0], preferred_element_type=jnp.float32)
        if kind == "gelu":
            return *gelu_both(result), *wholes
        return result if kind == "wide" else result.astype(jnp.bfloat16), *wholes


def body(
    tokens,
    grad_output,
    clip_height,
    clip_width,
    modulation,
    sp_qkv,
    sp_out,
    sp_up,
    sp_down,
    sp_table,
    st_qkv,
    st_out,
    st_up,
    st_down,
    st_table,
    quick,
):
    model_width = tokens.shape[-1]
    half_len = tokens.shape[-2]
    pair_windows = PAIR_LOCS * FR
    shard_index = lax.axis_index("win")
    clip_index = lax.axis_index("clip")
    pair_index = shard_index // 2
    own_half = shard_index % 2
    own_core = clip_index % 2
    own_x = clip_index // 2
    row_places = [
        (own_x ^ x_rel) * 2 + (own_core ^ c_rel) for c_rel in range(2) for x_rel in range(2)
    ]
    place = {
        "rows": jnp.stack(row_places).astype(jnp.int32),
        "cols": jnp.stack([own_half, own_half ^ 1]).astype(jnp.int32),
    }
    weights = Weights(
        (sp_qkv, sp_out, sp_up, sp_down, st_qkv, st_out, st_up, st_down), place, quick
    )
    mod = modulation[0]

    location = pair_index
    token_ids = jnp.arange(WS * WS, dtype=jnp.int32)
    row_pos = location // LOC_W * WS + token_ids // WS
    col_pos = location % LOC_W * WS + token_ids % WS
    sp_valid = (row_pos < clip_height[0]) & (col_pos < clip_width[0])
    sp_allowed = (sp_valid[None, :, None] | jnp.eye(WS * WS, dtype=bool)[None]).astype(jnp.float32)
    joint_len = FR * HS * HS
    joint_ids = jnp.arange(joint_len, dtype=jnp.int32)
    joint_row = location // LOC_W * WS + own_half * HS + joint_ids // HS % HS
    joint_col = location % LOC_W * WS + jnp.arange(2, dtype=jnp.int32)[:, None] * HS + joint_ids[None] % HS
    st_valid = (joint_row[None] < clip_height[0]) & (joint_col < clip_width[0])
    st_allowed = (st_valid[:, :, None] | jnp.eye(joint_len, dtype=bool)[None]).astype(jnp.float32)

    half_tokens = tokens.reshape(pair_windows, half_len, model_width)
    keep_part, send_part = split_halves(half_tokens, own_half)
    came_part = weights.begin(from_pair(send_part))
    came_part = weights.go([(0, "near")], came_part)
    win_input = join_windows(keep_part, came_part, own_half).astype(jnp.float32)
    attn_in_a = modulated_norm(win_input, mod[0], mod[1])

    go = weights.go
    state = (win_input, attn_in_a, sp_table)
    win_input, attn_in_a, sp_table = go([(0, "far"), (0, "core_near")], state)
    sp_strip = spatial_strip(sp_table)
    state = go([(1, "near")], (win_input, attn_in_a, sp_strip, sp_allowed))
    win_input, attn_in_a, sp_strip, sp_allowed = go([(0, "core_far")], state)
    qkv_a, w_qkv_a, w_out_a = weights.apply(0, attn_in_a, "narrow")
    win_input, qkv_a, w_out_a = go([(1, "far")], (win_input, qkv_a, w_out_a))
    win_input, qkv_a, w_out_a = go([(2, "near")], (win_input, qkv_a, w_out_a))
    attn_out_a, probs_a = attend(qkv_a, sp_strip, sp_allowed, SLOTS, WS * WS)
    win_input, attn_out_a, w_out_a = go([(1, "core_near")], (win_input, attn_out_a, w_out_a))
    mixed_a = product(attn_out_a, w_out_a)
    win_middle = win_input + mod[2] * mixed_a
    keep_part, send_part = split_windows(win_middle, own_half)
    send_part = send_part.astype(jnp.bfloat16)
    keep_part, send_part, st_table = go([(1, "core_far")], (keep_part, send_part, st_table))
    came_part = from_pair(send_part)
    keep_part, st_table = go([(2, "far"), (2, "core_near")], (keep_part, st_table))
    st_strip = joint_strip(st_table)
    keep_part, came_part, st_strip, st_allowed = lax.optimization_barrier(
        (keep_part, came_part, st_strip, st_allowed)
    )
    middle_a = joint_group(join_halves(keep_part, came_part.astype(jnp.float32), own_half, pair_windows))
    mlp_in_a = modulated_norm(middle_a, mod[3], mod[4])

    hidden_a, slope_a, w_up_a = weights.apply(1, mlp_in_a, "gelu")
    state = go([(2, "core_far")], (middle_a, hidden_a, slope_a))
    middle_a, hidden_a, slope_a = go([(3, "far")], state)
    downward_a, w_down_a = weights.apply(2, hidden_a, "wide")
    middle_a, downward_a = go([(3, "core_near")], (middle_a, downward_a))
    first_out, attn_in_b = add_branch(middle_a, downward_a, mod[5], mod[6], mod[7])

    first_out, attn_in_b = go([(3, "core_far")], (first_out, attn_in_b))
    first_out, attn_in_b = go([(4, "far")], (first_out, attn_in_b))
    qkv_b, w_qkv_b, w_out_b = weights.apply(3, attn_in_b, "narrow")
    first_out, qkv_b, w_out_b = go([(4, "core_near")], (first_out, qkv_b, w_out_b))
    attn_out_b, probs_b = attend(qkv_b, st_strip, st_allowed, 2, joint_len)
    first_out, attn_out_b, w_out_b = go([(4, "core_far")], (first_out, attn_out_b, w_out_b))
    first_out, attn_out_b, w_out_b = go([(5, "far")], (first_out, attn_out_b, w_out_b))
    mixed_b = product(attn_out_b, w_out_b)
    middle_b, mlp_in_b = add_branch(first_out, mixed_b, mod[8], mod[9], mod[10])
    hidden_b, slope_b, w_up_b = weights.apply(4, mlp_in_b, "gelu")
    middle_b, hidden_b, slope_b = go([(5, "core_near"), (5, "core_far")], (middle_b, hidden_b, slope_b))

    def start_grad(xs, dys, rows, widths, starts, sources, olders=()):
        if quick:
            return Scatter(xs, dys, place, rows, widths, starts, sources, olders)
        return Plain(xs, dys, widths, starts, sources)

    def rounds(jobs, state):
        if quick:
            return together(jobs, state)
        return state

    def hold(jobs, state):
        if not quick:
            return state
        state, held = lax.optimization_barrier((state, [job.values for job in jobs]))
        for job, values in zip(jobs, held):
            job.values = values
        return state

    def settle(jobs, state):
        state = hold(jobs, state)
        if quick:
            for job in jobs:
                job.fold()
        return state

    grad_out_b = joint_group(grad_output.reshape(-1, model_width)).astype(jnp.float32)
    grad_down_b = (mod[11] * grad_out_b).astype(jnp.bfloat16)
    d_st_down = start_grad([hidden_b], [grad_down_b], 1024, (128,), (0,), (0,))
    grad_down_b, hidden_b = rounds([d_st_down], (grad_down_b, hidden_b))
    downward_b, w_down_b = weights.apply(5, hidden_b, "wide")
    grad_up_b = product_scaled(grad_down_b, w_down_b, slope_b)
    d_st_up = start_grad([mlp_in_b], [grad_up_b], 256, (512,), (0,), (0,), [d_st_down])
    grad_up_b, downward_b = rounds([d_st_up, d_st_down], (grad_up_b, downward_b))
    out_rows = middle_b + mod[11] * downward_b
    out_tokens = joint_ungroup(out_rows).reshape(tokens.shape)
    grad_gate_mb = jnp.sum(grad_out_b * downward_b, axis=0)
    grad_mlp_b = product_turned(grad_up_b, w_up_b)
    grad_middle_b, grad_mixed_b, sums_mb = norm_back(
        grad_mlp_b, middle_b, grad_out_b, mod[10], mixed_b, mod[8]
    )
    state = (grad_middle_b, grad_mixed_b)
    state = settle([d_st_up, d_st_down], state)
    grad_middle_b, grad_mixed_b = rounds([d_st_up, d_st_down], state)
    grad_attn_b = product_turned(grad_mixed_b, w_out_b, jnp.bfloat16)
    grad_qkv_b, strip_grad_b = attend_back(
        qkv_b, probs_b, grad_attn_b, 2, joint_len, *st_strip.shape[1:], (2, 128 * (2 * FR - 1))
    )
    grad_middle_b, grad_qkv_b, strip_grad_b, grad_gate_mb = hold(
        [d_st_down], (grad_middle_b, grad_qkv_b, strip_grad_b, grad_gate_mb)
    )
    d_st_attn = start_grad(
        [attn_in_b, attn_out_b],
        [grad_qkv_b, grad_qkv_b, grad_mixed_b],
        256,
        (256, 128, 128),
        (0, 8, 0),
        (0, 0, 1),
        [d_st_down],
    )
    state = hold([d_st_attn], (grad_middle_b, grad_qkv_b, strip_grad_b))
    state = settle([d_st_up], state)
    grad_middle_b, grad_qkv_b, strip_grad_b = rounds([d_st_attn, d_st_up, d_st_down], state)
    grad_in_b = product_turned(grad_qkv_b, w_qkv_b)
    grad_first, grad_down_a, sums_ab = norm_back(
        grad_in_b, first_out, grad_middle_b, mod[7], downward_a, mod[5]
    )
    grad_first, grad_down_a = hold([d_st_attn, d_st_up], (grad_first, grad_down_a))
    d_sp_down = start_grad(
        [hidden_a], [grad_down_a], 1024, (128,), (0,), (0,), [d_st_attn, d_st_up]
    )
    grad_first, grad_down_a = rounds([d_sp_down, d_st_attn, d_st_up], (grad_first, grad_down_a))
    grad_up_a = product_scaled(grad_down_a, w_down_a, slope_a)
    grad_first, grad_up_a = hold([d_sp_down], (grad_first, grad_up_a))
    d_sp_up = start_grad([mlp_in_a], [grad_up_a], 256, (512,), (0,), (0,), [d_sp_down])
    grad_first, grad_up_a = hold([d_sp_up], (grad_first, grad_up_a))
    grad_first, grad_up_a = settle([d_st_attn], (grad_first, grad_up_a))
    grad_first, grad_up_a = hold([d_sp_up], (grad_first, grad_up_a))
    grad_first, grad_up_a = rounds([d_sp_up, d_st_attn], (grad_first, grad_up_a))
    grad_mlp_a = product_turned(grad_up_a, w_up_a)
    grad_middle_a, sums_ma = norm_back(grad_mlp_a, middle_a, grad_first, mod[4])
    grad_middle_a = joint_ungroup(grad_middle_a)
    half_rows = grad_middle_a.reshape(pair_windows, -1, model_width)
    keep_part, send_part = split_halves(half_rows, own_half)
    send_part = send_part.astype(jnp.bfloat16)
    keep_part, send_part = hold([d_sp_up, d_st_attn], (keep_part, send_part))
    came_part = from_pair(send_part)
    keep_part = rounds([d_sp_down], keep_part)
    if quick:
        d_st_attn.fold()
        d_sp_up.fold()
    keep_part, came_part = rounds([d_st_attn], (keep_part, came_part))
    grad_win = join_windows(keep_part, came_part.astype(jnp.float32), own_half)
    grad_mixed_a = (mod[2] * grad_win).astype(jnp.bfloat16)
    grad_gate_aa = jnp.sum(grad_win * mixed_a, axis=0)
    grad_win, grad_mixed_a = rounds([d_sp_up], (grad_win, grad_mixed_a))
    grad_attn_a = product_turned(grad_mixed_a, w_out_a, jnp.bfloat16)
    grad_qkv_a, strip_grad_a = attend_back(
        qkv_a, probs_a, grad_attn_a, SLOTS, WS * WS, *sp_strip.shape[1:], (2, 2 * WS * WS)
    )
    grad_win, grad_qkv_a, strip_grad_a = settle([d_sp_down], (grad_win, grad_qkv_a, strip_grad_a))
    grad_win, grad_qkv_a, strip_grad_a = hold([d_st_attn], (grad_win, grad_qkv_a, strip_grad_a))
    grad_win, grad_qkv_a, strip_grad_a = rounds([d_sp_down], (grad_win, grad_qkv_a, strip_grad_a))
    d_sp_attn = start_grad(
        [attn_in_a, attn_out_a], [grad_qkv_a, grad_mixed_a], 256, (384, 128), (0, 0), (0, 1)
    )
    state = hold([d_sp_attn, d_sp_up, d_sp_down], (grad_win, grad_qkv_a, strip_grad_a, strip_grad_b))
    if quick:
        d_sp_up.fold()
        d_sp_down.fold()
    grad_win, grad_qkv_a, strip_grad_a, strip_grad_b = state
    tables = jnp.concatenate([strip_grad_a, strip_grad_b], axis=2)
    table_total = Total(tables, ("core", "z1", "z0", "y", "x"))
    state = (grad_win, grad_qkv_a)
    state = rounds([d_sp_attn, d_sp_up, d_sp_down, table_total], state)
    state = settle([d_sp_attn, d_sp_up], state)
    grad_win, grad_qkv_a = rounds([d_sp_attn, d_sp_up, table_total], state)
    grad_in_a = product_turned(grad_qkv_a, w_qkv_a)
    win_sum, sums_aa = norm_back(grad_in_a, win_input, grad_win, mod[1])
    win_sum, sums_aa = settle([d_sp_attn], (win_sum, sums_aa))
    mod_rows = [
        sums_aa[0],
        sums_aa[1],
        grad_gate_aa,
        sums_ma[0],
        sums_ma[1],
        sums_ab[2],
        sums_ab[0],
        sums_ab[1],
        sums_mb[2],
        sums_mb[0],
        sums_mb[1],
        grad_gate_mb,
    ]
    mod_total = Total(jnp.stack(mod_rows, axis=0), ("z1", "z0", "y"))
    win_sum = rounds([d_sp_attn, table_total], win_sum)
    keep_part, send_part = split_windows(win_sum, own_half)
    send_part = send_part.astype(jnp.bfloat16)
    keep_part, send_part = settle([d_sp_attn], (keep_part, send_part))
    keep_part, send_part = rounds([d_sp_attn, table_total, mod_total], (keep_part, send_part))
    came_part = from_pair(send_part)
    rounds([table_total, mod_total], ())
    rounds([mod_total], ())
    came_part = came_part.astype(jnp.float32)
    grad_tokens = join_halves(keep_part, came_part, own_half, pair_windows).reshape(tokens.shape)
    if quick:
        grad_modulation = mod_total.result()[None]
        table_sums = table_total.result()
    else:
        grad_modulation = lax.psum(jnp.stack(mod_rows, axis=0), "win")[None]
        table_sums = lax.psum(table_total.result(), ("clip", "win"))
    grad_sp_table = spatial_strip_back(table_sums[:, :, : 2 * WS * WS])
    grad_st_table = joint_strip_back(table_sums[:, :, 2 * WS * WS :])
    wide = d_st_attn.values
    wide_a = d_sp_attn.values
    out_width = wide.shape[1] // 4
    return (
        out_tokens,
        grad_tokens,
        grad_modulation,
        wide_a[:, : 3 * out_width],
        wide_a[:, 3 * out_width :],
        d_sp_up.values,
        d_sp_down.values,
        grad_sp_table,
        wide[:, : 2 * out_width],
        wide[:, 2 * out_width : 3 * out_width],
        wide[:, 3 * out_width :],
        d_st_up.values,
        d_st_down.values,
        grad_st_table,
    )


class Plain:
    def __init__(self, xs, dys, widths, starts, sources):
        grads = []
        for dy, width, start, source in zip(dys, widths, starts, sources):
            x = xs[source]
            part = dy[:, start * 2 * width : start * 2 * width + 8 * width]
            full = lax.dot_general(x, part, TN, preferred_element_type=jnp.float32)
            full = lax.psum_scatter(
                full.astype(jnp.bfloat16), "clip", scatter_dimension=0, tiled=True
            )
            grads.append(lax.psum_scatter(full, "win", scatter_dimension=1, tiled=True))
        self.values = jnp.concatenate(grads, axis=1).astype(jnp.float32)


def solution(mesh):
    grid = P("clip", "win")
    whole = P("clip", "win", None, None, None, None)
    in_specs = (whole, whole, P("clip"), P("clip"), P("clip", None, None)) + ((grid,) * 4 + (P(),)) * 2
    out_specs = (whole, whole, P("clip", None, None)) + (grid,) * 4 + (P(),) + (grid,) * 5 + (P(),)
    quick = mesh.shape["clip"] == 4 and mesh.shape["win"] == 8
    return jax.shard_map(
        partial(body, quick=quick), mesh=mesh, in_specs=in_specs, out_specs=out_specs, check_vma=False
    )
```
